32 devices in a mesh: dp: 4 (over y, x), ctx: 8 (over z, core).
Axes of the slice: x: 2, y: 2, z: 4, core: 2. Of those that a mesh axis runs over, the one named last changes fastest.
Arguments:
- inputs: bfloat16 [4, 1024, 2048], P('dp', 'ctx'), may hold values from -6 to 6
- attn_gain: bfloat16 [2048], P('dp'), may hold values from 0.25 to 1.75
- w_query: bfloat16 [2048, 2048], P('dp'), may hold values from -0.125 to 0.125
- w_key: bfloat16 [2048, 512], P('dp'), may hold values from -0.125 to 0.125
- w_value: bfloat16 [2048, 512], P('dp'), may hold values from -0.125 to 0.125
- q_gain: bfloat16 [64], replicated, may hold values from 0.25 to 1.75
- key_norm_gain: bfloat16 [64], replicated, may hold values from 0.25 to 1.75
- w_out: bfloat16 [2048, 2048], P('dp'), may hold values from -1.75 to 1.75
- ffn_gain: bfloat16 [2048], P('dp'), may hold values from 0.25 to 1.75
- w_gate: bfloat16 [2048, 8192], P('dp'), may hold values from -0.125 to 0.125
- w_up: bfloat16 [2048, 8192], P('dp'), may hold values from -0.125 to 0.125
- w_down: bfloat16 [8192, 2048], P('dp'), may hold values from -0.109375 to 0.109375
- stretch_map: int32 [16], replicated, may hold values from 0 to 15, as said below
- pos_ids: int32 [4, 1024], P('dp', 'ctx'), may hold values from 0 to 1791, as said below
- cotangent: bfloat16 [4, 1024, 2048], P('dp', 'ctx'), may hold values from -6 to 6
Outputs:
- output: bfloat16 [4, 1024, 2048], P('dp', 'ctx')
- input_grad: bfloat16 [4, 1024, 2048], P('dp', 'ctx')
- attn_gain_grad: float32 [2048], P('dp')
- w_query_grad: float32 [2048, 2048], P('dp')
- w_key_grad: float32 [2048, 512], P('dp')
- w_value_grad: float32 [2048, 512], P('dp')
- q_gain_grad: float32 [64], replicated
- k_gain_grad: float32 [64], replicated
- w_out_grad: float32 [2048, 2048], P('dp')
- ffn_gain_grad: float32 [2048], P('dp')
- w_gate_grad: float32 [2048, 8192], P('dp')
- w_up_grad: float32 [2048, 8192], P('dp')
- w_down_grad: float32 [8192, 2048], P('dp')
The draws below stay inside these ranges and needn't reach their ends.
Inputs may be any that keep to these rules, and one draw needn't show every extreme that they name: Stored block b of 64 rows holds stretch stretch_map[b]; the map is a permutation, and blocks 2 i and 2 i + 1 hold stretches that add up to 15. pos_ids[s, r] is stretch_map[r // 64] * 64 + r % 64 plus an offset of sequence s; the offsets are distinct multiples of 256.
All inputs are finite; a program needn't handle non-finite values.
Results may differ from the reference program's by a relative error of at most 0.025.
Values may be sent and summed in bfloat16 or wider, within the bound.
A program may use at most 1 GiB of HBM per device.

```python
from functools import partial
import jax
import jax.numpy as jnp
from jax import lax

D = 2048
QUERY_HEADS = 32
KEY_VALUE_HEADS = 8
HEAD_SIZE = 64
FF = 8192
HALF = 64
STRETCHES = 16
LENGTH = 1024
SEQS = 4
QDIM = 2048
KDIM = 512


def paired_order(key):
    pair_count = STRETCHES // 2
    leading = jax.random.permutation(jax.random.fold_in(key, 17), pair_count).astype(jnp.int32)
    flips = jax.random.randint(jax.random.fold_in(key, 29), (pair_count,), 0, 2)
    mirrored = (STRETCHES - 1 - leading).astype(jnp.int32)
    lead_stretch = jnp.where(flips == 1, mirrored, leading)
    tail_stretch = jnp.where(flips == 1, leading, mirrored)
    return jnp.stack([lead_stretch, tail_stretch], axis=1).reshape(STRETCHES).astype(jnp.int32)


def draw_stretch_map(key, part):
    order = paired_order(key)
    return order


def draw_pos_ids(key, part):
    order = paired_order(key)
    key = jax.random.fold_in(key, 5)
    stored = jnp.arange(LENGTH, dtype=jnp.int32)
    places = order[stored // HALF] * HALF + stored % HALF
    offsets = jax.random.permutation(key, SEQS).astype(jnp.int32) * (LENGTH // SEQS)
    return (offsets[:, None] + places[None, :]).astype(jnp.int32)


def shard_levels(stream_key, shape, shards, smallest, top_value):
    def one(dim, parts):
        steps = jax.random.uniform(jax.random.fold_in(jax.random.fold_in(stream_key, 6), dim), (parts,), jnp.float32, smallest / len(shards), top_value / len(shards))
        return jnp.repeat(jnp.exp(steps), shape[dim] // parts).reshape((-1,) + (1,) * (len(shape) - dim - 1))

    factor_of = one(*shards[0])
    for cut in shards[1:]:
        factor_of = factor_of * one(*cut)
    return factor_of


def scatter_about(rng, extent, width, limit, cuts=(), held_as=jnp.bfloat16):
    loudness = shard_levels(rng, extent, cuts, -0.22, 0.18) if cuts else 1.0
    array = jax.random.normal(rng, extent, jnp.float32) * width * loudness
    return jnp.minimum(jnp.maximum(array, -limit), limit).astype(held_as)


def setup_inputs(seed: int = 0) -> dict:
    key_of = jax.random.split(jax.random.key(seed), 16)
    inputs = scatter_about(key_of[0], (SEQS, LENGTH, D), 1.0, 6.0, ((0, 4), (1, 8)))
    attn_gain = jnp.clip(1.0 + 0.15 * jax.random.normal(key_of[1], (D,), jnp.float32), 0.25, 1.75).astype(jnp.bfloat16)
    w_query = scatter_about(key_of[2], (D, QDIM), D ** -0.5, 0.125, ((0, 4),))
    w_key = scatter_about(key_of[3], (D, KDIM), D ** -0.5, 0.125, ((0, 4),))
    w_value = scatter_about(key_of[4], (D, KDIM), D ** -0.5, 0.125, ((0, 4),))
    q_gain = jnp.clip(1.0 + 0.15 * jax.random.normal(key_of[5], (HEAD_SIZE,), jnp.float32), 0.25, 1.75).astype(jnp.bfloat16)
    key_norm_gain = jnp.clip(1.0 + 0.15 * jax.random.normal(key_of[6], (HEAD_SIZE,), jnp.float32), 0.25, 1.75).astype(jnp.bfloat16)
    w_out = scatter_about(key_of[7], (QDIM, D), (max(1, QDIM * 6 // LENGTH)) ** -0.5, 1.75, ((0, 4),))
    ffn_gain = jnp.clip(1.0 + 0.15 * jax.random.normal(key_of[8], (D,), jnp.float32), 0.25, 1.75).astype(jnp.bfloat16)
    w_gate = scatter_about(key_of[9], (D, FF), D ** -0.5, 0.125, ((0, 4),))
    w_up = scatter_about(key_of[10], (D, FF), D ** -0.5, 0.125, ((0, 4),))
    w_down = scatter_about(key_of[11], (FF, D), (FF // 3) ** -0.5, 0.109375, ((0, 4),))
    stretch_map = draw_stretch_map(jax.random.fold_in(key_of[15], 71), 0)
    pos_ids = draw_pos_ids(jax.random.fold_in(key_of[15], 71), 0)
    cotangent = scatter_about(key_of[14], (SEQS, LENGTH, D), 1.0, 6.0, ((0, 4), (1, 8)))
    return dict(inputs=inputs, attn_gain=attn_gain, w_query=w_query, w_key=w_key, w_value=w_value, q_gain=q_gain, key_norm_gain=key_norm_gain, w_out=w_out, ffn_gain=ffn_gain, w_gate=w_gate, w_up=w_up, w_down=w_down, stretch_map=stretch_map, pos_ids=pos_ids, cotangent=cotangent)


NORM_EPSILON = 1e-05
ROPE_BASE = 1000000.0
MASKED_SCORE = -1e+30
HIGHEST = lax.Precision.HIGHEST

@jax.custom_vjp
def reduced_copy(v):
    return lax.optimization_barrier(v.astype(jnp.bfloat16)).astype(jnp.float32)

@jax.custom_vjp
def reduced_copy_back(v):
    return v

def low_keep(v):
    return (reduced_copy(v), None)

def low_pass(kept, grad):
    return (grad,)

def back_keep(v):
    return (v, None)

def back_low(kept, grad):
    return (reduced_copy(grad),)
reduced_copy.defvjp(low_keep, low_pass)
reduced_copy_back.defvjp(back_keep, back_low)

def rows_norm_apply(values, gain):
    return values * lax.rsqrt(lax.optimization_barrier(jnp.mean(values * values, axis=-1, keepdims=True)) + NORM_EPSILON) * gain

def frequencies():
    steps_half = jnp.arange(HEAD_SIZE // 2, dtype=jnp.float32)
    return jnp.power(jnp.float32(ROPE_BASE), -2.0 * steps_half / HEAD_SIZE)

def apply_rotary(values, rotary_angles):
    middle = values.shape[-1] // 2
    cosine = jnp.cos(rotary_angles)[:, None, :]
    sine_table = jnp.sin(rotary_angles)[:, None, :]
    first_half = values[..., :middle]
    second_half = values[..., middle:]
    return jnp.concatenate([first_half * cosine - second_half * sine_table, second_half * cosine + first_half * sine_table], axis=-1)

def head_attention(operands, places):
    query_group, key_head, value_head = operands
    scores = jnp.einsum('qgd,kd->gqk', query_group, key_head, precision=HIGHEST) * HEAD_SIZE ** (-0.5)
    scores = reduced_copy_back(scores)
    allowed = places[None, :] <= places[:, None]
    scores = jnp.where(allowed[None], scores, MASKED_SCORE)
    top_score = lax.optimization_barrier(jnp.max(scores, axis=-1, keepdims=True))
    weights = jnp.exp(scores - top_score)
    softmax_probs = weights / lax.optimization_barrier(jnp.sum(weights, axis=-1, keepdims=True))
    return jnp.einsum('gqk,kd->qgd', reduced_copy(softmax_probs), value_head, precision=HIGHEST)

def sequence_forward(seq_values, places, positions, attn_gain, w_query, w_key, w_value, q_gain, key_norm_gain, w_out, ffn_gain, w_gate, w_up, w_down):
    context_length = seq_values.shape[0]
    heads_per_group = QUERY_HEADS // KEY_VALUE_HEADS
    normed = reduced_copy(rows_norm_apply(seq_values, attn_gain))
    query_pre = reduced_copy_back(jnp.dot(normed, w_query, precision=HIGHEST))
    key_before_norm = reduced_copy_back(jnp.dot(normed, w_key, precision=HIGHEST))
    gathered_values = reduced_copy(reduced_copy_back(jnp.dot(normed, w_value, precision=HIGHEST)))
    rotary_angles = positions.astype(jnp.float32)[:, None] * frequencies()[None, :]
    query_matrix = reduced_copy(reduced_copy_back(apply_rotary(rows_norm_apply(query_pre.reshape(context_length, QUERY_HEADS, HEAD_SIZE), q_gain), rotary_angles)))
    gathered_keys = reduced_copy(reduced_copy_back(apply_rotary(rows_norm_apply(key_before_norm.reshape(context_length, KEY_VALUE_HEADS, HEAD_SIZE), key_norm_gain), rotary_angles)))
    grouped_heads = query_matrix.reshape(context_length, KEY_VALUE_HEADS, heads_per_group, HEAD_SIZE).transpose(1, 0, 2, 3)
    key_heads = gathered_keys.transpose(1, 0, 2)
    heads_of_value = gathered_values.reshape(context_length, KEY_VALUE_HEADS, HEAD_SIZE).transpose(1, 0, 2)
    head_step = jax.checkpoint(partial(head_attention, places=places))
    mixed_heads = lax.map(head_step, (grouped_heads, key_heads, heads_of_value))
    mixed_rows = mixed_heads.transpose(1, 0, 2, 3).reshape(context_length, QUERY_HEADS * HEAD_SIZE)
    mixed_rows = reduced_copy(reduced_copy_back(mixed_rows))
    hidden_in = seq_values + reduced_copy_back(jnp.dot(mixed_rows, w_out, precision=HIGHEST))
    normed_two = reduced_copy(rows_norm_apply(hidden_in, ffn_gain))
    gate_pre = reduced_copy_back(jnp.dot(normed_two, w_gate, precision=HIGHEST))
    up_pre = reduced_copy_back(jnp.dot(normed_two, w_up, precision=HIGHEST))
    activated = reduced_copy(jax.nn.silu(gate_pre) * up_pre)
    return hidden_in + jnp.dot(activated, w_down, precision=HIGHEST)

def reference(inputs, attn_gain, w_query, w_key, w_value, q_gain, key_norm_gain, w_out, ffn_gain, w_gate, w_up, w_down, stretch_map, pos_ids, cotangent):
    stored = jnp.arange(LENGTH, dtype=jnp.int32)
    places = (stretch_map[stored // HALF] * HALF + stored % HALF).astype(jnp.int32)
    params = tuple((param_item.astype(jnp.float32) for param_item in (attn_gain, w_query, w_key, w_value, q_gain, key_norm_gain, w_out, ffn_gain, w_gate, w_up, w_down)))

    def one_sequence(totals, seq_batch):
        seq_inputs, seq_pos, seq_cot = seq_batch

        def forward(seq_values, *weights_all):
            return sequence_forward(seq_values, places, seq_pos, *weights_all)
        result, pullback = jax.vjp(forward, seq_inputs.astype(jnp.float32), *params)
        grads_all = pullback(seq_cot.astype(jnp.float32))
        new_totals = tuple((running + extra for running, extra in zip(totals, grads_all[1:])))
        return (new_totals, (result.astype(jnp.bfloat16), grads_all[0].astype(jnp.bfloat16)))
    start_totals = tuple((jnp.zeros(param_item.shape, jnp.float32) for param_item in params))
    totals, (outputs, input_grads) = lax.scan(one_sequence, start_totals, (inputs, pos_ids, cotangent))
    return (outputs, input_grads, totals[0], totals[1], totals[2], totals[3], totals[4], totals[5], totals[6], totals[7], totals[8], totals[9], totals[10])
```

```python
from functools import partial

import jax
import jax.numpy as jnp
from jax import lax
from jax.sharding import Mesh, PartitionSpec as P

NORM_EPSILON = 1e-05
ROPE_BASE = 1000000.0
MASKED_SCORE = -1e30
BF16 = jnp.bfloat16
F32 = jnp.float32


def dot(left, right):
    return jnp.dot(left, right, preferred_element_type=F32)


def contract_rows(left, right):
    return lax.dot_general(left, right, (((0,), (0,)), ((), ())), preferred_element_type=F32)


def contract_cols(left, right):
    return lax.dot_general(left, right, (((1,), (1,)), ((), ())), preferred_element_type=F32)


def normalize(values):
    inverse = lax.rsqrt(jnp.mean(values * values, axis=-1, keepdims=True) + NORM_EPSILON)
    return (values * inverse, inverse)


def normalize_back(grad_hat, scaled, inverse):
    return inverse * (grad_hat - scaled * jnp.mean(grad_hat * scaled, axis=-1, keepdims=True))


def apply_rotary(values, cosine, sine):
    middle = values.shape[-1] // 2
    first, second = values[..., :middle], values[..., middle:]
    return jnp.concatenate([first * cosine - second * sine, second * cosine + first * sine], axis=-1)


def rotate_back(values, cosine, sine):
    middle = values.shape[-1] // 2
    first, second = values[..., :middle], values[..., middle:]
    return jnp.concatenate([first * cosine + second * sine, second * cosine - first * sine], axis=-1)


def masked_scores(query_rows, key_rows, query_places, key_places, score_scale):
    scores = contract_cols(query_rows, key_rows) * score_scale
    allowed = key_places[None, :] <= query_places[:, None]
    return jnp.where(allowed, scores, MASKED_SCORE)


def attend_head(operands, query_places, key_places, score_scale):
    query_rows, key_rows, value_rows = operands
    scores = masked_scores(query_rows, key_rows, query_places, key_places, score_scale)
    top_score = jnp.max(scores, axis=-1, keepdims=True)
    weights = jnp.exp(scores - top_score)
    weight_sum = jnp.sum(weights, axis=-1, keepdims=True)
    probs = (weights / weight_sum).astype(BF16)
    return (dot(probs, value_rows), (top_score + jnp.log(weight_sum))[:, 0])


def attend_back(operands, query_places, key_places, score_scale):
    query_rows, key_rows, value_rows, grad_rows, log_total = operands
    scores = masked_scores(query_rows, key_rows, query_places, key_places, score_scale)
    probs = jnp.exp(scores - log_total[:, None])
    grad_probs = contract_cols(grad_rows, value_rows)
    inner = jnp.sum(probs * grad_probs, axis=-1, keepdims=True)
    grad_scores = (probs * (grad_probs - inner)).astype(BF16)
    grad_query = dot(grad_scores, key_rows) * score_scale
    grad_key = contract_rows(grad_scores, query_rows) * score_scale
    grad_value = contract_rows(probs.astype(BF16), grad_rows)
    return (grad_query, grad_key, grad_value)


def columns_to_owner(weight, dp, parts, part):
    rows, cols = weight.shape
    width = cols // (dp * parts)
    cut = weight.reshape(rows, dp, parts, width)
    mine = lax.dynamic_index_in_dim(cut, part, 2, keepdims=False) if parts > 1 else cut[:, :, 0]
    out = lax.all_to_all(mine.transpose(1, 0, 2), "dp", 0, 0)
    return out.reshape(dp * rows, width)


def rows_to_owner(grad, dp):
    rows, width = grad.shape
    return lax.all_to_all(grad.reshape(dp, rows // dp, width), "dp", 0, 0)


def local(
    inputs, attn_gain, w_query, w_key, w_value, q_gain, key_norm_gain, w_out, ffn_gain,
    w_gate, w_up, w_down, stretch_map, pos_ids, cotangent,
):
    dp, lines, cores = lax.axis_size("dp"), lax.axis_size("z"), lax.axis_size("core")
    core = lax.axis_index("core")
    rows, width = inputs.shape[1], inputs.shape[2]
    head = q_gain.shape[0]
    query_width, key_width, hidden = w_query.shape[1], w_key.shape[1], w_gate.shape[1]
    half = rows // 2
    stretches = stretch_map.shape[0]
    length = stretches * half
    group = query_width // key_width
    kv_heads = key_width // head // dp
    q_heads = kv_heads * group
    tokens = dp * rows
    scale = head ** (-0.5)
    ctx = lax.axis_index("z") * cores + core

    index = jnp.arange(rows, dtype=jnp.int32)
    blocks = jnp.arange(stretches, dtype=jnp.int32)
    own = 2 * ctx + index // half
    query_places = jnp.sum(jnp.where(blocks[None, :] == own[:, None], stretch_map[None, :], 0), axis=1) * half + index % half
    key_places = jnp.repeat(stretch_map, half, total_repeat_length=length) * half + jnp.tile(
        jnp.arange(half, dtype=jnp.int32), stretches
    )
    group_places = jnp.tile(query_places, group)
    frequency = jnp.power(F32(ROPE_BASE), -2.0 * jnp.arange(head // 2, dtype=F32) / head)
    positions = lax.all_gather(pos_ids[0], "dp").reshape(tokens)
    angles = positions.astype(F32)[:, None] * frequency[None, :]
    cosine, sine = jnp.cos(angles)[:, None, :], jnp.sin(angles)[:, None, :]

    gain_one = lax.all_gather(attn_gain, "dp", axis=0, tiled=True).astype(F32)
    gain_two = lax.all_gather(ffn_gain, "dp", axis=0, tiled=True).astype(F32)
    wq = columns_to_owner(w_query, dp, 1, 0)
    wk = columns_to_owner(w_key, dp, 1, 0)
    wv = columns_to_owner(w_value, dp, 1, 0)
    wg = columns_to_owner(w_gate, dp, cores, core)
    wu = columns_to_owner(w_up, dp, cores, core)
    slice_rows = hidden // dp // cores
    wd = lax.dynamic_slice_in_dim(w_down, core * slice_rows, slice_rows, 0)
    own_x = inputs[0].astype(F32)
    hat_one, inverse_one = normalize(own_x)
    x_all = lax.all_gather(inputs[0], "dp", axis=0, tiled=True)
    normed_one = (normalize(x_all.astype(F32))[0] * gain_one).astype(BF16)
    q_gain_f, k_gain_f = q_gain.astype(F32), key_norm_gain.astype(F32)
    query_hat, query_inverse = normalize(dot(normed_one, wq).reshape(tokens, q_heads, head))
    query_rot = apply_rotary(query_hat * q_gain_f, cosine, sine).astype(BF16)
    key_hat, key_inverse = normalize(dot(normed_one, wk).reshape(tokens, kv_heads, head))
    key_rot = apply_rotary(key_hat * k_gain_f, cosine, sine).astype(BF16)
    value_low = dot(normed_one, wv).astype(BF16)
    keys_values = jnp.concatenate([key_rot.reshape(dp, rows, kv_heads * head), value_low.reshape(dp, rows, kv_heads * head)], axis=2)
    kv_all = lax.all_gather(keys_values, ("z", "core"), axis=1, tiled=True)
    kv_all = kv_all.reshape(dp, length, 2, kv_heads, head).transpose(2, 0, 3, 1, 4).reshape(2, dp * kv_heads, length, head)
    key_heads, value_heads = kv_all[0], kv_all[1]

    def to_heads(values):
        return (
            values.reshape(dp, rows, kv_heads, group, head).transpose(0, 2, 3, 1, 4).reshape(dp * kv_heads, group * rows, head)
        )

    def from_heads(values):
        return (
            values.reshape(dp, kv_heads, group, rows, head).transpose(0, 3, 1, 2, 4).reshape(tokens, q_heads * head)
        )

    query_grouped = to_heads(query_rot)
    mixed, log_total = lax.map(
        partial(attend_head, query_places=group_places, key_places=key_places, score_scale=scale),
        (query_grouped, key_heads, value_heads),
    )
    mixed_low = from_heads(mixed).astype(BF16)
    attn_part = dot(mixed_low, w_out)
    attn_out = jnp.sum(lax.all_to_all(attn_part.astype(BF16).reshape(dp, rows, width), "dp", 0, 0).astype(F32), axis=0)
    hidden_in = own_x + attn_out
    hat_two, inverse_two = normalize(hidden_in)

    normed_two = (hat_two * gain_two).astype(BF16)
    plane = tokens * cores

    def plane_gather(values):
        return lax.all_gather(values, ("dp", "core")).reshape(plane, width)

    def plane_sum(values):
        parts = lax.all_to_all(values.reshape(dp * cores, rows, width).astype(BF16), ("dp", "core"), 0, 0)
        return jnp.sum(parts.astype(F32), axis=0)

    normed_two_all = plane_gather(normed_two)
    cot_all = plane_gather(cotangent[0])
    gate = dot(normed_two_all, wg)
    up = dot(normed_two_all, wu)
    sig = jax.nn.sigmoid(gate)
    act = gate * sig
    act_low = (act * up).astype(BF16)
    output = (hidden_in + plane_sum(dot(act_low, wd))).astype(BF16)[None]
    grad_act = contract_cols(cot_all, wd)
    grad_gate = (grad_act * up * sig * (1.0 + gate * (1.0 - sig))).astype(BF16)
    grad_up = (grad_act * act).astype(BF16)
    grad_normed_two = plane_sum(contract_cols(grad_gate, wg) + contract_cols(grad_up, wu))
    gain_grad_two = jnp.sum(grad_normed_two * hat_two, axis=0)
    grad_hidden = cotangent[0].astype(F32) + normalize_back(grad_normed_two * gain_two, hat_two, inverse_two)

    grad_hidden_all = lax.all_gather(grad_hidden.astype(BF16), "dp", axis=0, tiled=True)
    grad_mixed = contract_cols(grad_hidden_all, w_out).astype(BF16)
    grad_q, grad_k, grad_v = lax.map(
        partial(attend_back, query_places=group_places, key_places=key_places, score_scale=scale),
        (query_grouped, key_heads, value_heads, to_heads(grad_mixed), log_total),
    )
    grad_query_rot = from_heads(grad_q).astype(BF16).astype(F32).reshape(tokens, q_heads, head)
    kv_grad = jnp.stack([grad_k, grad_v]).reshape(2, dp, kv_heads, length, head).transpose(3, 1, 0, 2, 4).astype(BF16)
    kv_grad = lax.psum_scatter(kv_grad, ("z", "core"), scatter_dimension=0, tiled=True).transpose(1, 0, 2, 3, 4).reshape(tokens, 2, kv_heads, head)
    grad_key_rot = kv_grad[:, 0].astype(F32)
    grad_value_low = kv_grad[:, 1].reshape(tokens, kv_heads * head)
    grad_query_gained = rotate_back(grad_query_rot, cosine, sine)
    q_gain_grad = jnp.sum(grad_query_gained * query_hat, axis=(0, 1))
    grad_query_pre = normalize_back(grad_query_gained * q_gain_f, query_hat, query_inverse).reshape(tokens, -1).astype(BF16)
    grad_key_gained = rotate_back(grad_key_rot, cosine, sine)
    k_gain_grad = jnp.sum(grad_key_gained * key_hat, axis=(0, 1))
    grad_key_pre = normalize_back(grad_key_gained * k_gain_f, key_hat, key_inverse).reshape(tokens, -1).astype(BF16)
    normed_part = contract_cols(grad_query_pre, wq) + contract_cols(grad_key_pre, wk) + contract_cols(grad_value_low, wv)
    grad_normed_one = jnp.sum(
        lax.all_to_all(normed_part.astype(BF16).reshape(dp, rows, width), "dp", 0, 0).astype(F32), axis=0
    )
    gain_grad_one = jnp.sum(grad_normed_one * hat_one, axis=0)
    input_grad = (grad_hidden + normalize_back(grad_normed_one * gain_one, hat_one, inverse_one)).astype(BF16)[None]

    def finish_columns(grad):
        return rows_to_owner(lax.psum(grad.astype(BF16), "z"), dp)

    down = lax.all_gather(lax.psum(contract_rows(act_low, cot_all).astype(BF16), "z"), "core", axis=0, tiled=True)

    def finish_hidden(grad):
        mine = lax.all_gather(finish_columns(grad), "core")
        return mine.transpose(2, 1, 0, 3).reshape(width // dp, hidden).astype(F32)

    gate_grad = finish_hidden(contract_rows(normed_two_all, grad_gate))
    up_grad = finish_hidden(contract_rows(normed_two_all, grad_up))
    out_grad = lax.psum(contract_rows(mixed_low, grad_hidden_all).astype(BF16), ("z", "core")).astype(F32)

    def finish_heads(grad):
        mine = rows_to_owner(lax.psum(grad.astype(BF16), ("z", "core")), dp)
        return mine.transpose(1, 0, 2).reshape(width // dp, -1).astype(F32)

    query_grad = finish_heads(contract_rows(normed_one, grad_query_pre))
    key_grad = finish_heads(contract_rows(normed_one, grad_key_pre))
    value_grad = finish_heads(contract_rows(normed_one, grad_value_low))
    gains = jnp.concatenate([gain_grad_one, gain_grad_two, q_gain_grad, k_gain_grad])
    gains = lax.psum(gains, ("dp", "z", "core"))
    place = lax.axis_index("dp")
    piece = width // dp
    attn_gain_grad = lax.dynamic_slice_in_dim(gains, place * piece, piece, 0)
    ffn_gain_grad = lax.dynamic_slice_in_dim(gains, width + place * piece, piece, 0)
    return (
        output, input_grad, attn_gain_grad, query_grad, key_grad, value_grad,
        gains[2 * width : 2 * width + head], gains[2 * width + head :], out_grad, ffn_gain_grad,
        gate_grad, up_grad, down.astype(F32),
    )


def solution(mesh):
    dp, ctx = mesh.shape["dp"], mesh.shape["ctx"]
    fine = Mesh(mesh.devices.reshape(dp, ctx // 2, 2), ("dp", "z", "core"))
    tokens = P("dp", ("z", "core"), None)
    rows = P("dp", None)
    in_specs = (
        tokens, P("dp"), rows, rows, rows, P(), P(), rows, P("dp"), rows, rows, rows, P(), P("dp", ("z", "core")), tokens,
    )
    out_specs = (tokens, tokens, P("dp"), rows, rows, rows, P(), P(), rows, P("dp"), rows, rows, rows)
    return jax.shard_map(local, mesh=fine, in_specs=in_specs, out_specs=out_specs, check_vma=False)
```

```python
from functools import partial

import jax
import jax.numpy as jnp
from jax import lax
from jax.experimental import pallas as pl
from jax.experimental.pallas import tpu as pltpu
from jax.sharding import Mesh, PartitionSpec as P

NORM_EPSILON = 1e-05
ROPE_BASE = 1000000.0
MASKED_SCORE = -1e30
BF16 = jnp.bfloat16
F32 = jnp.float32
MESH = pl.DeviceIdType.MESH
MIB = 2**20


def dot(left, right):
    return jnp.dot(left, right, preferred_element_type=F32)


def contract_rows(left, right):
    return lax.dot_general(left, right, (((0,), (0,)), ((), ())), preferred_element_type=F32)


def contract_cols(left, right):
    return lax.dot_general(left, right, (((1,), (1,)), ((), ())), preferred_element_type=F32)


def normalize(values):
    inverse = lax.rsqrt(jnp.mean(values * values, axis=-1, keepdims=True) + NORM_EPSILON)
    return (values * inverse, inverse)


def normalize_back(grad_hat, scaled, inverse):
    return inverse * (grad_hat - scaled * jnp.mean(grad_hat * scaled, axis=-1, keepdims=True))


def apply_rotary(values, cosine, sine):
    middle = values.shape[-1] // 2
    first, second = values[..., :middle], values[..., middle:]
    return jnp.concatenate([first * cosine - second * sine, second * cosine + first * sine], axis=-1)


def rotate_back(values, cosine, sine):
    middle = values.shape[-1] // 2
    first, second = values[..., :middle], values[..., middle:]
    return jnp.concatenate([first * cosine + second * sine, second * cosine - first * sine], axis=-1)


def attend_kernel(head, group, query, keys_values, bias, mixed, log_total):
    length = bias.shape[0]
    rows = query.shape[1]
    kv_heads = query.shape[2] // head // group
    scale = head ** (-0.5)
    both = keys_values[:, 0].reshape(length, 2 * kv_heads * head)
    mask = jnp.concatenate([bias[...]] * group, axis=1)
    for g in range(kv_heads):
        keys = both[:, g * head : (g + 1) * head]
        values = both[:, (kv_heads + g) * head : (kv_heads + g + 1) * head]
        queries = stack_heads(query, g, group, head)
        scores = contract_cols(keys, queries) * scale + mask
        top = jnp.max(scores, axis=0, keepdims=True)
        weights = jnp.exp(scores - top)
        total = jnp.sum(weights, axis=0, keepdims=True)
        probs = (weights * (1.0 / total)).astype(BF16)
        out = contract_rows(values, probs)
        log_total[0, pl.ds(g, 1), :] = top + jnp.log(total)
        unstack_heads(mixed, out.T.astype(BF16), g, group, head, rows)


def stack_heads(ref, g, group, head):
    return jnp.concatenate([ref[0, :, (g * group + h) * head : (g * group + h + 1) * head] for h in range(group)], axis=0)


def unstack_heads(ref, values, g, group, head, rows):
    ref[0, :, g * group * head : (g + 1) * group * head] = jnp.concatenate(
        [values[h * rows : (h + 1) * rows] for h in range(group)], axis=1
    )


def attend_back_kernel(head, group, query, keys_values, bias, log_total, grad_mixed, grad_query, grad_kv):
    length = bias.shape[0]
    rows = query.shape[1]
    kv_heads = query.shape[2] // head // group
    scale = head ** (-0.5)
    both = keys_values[:, 0].reshape(length, 2 * kv_heads * head)
    mask = jnp.concatenate([bias[...]] * group, axis=1)
    grads = [None] * (2 * kv_heads)
    for g in range(kv_heads):
        keys = both[:, g * head : (g + 1) * head]
        values = both[:, (kv_heads + g) * head : (kv_heads + g + 1) * head]
        queries = stack_heads(query, g, group, head)
        grad_out = stack_heads(grad_mixed, g, group, head)
        scores = contract_cols(keys, queries) * scale + mask
        probs = jnp.exp(scores - log_total[0, pl.ds(g, 1), :])
        grad_probs = contract_cols(values, grad_out)
        inner = jnp.sum(probs * grad_probs, axis=0, keepdims=True)
        grad_scores = (probs * (grad_probs - inner)).astype(BF16)
        grads[g] = dot(grad_scores, queries) * scale
        grads[kv_heads + g] = dot(probs.astype(BF16), grad_out)
        back = contract_rows(keys, grad_scores) * scale
        unstack_heads(grad_query, back.T.astype(BF16), g, group, head, rows)
    grad_kv[:, 0] = jnp.concatenate(grads, axis=1).astype(BF16).reshape(grad_kv[:, 0].shape)


def attend(query, keys_values, bias, head, group, grad_mixed=None, log_total=None):
    seqs, rows, width = query.shape
    spans, _, _, kv_width = keys_values.shape
    length = bias.shape[0]
    kv_heads = width // head // group
    row_spec = pl.BlockSpec((1, rows, width), lambda s: (s, 0, 0))
    kv_spec = pl.BlockSpec((spans, 1, rows, kv_width), lambda s: (0, s, 0, 0))
    log_spec = pl.BlockSpec((1, kv_heads, group * rows), lambda s: (s, 0, 0))
    bias_spec = pl.BlockSpec((length, rows), lambda s: (0, 0))
    rows_out = jax.ShapeDtypeStruct(query.shape, BF16)
    params = pltpu.CompilerParams(vmem_limit_bytes=56 * MIB)
    flops = 4 * seqs * rows * length * width
    if grad_mixed is None:
        return pl.pallas_call(
            partial(attend_kernel, head, group),
            grid=(seqs,),
            in_specs=[row_spec, kv_spec, bias_spec],
            out_specs=(row_spec, log_spec),
            out_shape=(rows_out, jax.ShapeDtypeStruct((seqs, kv_heads, group * rows), F32)),
            compiler_params=params,
            cost_estimate=pl.CostEstimate(flops=flops, bytes_accessed=4 * MIB, transcendentals=flops // 256),
            name="attend",
        )(query, keys_values, bias)
    return pl.pallas_call(
        partial(attend_back_kernel, head, group),
        grid=(seqs,),
        in_specs=[row_spec, kv_spec, bias_spec, log_spec, row_spec],
        out_specs=(row_spec, kv_spec),
        out_shape=(rows_out, jax.ShapeDtypeStruct(keys_values.shape, BF16)),
        compiler_params=params,
        cost_estimate=pl.CostEstimate(flops=5 * flops // 2, bytes_accessed=8 * MIB, transcendentals=flops // 256),
        name="attend_back",
    )(query, keys_values, bias, log_total, grad_mixed)


def places():
    dp, z, core = lax.axis_index("dp"), lax.axis_index("z"), lax.axis_index("core")
    return dp, z, core


def line_of(z, lines):
    left = z < lines // 2
    step = jnp.where(left, 1, -1)
    place = jnp.where(left, z, lines - 1 - z)
    inner = z + step
    outer = jnp.clip(z - step, 0, lines - 1)
    return place, inner, outer


def sum_kernel(dims, down, gate_up, out_part, qkv_part,
               down_sum, gate_sum, up_sum, out_sum, qkv_sum,
               own, first, second, pair_o, pair_q, mine_q,
               own_sem, a2a_send, first_send, first_recv, second_send, second_recv,
               core_send, core_recv, out_sem, pair_send, pair_recv):
    dp_n, lines, n_down, n_blocks = dims
    dp, z, core = places()
    place, inner, outer = line_of(z, lines)
    middle = lines // 2 - 1
    rows = own.shape[1]
    quarter = rows // 4
    half = rows // 2
    n_gu = dp_n * n_blocks
    n_out = 2
    n_main = own.shape[0]
    other = 1 - core

    barrier = pltpu.get_barrier_semaphore()
    for shift in range(1, dp_n):
        pl.semaphore_signal(barrier, device_id=(lax.rem(dp + shift, dp_n), z, core), device_id_type=MESH)
    pl.semaphore_signal(barrier, device_id=(dp, z, other), device_id_type=MESH)
    pl.semaphore_signal(barrier, device_id=(dp, inner, core), device_id_type=MESH)

    @pl.when(place > 0)
    def _():
        pl.semaphore_signal(barrier, device_id=(dp, outer, core), device_id_type=MESH)

    pl.semaphore_wait(barrier, dp_n + 1 + jnp.minimum(place, 1))

    def pair_copies(side):
        copies = []
        for j in range(n_out):
            for c in range(4):
                copies.append((
                    out_part.at[pl.ds(side * half + j * quarter, quarter), pl.ds(c * 512, 512)],
                    j, c))
        return copies

    pair_q_copy = [
        pltpu.make_async_remote_copy(
            qkv_part.at[pl.ds(i * rows + other * half, half)], pair_q.at[i],
            pair_send.at[i], pair_recv.at[i], device_id=(dp, z, other), device_id_type=MESH)
        for i in range(dp_n)
    ]
    pair_o_copy = [
        pltpu.make_async_remote_copy(
            src, pair_o.at[j, pl.ds(c * quarter, quarter)], pair_send.at[dp_n + j * 4 + c], pair_recv.at[dp_n + j * 4 + c],
            device_id=(dp, z, other), device_id_type=MESH)
        for src, j, c in pair_copies(other)
    ]

    def down_copies(k):
        return [
            pltpu.make_async_copy(
                down.at[pl.ds(k * quarter, quarter), pl.ds(c * 512, 512)], own.at[k, pl.ds(c * quarter, quarter)],
                own_sem.at[k * 4 + c])
            for c in range(4)
        ]

    gu_sem = 4 * n_down

    def gu_copies(b):
        local = pltpu.make_async_copy(
            gate_up.at[pl.ds(dp * rows, rows), pl.ds(b * 512, 512)], own.at[n_down + b * dp_n + dp],
            own_sem.at[gu_sem + b * dp_n + dp])
        remote = []
        for shift in range(1, dp_n):
            to = lax.rem(dp + shift, dp_n)
            remote.append(pltpu.make_async_remote_copy(
                gate_up.at[pl.ds(to * rows, rows), pl.ds(b * 512, 512)], own.at[n_down + b * dp_n + dp],
                a2a_send.at[b * dp_n + shift], own_sem.at[gu_sem + b * dp_n + dp],
                device_id=(to, z, core), device_id_type=MESH))
        return local, remote

    def gu_wait(b, src):
        pltpu.make_async_copy(
            gate_up.at[pl.ds(0, rows), pl.ds(0, 512)], own.at[n_down + b * dp_n + src],
            own_sem.at[gu_sem + b * dp_n + src]).wait()

    @pl.loop(0, n_down)
    def _(k):
        for copy in down_copies(k):
            copy.start()

    @pl.loop(0, n_blocks)
    def _(b):
        local, remote = gu_copies(b)
        local.start()
        for copy in remote:
            copy.start()

    for copy in pair_q_copy + pair_o_copy:
        copy.start()
    o_base = gu_sem + n_gu
    own_out = [
        pltpu.make_async_copy(src, own.at[n_down + n_gu + j, pl.ds(c * quarter, quarter)], own_sem.at[o_base + j * 4 + c])
        for src, j, c in pair_copies(core)
    ]
    q_base = o_base + 4 * n_out
    own_qkv = [
        pltpu.make_async_copy(qkv_part.at[pl.ds(i * rows + core * half, half)], mine_q.at[i], own_sem.at[q_base + i])
        for i in range(dp_n)
    ]
    for copy in own_out + own_qkv:
        copy.start()

    def add(into, left, right):
        into[...] = (left[...].astype(F32) + right[...].astype(F32)).astype(BF16)

    qs_base = n_blocks * dp_n
    for i in range(dp_n):
        own_qkv[i].wait()
        pair_q_copy[i].wait_recv()
        add(mine_q.at[i], mine_q.at[i], pair_q.at[i])
    qr_base = q_base + dp_n
    piece = mine_q.shape[2] // 3
    across_n = 512 // piece
    per_chunk = 2 * across_n
    n_q = 3 * dp_n // per_chunk
    q_first = n_down + n_gu + n_out

    def q_place(number):
        spot = lax.rem(number, per_chunk)
        column = lax.rem(spot, across_n) * piece
        if not isinstance(column, int):
            column = pl.multiple_of(column, 128)
        return q_first + number // per_chunk, pl.ds((spot // across_n) * half, half), pl.ds(column, piece)

    def q_own(number):
        chunk, where, columns = q_place(number)
        return own.at[chunk, where, columns]

    q_remote = []
    for shift in range(1, dp_n):
        to = lax.rem(dp + shift, dp_n)
        for j in range(3):
            q_remote.append(pltpu.make_async_remote_copy(
                mine_q.at[to, :, pl.ds(j * piece, piece)], q_own(dp * 3 + j),
                a2a_send.at[qs_base + shift * 3 + j], own_sem.at[qr_base + dp * 3 + j],
                device_id=(to, z, core), device_id_type=MESH))
    for copy in q_remote:
        copy.start()
    for j in range(3):
        pltpu.make_async_copy(
            mine_q.at[dp, :, pl.ds(j * piece, piece)], q_own(dp * 3 + j), own_sem.at[qr_base + dp * 3 + j]).start()
    for j in range(n_out):
        for c in range(4):
            own_out[j * 4 + c].wait()
            pair_o_copy[j * 4 + c].wait_recv()
        add(own.at[n_down + n_gu + j], own.at[n_down + n_gu + j], pair_o.at[j])

    def to_inner(k, buf, n, across):
        land, sem = (buf[2], second_recv) if across else (buf[1], first_recv)
        return pltpu.make_async_remote_copy(
            buf[0].at[n], land.at[n], first_send.at[k], sem.at[k], device_id=(dp, inner, core), device_id_type=MESH)

    def stage_one(k, n, buf):
        own_b, first_b, second_b = buf

        @pl.when(place > 0)
        def _():
            to_inner(k, buf, n, False).wait_recv()
            add(own_b.at[n], own_b.at[n], first_b.at[n])

        @pl.when(place < middle)
        def _():
            to_inner(k, buf, n, False).start()

        @pl.when(place == middle)
        def _():
            to_inner(k, buf, n, True).start()

    def stage_two(k, n, buf, finish):
        own_b, first_b, second_b = buf
        across = to_inner(k, buf, n, True)
        across.wait_recv()
        across.wait_send()

        @pl.when(place == middle)
        def _():
            add(second_b.at[n], own_b.at[n], second_b.at[n])

        back = pltpu.make_async_remote_copy(
            second_b.at[n], second_b.at[n], second_send.at[k], second_recv.at[k],
            device_id=(dp, outer, core), device_id_type=MESH)

        @pl.when(place > 0)
        def _():
            back.start()

        finish(True)

    def stage_three(k, n, buf, finish):
        back = pltpu.make_async_remote_copy(
            buf[2].at[n], buf[2].at[n], second_send.at[k], second_recv.at[k],
            device_id=(dp, outer, core), device_id_type=MESH)

        @pl.when(place > 0)
        def _():
            back.wait_send()

        finish(False)

    main = (own, first, second)

    def both(k, c, src, dst, starting):
        sem = k * 8 + c
        local = pltpu.make_async_copy(src, dst, out_sem.at[sem])
        remote = pltpu.make_async_remote_copy(
            src, dst, core_send.at[sem], core_recv.at[sem], device_id=(dp, z, other), device_id_type=MESH)
        if starting:
            remote.start()
            local.start()
        else:
            local.wait()
            remote.wait_send()

    def arrived(k, c, dst):
        pltpu.make_async_remote_copy(
            dst, dst, core_send.at[k * 8 + c], core_recv.at[k * 8 + c], device_id=(dp, z, other),
            device_id_type=MESH).wait_recv()

    f8 = n_down * quarter

    def down_dst(k, c, who):
        return down_sum.at[pl.ds(who * f8 + k * quarter, quarter), pl.ds(c * 512, 512)]

    def finish_down(k, starting):
        for c in range(4):
            both(k, c, second.at[k, pl.ds(c * quarter, quarter)], down_dst(k, c, core), starting)

    def gu_dst(m, c, who):
        b, src = m // dp_n, lax.rem(m, dp_n)
        target = (gate_sum, up_sum)[c]
        return target.at[:, pl.ds((2 * src + who) * f8 + b * 256, 256)]

    def finish_gu(m, starting):
        k = n_down + m
        for c in range(2):
            both(k, c, second.at[k, :, pl.ds(c * 256, 256)], gu_dst(m, c, core), starting)

    def out_dst(j, c, who):
        return out_sum.at[pl.ds(who * half + j * quarter, quarter), pl.ds(c * 512, 512)]

    def finish_out(j, starting):
        k = n_down + n_gu + j
        for c in range(4):
            both(k, c, second.at[k, pl.ds(c * quarter, quarter)], out_dst(j, c, core), starting)

    def q_dst(number, who):
        column = lax.rem(number, 3) * piece
        return qkv_sum.at[number // 3, pl.ds(who * half, half), pl.ds(pl.multiple_of(column, 128), piece)]

    def finish_q(j, starting):
        for c in range(per_chunk):
            chunk, where, columns = q_place(c)
            both(q_first + j, c, second.at[q_first + j, where, columns], q_dst(j * per_chunk + c, core), starting)

    lag = 2 + 4 * (middle - place)
    most = 2 + 4 * middle

    def slot_one(k):
        @pl.when(k < n_down)
        def _():
            for copy in down_copies(k):
                copy.wait()

        @pl.when((k >= n_down) & (k < n_down + n_gu))
        def _():
            m = k - n_down
            gu_wait(m // dp_n, lax.rem(m, dp_n))

        @pl.when(k >= q_first)
        def _():
            for c in range(per_chunk):
                number = (k - q_first) * per_chunk + c
                pltpu.make_async_copy(
                    mine_q.at[0, :, pl.ds(0, piece)], q_own(number), own_sem.at[qr_base + number]).wait()

        stage_one(k, k, main)

    def slot_fin(k, starting):
        @pl.when(k < n_down)
        def _():
            finish_down(k, starting)

        @pl.when((k >= n_down) & (k < n_down + n_gu))
        def _():
            finish_gu(k - n_down, starting)

        @pl.when((k >= n_down + n_gu) & (k < q_first))
        def _():
            finish_out(k - n_down - n_gu, starting)

        @pl.when(k >= q_first)
        def _():
            finish_q(k - q_first, starting)

    @pl.loop(0, n_main + most)
    def _(t):
        @pl.when(t < n_main)
        def _():
            slot_one(t)

        @pl.when((t >= lag) & (t - lag < n_main))
        def _():
            k = t - lag
            stage_two(k, k, main, partial(slot_fin, k))

    @pl.loop(0, n_main)
    def _(k):
        stage_three(k, k, main, partial(slot_fin, k))

        @pl.when(k < n_down)
        def _():
            for c in range(4):
                arrived(k, c, down_dst(k, c, other))

        @pl.when((k >= n_down) & (k < n_down + n_gu))
        def _():
            for c in range(2):
                arrived(k, c, gu_dst(k - n_down, c, other))

        @pl.when((k >= n_down + n_gu) & (k < q_first))
        def _():
            for c in range(4):
                arrived(k, c, out_dst(k - n_down - n_gu, c, other))

        @pl.when(k >= q_first)
        def _():
            for c in range(per_chunk):
                arrived(k, c, q_dst((k - q_first) * per_chunk + c, other))

    @pl.loop(0, n_blocks)
    def _(b):
        for copy in gu_copies(b)[1]:
            copy.wait_send()

    for copy in q_remote + pair_q_copy + pair_o_copy:
        copy.wait_send()


def sum_grads(down, gate_up, out_part, qkv_part, dp_n, lines, collective_id):
    width = out_part.shape[1]
    rows = width // dp_n
    f8 = down.shape[0]
    n_down = f8 // (rows // 4)
    n_blocks = f8 // 256
    cols = qkv_part.shape[1]
    n_main = n_down + dp_n * n_blocks + 2 + dp_n * cols // 1024
    hbm = pl.BlockSpec(memory_space=pl.ANY)
    chunk = pltpu.VMEM((n_main, rows, 512), BF16)
    small = pltpu.VMEM((dp_n, rows // 2, cols), BF16)
    dma = pltpu.SemaphoreType.DMA
    own_sems = 4 * n_down + dp_n * n_blocks + 8 + 4 * dp_n
    return pl.pallas_call(
        partial(sum_kernel, (dp_n, lines, n_down, n_blocks)),
        out_shape=(
            jax.ShapeDtypeStruct((2 * f8, width), BF16),
            jax.ShapeDtypeStruct((rows, 2 * dp_n * f8), BF16),
            jax.ShapeDtypeStruct((rows, 2 * dp_n * f8), BF16),
            jax.ShapeDtypeStruct((rows, width), BF16),
            jax.ShapeDtypeStruct((dp_n, rows, cols), BF16),
        ),
        in_specs=[hbm] * 4,
        out_specs=(hbm,) * 5,
        scratch_shapes=[
            chunk, chunk, chunk,
            pltpu.VMEM((2, rows, 512), BF16), small, small,
            dma((own_sems,)), dma((n_blocks * dp_n + 3 * dp_n,)),
            dma((n_main,)), dma((n_main,)), dma((n_main,)), dma((n_main,)),
            dma((n_main * 8,)), dma((n_main * 8,)), dma((n_main * 8,)),
            dma((dp_n + 8,)), dma((dp_n + 8,)),
        ],
        compiler_params=pltpu.CompilerParams(collective_id=collective_id, has_side_effects=True, vmem_limit_bytes=60 * MIB),
        cost_estimate=pl.CostEstimate(flops=10**9, bytes_accessed=10**9, transcendentals=0),
        name="sum_grads",
    )(down, gate_up, out_part, qkv_part)


def columns_to_owner(weight, dp, parts, part):
    rows, cols = weight.shape
    width = cols // (dp * parts)
    cut = weight.reshape(rows, dp, parts, width)
    mine = lax.dynamic_index_in_dim(cut, part, 2, keepdims=False) if parts > 1 else cut[:, :, 0]
    out = lax.all_to_all(mine.transpose(1, 0, 2), "dp", 0, 0)
    return out.reshape(dp * rows, width)


def rows_to_owner(grad, dp):
    rows, width = grad.shape
    return lax.all_to_all(grad.reshape(dp, rows // dp, width), "dp", 0, 0)


def local(
    inputs, attn_gain, w_query, w_key, w_value, q_gain, key_norm_gain, w_out, ffn_gain,
    w_gate, w_up, w_down, stretch_map, pos_ids, cotangent,
):
    dp, lines, cores = lax.axis_size("dp"), lax.axis_size("z"), lax.axis_size("core")
    core = lax.axis_index("core")
    rows, width = inputs.shape[1], inputs.shape[2]
    head = q_gain.shape[0]
    query_width, key_width, hidden = w_query.shape[1], w_key.shape[1], w_gate.shape[1]
    half = rows // 2
    stretches = stretch_map.shape[0]
    length = stretches * half
    group = query_width // key_width
    kv_heads = key_width // head // dp
    q_heads = kv_heads * group
    tokens = dp * rows
    scale = head ** (-0.5)
    ctx = lax.axis_index("z") * cores + core

    index = jnp.arange(rows, dtype=jnp.int32)
    blocks = jnp.arange(stretches, dtype=jnp.int32)
    own = 2 * ctx + index // half
    query_places = jnp.sum(jnp.where(blocks[None, :] == own[:, None], stretch_map[None, :], 0), axis=1) * half + index % half
    key_places = jnp.repeat(stretch_map, half, total_repeat_length=length) * half + jnp.tile(
        jnp.arange(half, dtype=jnp.int32), stretches
    )
    bias = jnp.where(key_places[:, None] <= query_places[None, :], 0.0, MASKED_SCORE).astype(F32)
    frequency = jnp.power(F32(ROPE_BASE), -2.0 * jnp.arange(head // 2, dtype=F32) / head)
    positions = lax.all_gather(pos_ids[0], "dp").reshape(tokens)
    angles = positions.astype(F32)[:, None] * frequency[None, :]
    cosine, sine = jnp.cos(angles)[:, None, :], jnp.sin(angles)[:, None, :]

    gain_one = lax.all_gather(attn_gain, "dp", axis=0, tiled=True).astype(F32)
    gain_two = lax.all_gather(ffn_gain, "dp", axis=0, tiled=True).astype(F32)
    wq = columns_to_owner(w_query, dp, 1, 0)
    wk = columns_to_owner(w_key, dp, 1, 0)
    wv = columns_to_owner(w_value, dp, 1, 0)
    wg = columns_to_owner(w_gate, dp, cores, core)
    wu = columns_to_owner(w_up, dp, cores, core)
    slice_rows = hidden // dp // cores
    wd = lax.dynamic_slice_in_dim(w_down, core * slice_rows, slice_rows, 0)
    own_x = inputs[0].astype(F32)
    hat_one, inverse_one = normalize(own_x)
    x_all = lax.all_gather(inputs[0], "dp", axis=0, tiled=True)
    normed_one = (normalize(x_all.astype(F32))[0] * gain_one).astype(BF16)
    q_gain_f, k_gain_f = q_gain.astype(F32), key_norm_gain.astype(F32)
    query_hat, query_inverse = normalize(dot(normed_one, wq).reshape(tokens, q_heads, head))
    query_rot = apply_rotary(query_hat * q_gain_f, cosine, sine).astype(BF16)
    key_hat, key_inverse = normalize(dot(normed_one, wk).reshape(tokens, kv_heads, head))
    key_rot = apply_rotary(key_hat * k_gain_f, cosine, sine).astype(BF16)
    value_low = dot(normed_one, wv).astype(BF16)
    keys_values = jnp.concatenate([key_rot.reshape(dp, rows, kv_heads * head), value_low.reshape(dp, rows, kv_heads * head)], axis=2)
    keys_values = lax.all_gather(keys_values, ("z", "core"))
    query_rows = query_rot.reshape(dp, rows, q_heads * head)
    mixed, log_total = attend(query_rows, keys_values, bias, head, group)
    mixed_low = mixed.reshape(tokens, q_heads * head)
    attn_part = dot(mixed_low, w_out)
    attn_out = jnp.sum(lax.all_to_all(attn_part.astype(BF16).reshape(dp, rows, width), "dp", 0, 0).astype(F32), axis=0)
    hidden_in = own_x + attn_out
    hat_two, inverse_two = normalize(hidden_in)

    normed_two = (hat_two * gain_two).astype(BF16)
    plane = tokens * cores

    def plane_gather(values):
        return lax.all_gather(values, ("dp", "core")).reshape(plane, width)

    def plane_sum(values):
        parts = lax.all_to_all(values.reshape(dp * cores, rows, width).astype(BF16), ("dp", "core"), 0, 0)
        return jnp.sum(parts.astype(F32), axis=0)

    normed_two_all = plane_gather(normed_two)
    cot_all = plane_gather(cotangent[0])
    gate = dot(normed_two_all, wg)
    up = dot(normed_two_all, wu)
    sig = jax.nn.sigmoid(gate)
    act = gate * sig
    act_low = (act * up).astype(BF16)
    output = (hidden_in + plane_sum(dot(act_low, wd))).astype(BF16)[None]
    grad_act = contract_cols(cot_all, wd)
    grad_gate = (grad_act * up * sig * (1.0 + gate * (1.0 - sig))).astype(BF16)
    grad_up = (grad_act * act).astype(BF16)
    grad_normed_two = plane_sum(contract_cols(grad_gate, wg) + contract_cols(grad_up, wu))
    gain_grad_two = jnp.sum(grad_normed_two * hat_two, axis=0)
    grad_hidden = cotangent[0].astype(F32) + normalize_back(grad_normed_two * gain_two, hat_two, inverse_two)

    grad_hidden_all = lax.all_gather(grad_hidden.astype(BF16), "dp", axis=0, tiled=True)
    grad_mixed = contract_cols(grad_hidden_all, w_out).astype(BF16)
    grad_q, grad_kv = attend(
        query_rows, keys_values, bias, head, group, grad_mixed.reshape(dp, rows, q_heads * head), log_total
    )
    grad_query_rot = grad_q.astype(F32).reshape(tokens, q_heads, head)
    grad_kv = jnp.sum(lax.all_to_all(grad_kv, ("z", "core"), 0, 0).astype(F32), axis=0).astype(BF16)
    grad_kv = grad_kv.reshape(tokens, 2, kv_heads, head)
    grad_key_rot = grad_kv[:, 0].astype(F32)
    grad_value_low = grad_kv[:, 1].reshape(tokens, kv_heads * head)
    grad_query_gained = rotate_back(grad_query_rot, cosine, sine)
    q_gain_grad = jnp.sum(grad_query_gained * query_hat, axis=(0, 1))
    grad_query_pre = normalize_back(grad_query_gained * q_gain_f, query_hat, query_inverse).reshape(tokens, -1).astype(BF16)
    grad_key_gained = rotate_back(grad_key_rot, cosine, sine)
    k_gain_grad = jnp.sum(grad_key_gained * key_hat, axis=(0, 1))
    grad_key_pre = normalize_back(grad_key_gained * k_gain_f, key_hat, key_inverse).reshape(tokens, -1).astype(BF16)
    normed_part = contract_cols(grad_query_pre, wq) + contract_cols(grad_key_pre, wk) + contract_cols(grad_value_low, wv)
    grad_normed_one = jnp.sum(
        lax.all_to_all(normed_part.astype(BF16).reshape(dp, rows, width), "dp", 0, 0).astype(F32), axis=0
    )
    gain_grad_one = jnp.sum(grad_normed_one * hat_one, axis=0)
    input_grad = (grad_hidden + normalize_back(grad_normed_one * gain_one, hat_one, inverse_one)).astype(BF16)[None]

    down_part = contract_rows(act_low, cot_all).astype(BF16)
    blocks_n = slice_rows // 256
    grad_both = jnp.stack(
        [grad_gate.reshape(plane, blocks_n, 256), grad_up.reshape(plane, blocks_n, 256)], axis=2
    ).reshape(plane, 2 * slice_rows)
    both_part = contract_rows(normed_two_all, grad_both).astype(BF16)
    out_part = contract_rows(mixed_low, grad_hidden_all).astype(BF16)
    grad_qkv = jnp.concatenate([grad_query_pre, grad_key_pre, grad_value_low], axis=1)
    qkv_part = contract_rows(normed_one, grad_qkv).astype(BF16)
    down, gate_grad, up_grad, out_grad, qkv_sum = sum_grads(down_part, both_part, out_part, qkv_part, dp, lines, 1)
    q_cols, kv_cols = q_heads * head, kv_heads * head
    qkv_rows = qkv_sum.transpose(1, 0, 2).astype(F32)
    query_grad = qkv_rows[:, :, :q_cols].reshape(width // dp, query_width)
    key_grad = qkv_rows[:, :, q_cols : q_cols + kv_cols].reshape(width // dp, key_width)
    value_grad = qkv_rows[:, :, q_cols + kv_cols :].reshape(width // dp, key_width)
    gains = jnp.concatenate([gain_grad_one, gain_grad_two, q_gain_grad, k_gain_grad])
    gains = lax.psum(gains, ("dp", "z", "core"))
    place = lax.axis_index("dp")
    piece = width // dp
    attn_gain_grad = lax.dynamic_slice_in_dim(gains, place * piece, piece, 0)
    ffn_gain_grad = lax.dynamic_slice_in_dim(gains, width + place * piece, piece, 0)
    return (
        output, input_grad, attn_gain_grad, query_grad, key_grad, value_grad,
        gains[2 * width : 2 * width + head], gains[2 * width + head :], out_grad.astype(F32), ffn_gain_grad,
        gate_grad.astype(F32), up_grad.astype(F32), down.astype(F32),
    )


def solution(mesh):
    dp, ctx = mesh.shape["dp"], mesh.shape["ctx"]
    fine = Mesh(mesh.devices.reshape(dp, ctx // 2, 2), ("dp", "z", "core"))
    tokens = P("dp", ("z", "core"), None)
    rows = P("dp", None)
    in_specs = (
        tokens, P("dp"), rows, rows, rows, P(), P(), rows, P("dp"), rows, rows, rows, P(), P("dp", ("z", "core")), tokens,
    )
    out_specs = (tokens, tokens, P("dp"), rows, rows, rows, P(), P(), rows, P("dp"), rows, rows, rows)
    return jax.shard_map(local, mesh=fine, in_specs=in_specs, out_specs=out_specs, check_vma=False)
```

```python
from functools import partial
from types import SimpleNamespace
from typing import Any, NamedTuple

import jax
import jax.numpy as jnp
from jax import lax
from jax.experimental import pallas as pl
from jax.experimental.pallas import tpu as pltpu
from jax.sharding import Mesh, PartitionSpec as P

NORM_EPSILON = 1e-05
ROPE_BASE = 1000000.0
MASKED_SCORE = -1e30
BF16 = jnp.bfloat16
F32 = jnp.float32
MESH = pl.DeviceIdType.MESH
MIB = 2**20


def dot(left, right):
    return jnp.dot(left, right, preferred_element_type=F32)


def contract_rows(left, right):
    return lax.dot_general(left, right, (((0,), (0,)), ((), ())), preferred_element_type=F32)


def contract_cols(left, right):
    return lax.dot_general(left, right, (((1,), (1,)), ((), ())), preferred_element_type=F32)


def places():
    dp, z, core = lax.axis_index("dp"), lax.axis_index("z"), lax.axis_index("core")
    return dp, z, core


def line_of(z, lines):
    left = z < lines // 2
    step = jnp.where(left, 1, -1)
    place = jnp.where(left, z, lines - 1 - z)
    inner = z + step
    outer = jnp.clip(z - step, 0, lines - 1)
    return place, inner, outer


class Line:
    def __init__(self, refs, dims):
        vars(self).update(vars(refs))
        vars(self).update(vars(dims))
        self.dp, self.z, self.core = places()
        self.place, self.inner, self.outer = line_of(self.z, self.lines)
        self.middle = self.lines // 2 - 1
        self.side = self.z // (self.lines // 2)
        self.other = 1 - self.core
        self.second = self.totals.at[self.core]
        self.quarter = self.rows // 4
        self.half = self.rows // 2
        self.lag = 5 + 2 * (self.middle - self.place)
        self.most = 5 + 2 * self.middle + 3
        self.n_ffn = self.n_blocks * self.per_block
        self.q_first = self.n_ffn + 2
        self.piece = self.qkv_cols // 3
        self.across = 512 // self.piece
        self.per_chunk = 2 * self.across
        self.position = 0

    def ours(self, k):
        return lax.rem(k // self.per_block + lax.rem(k, self.per_block), 2) == self.side

    def shift_of(self, k):
        part = lax.rem(k, self.per_block) - self.down_block
        return jnp.where(k < self.n_ffn, jnp.maximum(part, 0), 0)

    def send_inner(self, k, src):
        return pltpu.make_async_remote_copy(
            src, self.first.at[k], self.first_send.at[k], self.first_recv.at[k],
            device_id=(self.dp, self.inner, self.core), device_id_type=MESH)

    def send_across(self, k, src):
        return pltpu.make_async_remote_copy(
            src, self.cross.at[k], self.first_send.at[k], self.cross_recv.at[k],
            device_id=(self.dp, self.inner, self.core), device_id_type=MESH)

    def send_owner(self, k):
        total = self.total_slot.at[lax.rem(k, 4)]
        shift = self.shift_of(k)
        local = pltpu.make_async_copy(total, self.second.at[k], self.second_recv.at[k])
        remote = pltpu.make_async_remote_copy(
            total, self.second.at[k], self.owner_send.at[k], self.second_recv.at[k],
            device_id=(lax.rem(self.dp + shift, self.dp_n), self.z, self.core), device_id_type=MESH)
        return shift, local, remote

    def spread_across(self, k):
        return pltpu.make_async_remote_copy(
            self.second.at[k], self.second.at[k], self.across_send.at[k], self.second_recv.at[k],
            device_id=(self.dp, self.inner, self.core), device_id_type=MESH)

    def spread_outer(self, k):
        return pltpu.make_async_remote_copy(
            self.second.at[k], self.second.at[k], self.second_send.at[k], self.second_recv.at[k],
            device_id=(self.dp, self.outer, self.core), device_id_type=MESH)

    def load(self, src, dst, n):
        return pltpu.make_async_copy(src, dst, self.load_sem.at[n])

    def ready(self, k):
        @pl.when(k >= self.q_first)
        def _():
            for c in range(self.per_chunk):
                number = (k - self.q_first) * self.per_chunk + c
                spot = self.q_own(number)
                pltpu.make_async_copy(spot, spot, self.own_sem.at[number]).wait()

    def stage_one(self, k):
        self.ready(k)
        mine = self.sum_slot.at[lax.rem(k, 4)]

        @pl.when(self.place == 0)
        def _():
            @pl.when(k >= 2)
            def _():
                self.send_inner(k - 2, self.own.at[k - 2]).wait_send()

            self.send_inner(k, self.own.at[k]).start()

        @pl.when(self.place > 0)
        def _():
            self.load(self.own.at[k], mine, 0).start()
            self.send_inner(k, mine).wait_recv()
            self.load(self.first.at[k], self.in_slot, 1).start()
            self.load(self.own.at[k], mine, 0).wait()
            self.load(self.first.at[k], self.in_slot, 1).wait()
            add_chunk(mine, mine, self.in_slot)

            @pl.when(self.place < self.middle)
            def _():
                self.send_inner(k, mine).start()

            @pl.when((self.place == self.middle) & jnp.logical_not(self.ours(k)))
            def _():
                self.send_across(k, mine).start()

    def stage_sum(self, k):
        @pl.when((self.place == self.middle) & self.ours(k))
        def _():
            mine = self.sum_slot.at[lax.rem(k, 4)]
            self.send_across(k, mine).wait_recv()
            arrived = self.load(self.cross.at[k], self.in_slot, 2)
            arrived.start()
            arrived.wait()
            add_chunk(self.total_slot.at[lax.rem(k, 4)], mine, self.in_slot)
            shift, local, remote = self.send_owner(k)

            @pl.when(shift == 0)
            def _():
                local.start()

            @pl.when(shift > 0)
            def _():
                remote.start()

    def stage_sent(self, k):
        @pl.when((self.place > 0) & ((self.place < self.middle) | jnp.logical_not(self.ours(k))))
        def _():
            self.send_inner(k, self.own.at[k]).wait_send()

    def stage_handed(self, k):
        shift, _, remote = self.send_owner(k)

        @pl.when((self.place == self.middle) & self.ours(k) & (shift > 0))
        def _():
            remote.wait_send()

    def stage_two(self, k):
        self.spread_outer(k).wait_recv()

        @pl.when((self.place == self.middle) & self.ours(k))
        def _():
            self.spread_across(k).start()

        @pl.when(self.place > 0)
        def _():
            self.spread_outer(k).start()

        self.deliver(k).start()

    def stage_three(self, k):
        @pl.when((self.place == self.middle) & self.ours(k))
        def _():
            self.spread_across(k).wait_send()

        @pl.when(self.place > 0)
        def _():
            self.spread_outer(k).wait_send()

        @pl.when((self.place == 0) & (k >= self.chunks - 2))
        def _():
            self.send_inner(k, self.own.at[k]).wait_send()

        self.deliver(k).wait_send()

    def q_place(self, number):
        spot = lax.rem(number, self.per_chunk)
        column = lax.rem(spot, self.across) * self.piece
        if not isinstance(column, int):
            column = pl.multiple_of(column, 128)
        return number // self.per_chunk, pl.ds((spot // self.across) * self.half, self.half), pl.ds(column, self.piece)

    def q_own(self, number):
        chunk, where, columns = self.q_place(number)
        return self.own.at[self.q_first + chunk, where, columns]

    def deliver(self, k):
        return pltpu.make_async_remote_copy(
            self.second.at[k], self.second.at[k], self.core_send.at[k], self.core_recv.at[k],
            device_id=(self.dp, self.z, self.other), device_id_type=MESH)

    def advance(self, count):
        start = self.position
        self.position += count

        @pl.loop(start, start + count)
        def _(t):
            self.slot(t)

    def slot(self, t):
        @pl.when(t < self.chunks)
        def _():
            self.stage_one(t)

        def when(k, act, extra=True):
            @pl.when((k >= 0) & (k < self.chunks) & extra)
            def _():
                act(k)

        at_middle = self.place == self.middle
        when(t - 2, self.stage_sum)
        when(t - 3, self.stage_sent)
        when(t - 4, self.stage_handed)
        early = at_middle & self.ours(jnp.maximum(t - 3, 0))
        late = jnp.logical_not(at_middle & self.ours(jnp.maximum(t - self.lag, 0)))
        when(t - 3, self.stage_two, early)
        when(t - self.lag, self.stage_two, late)
        when(t - self.lag - 3, self.stage_three)

    def advance_at(self, first, count):
        for j in range(count):
            self.slot(first + j)

    def finish(self):
        self.advance(self.chunks + self.most - self.position)

        @pl.loop(0, self.chunks)
        def _(k):
            self.deliver(k).wait_recv()


def add_chunk(into, left, right):
    rows = into.shape[0]

    @pl.loop(0, rows // 64)
    def _(i):
        part = pl.ds(i * 64, 64)
        into[part] = (left[part].astype(F32) + right[part].astype(F32)).astype(BF16)


class BackIn(NamedTuple):
    normed_two: Any
    cot_all: Any
    w_first: Any
    w_gate: Any
    w_up: Any
    w_down: Any
    hidden_in: Any
    w_out: Any
    w_qkv: Any
    normed_one: Any
    qk_pre: Any
    query: Any
    keys_values: Any
    log_total: Any
    mixed: Any
    bias: Any
    tables: Any
    gains: Any
    own_x: Any


class BackOut(NamedTuple):
    output: Any
    input_grad: Any
    gain_sum: Any
    totals: Any
    own: Any
    first: Any
    cross: Any
    w_land: Any
    dn2_pair: Any
    out_pair: Any
    out_land: Any
    out_keep: Any
    pair_o: Any
    pair_q: Any


class BackScratch(NamedTuple):
    sum_slot: Any
    total_slot: Any
    in_slot: Any
    kv_sum: Any
    grad_query: Any
    grad_qkv: Any
    dn2_land: Any
    land_slot: Any
    hidden_v: Any
    grad_hidden: Any
    own_x_v: Any
    cot_own: Any
    gains_v: Any
    gain_acc: Any
    dx_all: Any
    kv_pair: Any
    kv_land: Any
    gain_core: Any
    gain_dp: Any
    gain_z: Any
    dn1_land: Any
    result: Any
    pair_slot: Any
    pair_q_slot: Any
    load_sem: Any
    own_sem: Any
    first_send: Any
    first_recv: Any
    second_send: Any
    cross_recv: Any
    owner_send: Any
    across_send: Any
    second_recv: Any
    core_send: Any
    core_recv: Any
    w_send: Any
    w_recv: Any
    stage_sem: Any
    in_sem: Any
    sum_send: Any
    pair_recv: Any
    land_recv: Any
    dx_send: Any
    dx_recv: Any
    kv_send: Any
    kv_recv: Any
    pair_send: Any
    pair_land: Any
    dn1_send: Any
    dn1_recv: Any
    q_send: Any
    gain_send: Any
    gain_recv: Any


def norm_rows(values):
    inverse = lax.rsqrt(jnp.mean(values * values, axis=-1, keepdims=True) + NORM_EPSILON)
    return values * inverse, inverse


def back_kernel(dims, *refs):
    r = SimpleNamespace()
    for kind, first in ((BackIn, 0), (BackOut, len(BackIn._fields)), (BackScratch, len(BackIn._fields + BackOut._fields))):
        vars(r).update(kind(*refs[first : first + len(kind._fields)])._asdict())
    dp_n, lines, tokens, width = dims.dp_n, dims.lines, dims.tokens, dims.width
    rows, f8, n_blocks, per_block, down_block = dims.rows, dims.f8, dims.n_blocks, dims.per_block, dims.down_block
    head, group, kv_heads = dims.head, dims.group, dims.kv_heads
    q_cols, kv_cols, cols = dims.q_cols, dims.kv_cols, dims.qkv_cols
    plane = 2 * dp_n * tokens
    seq_tokens = dp_n * tokens
    length = lines * 2 * tokens
    scale = head ** (-0.5)
    line = Line(r, dims)
    dp, z, core, other = line.dp, line.z, line.core, line.other
    own = r.own
    half, quarter = rows // 2, rows // 4
    partner = (dp, z, other)
    n_ffn = line.n_ffn
    pairs = range(1, dp_n)

    def peer(shift):
        return lax.rem(dp + shift, dp_n)

    def local(src, dst, sem, n=0):
        return pltpu.make_async_copy(src, dst, sem.at[n])

    def remote(src, dst, send, n, recv, m, device):
        return pltpu.make_async_remote_copy(
            src, dst, send.at[n], recv.at[m], device_id=device, device_id_type=MESH)

    def span(index, size):
        return pl.ds(pl.multiple_of(index * size, size), size)

    def start(copies):
        for copy in copies:
            copy.start()

    def wait(copies):
        for copy in copies:
            copy.wait()

    barrier = pltpu.get_barrier_semaphore()
    for shift in pairs:
        pl.semaphore_signal(barrier, device_id=(peer(shift), z, core), device_id_type=MESH)
    for shift in range(1, 2 * lines):
        spot = lax.rem(2 * z + core + shift, 2 * lines)
        pl.semaphore_signal(barrier, device_id=(dp, spot // 2, lax.rem(spot, 2)), device_id_type=MESH)

    w_land = r.w_land

    def weight_copies(b):
        mine, sent = [], []
        for c, weight in enumerate((r.w_gate, r.w_up)):
            for shift in range(dp_n):
                to = peer(shift)
                src = weight.at[:, pl.ds(pl.multiple_of((2 * to + core) * f8 + b * 256, 256), 256)]
                dst = w_land.at[b, span(dp, rows), pl.ds(c * 256, 256)]
                slot = (b * dp_n + dp) * 2 + c
                if shift == 0:
                    mine.append(local(src, dst, r.w_recv, slot))
                else:
                    sent.append(remote(src, dst, r.w_send, (b * dp_n + shift) * 2 + c, r.w_recv, slot, (to, z, core)))
        return mine, sent

    def feed_forward(act, grads, wd, w_gu, stage):
        def blocks(n2, dy):
            loads = [
                local(r.normed_two, n2, r.in_sem, 0), local(r.cot_all, dy, r.in_sem, 1),
                local(r.w_down.at[span(core, f8)], wd, r.in_sem, 2),
            ]
            start(loads)

            first_weights = local(r.w_first, w_gu.at[0], r.in_sem, 3)
            first_weights.start()

            @pl.loop(1, n_blocks)
            def _(b):
                start(weight_copies(b)[0])

            pl.semaphore_wait(barrier, dp_n - 1 + 2 * lines - 1)

            start(weight_copies(1)[1])
            wait(loads)
            first_weights.wait()

            @pl.loop(0, n_blocks)
            def _(b):
                @pl.when(b > 0)
                def _():
                    @pl.loop(0, dp_n)
                    def _(src):
                        for c in range(2):
                            dst = w_land.at[b, pl.ds(0, rows), pl.ds(c * 256, 256)]
                            local(dst, dst, r.w_recv, (b * dp_n + src) * 2 + c).wait()

                    weights = local(w_land.at[b], w_gu.at[b], r.in_sem, 3)
                    weights.start()

                    @pl.when(b + 1 < n_blocks)
                    def _():
                        start(weight_copies(b + 1)[1])

                    weights.wait()

                @pl.loop(0, plane // 256)
                def _(i):
                    where = span(i, 256)
                    both = dot(n2[where], w_gu[b])
                    gate, up = both[:, :256], both[:, 256:]
                    grad_act = contract_cols(dy[where], wd[span(b, 256)])
                    sig = jax.nn.sigmoid(gate)
                    silu = gate * sig
                    act[b, where] = (silu * up).astype(BF16)
                    grads[b, where, 0:256] = (grad_act * up * sig * (1.0 + gate * (1.0 - sig))).astype(BF16)
                    grads[b, where, 256:512] = (grad_act * silu).astype(BF16)

                def to_own(j):
                    return local(stage.at[j], own.at[b * per_block + j], r.stage_sem, j)

                @pl.loop(0, 4)
                def _(c):
                    grad = contract_rows(act[b], dy[:, span(c, 512)]).astype(BF16)
                    for j in range(down_block):
                        stage[j, span(c, quarter), :] = grad[j * quarter : (j + 1) * quarter]

                for j in range(down_block):
                    to_own(j).start()

                @pl.loop(0, dp_n)
                def _(shift):
                    stage[down_block + shift] = contract_rows(n2[:, span(peer(shift), rows)], grads[b]).astype(BF16)
                    to_own(down_block + shift).start()

                @pl.loop(0, per_block)
                def _(j):
                    to_own(j).wait()


                line.advance_at(b * 2, 2)

        pl.run_scoped(blocks, pltpu.VMEM((plane, width), BF16), pltpu.VMEM((plane, width), BF16))
        line.position = n_blocks * 2

        def sums(part):
            def to_partner(hidden):
                base = 0 if hidden else dp_n
                return [
                    remote(part.at[i, span(other, tokens)], (r.dn2_pair if hidden else r.out_pair).at[i], r.sum_send, base + i, r.pair_recv, base + i, partner)
                    for i in range(dp_n)
                ]

            def plane_sum(hidden, product):
                @pl.loop(0, dp_n)
                def _(i):
                    @pl.loop(0, width // 512)
                    def _(n):
                        part[i, :, span(n, 512)] = product(span(i, 2 * tokens), span(n, 512)).astype(BF16)

                to_pair = to_partner(hidden)
                start(to_pair)
                for i in range(dp_n):
                    to_pair[i].wait_recv()
                    copy = local((r.dn2_pair if hidden else r.out_pair).at[i], r.land_slot, r.in_sem, 3)
                    copy.start()
                    copy.wait()
                    mine = part.at[i, span(core, tokens)]
                    add_rows(mine, mine, r.land_slot)

            def own_sums():
                return [
                    remote(part.at[peer(shift), span(core, tokens)], r.dn2_land.at[dp], r.sum_send, 2 * dp_n + shift,
                           r.land_recv, dp, (peer(shift), z, core))
                    for shift in pairs
                ]

            def hidden_grad(where, columns):
                total = contract_cols(grads[0, where], w_gu[0, columns])
                for b in range(1, n_blocks):
                    total += contract_cols(grads[b, where], w_gu[b, columns])
                return total

            def ffn_out(where, columns):
                total = dot(act[0, where], wd[pl.ds(0, 256), columns])
                for b in range(1, n_blocks):
                    total += dot(act[b, where], wd[pl.ds(b * 256, 256), columns])
                return total

            plane_sum(True, hidden_grad)
            mine = local(part.at[dp, span(core, tokens)], r.dn2_land.at[dp], r.in_sem, 4)
            start(own_sums() + [mine])
            line.advance(2)
            mine.wait()
            for copy in own_sums() + to_partner(True):
                copy.wait_send()
            plane_sum(False, ffn_out)
            keep = [local(part.at[i, span(core, tokens)], r.out_keep.at[i], r.in_sem, 8 + i) for i in range(dp_n)]
            start(keep)
            line.advance(1)
            wait(keep)
            for copy in to_partner(False):
                copy.wait_send()

        pl.run_scoped(sums, pltpu.VMEM((dp_n, 2 * tokens, width), BF16))

    pl.run_scoped(
        feed_forward,
        pltpu.VMEM((n_blocks, plane, 256), BF16), pltpu.VMEM((n_blocks, plane, 512), BF16), pltpu.VMEM((f8, width), BF16),
        pltpu.VMEM((n_blocks, width, 512), BF16), pltpu.VMEM((per_block, rows, 512), BF16),
    )

    def landed(land, base):
        for shift in pairs:
            src = peer(shift)
            local(land.at[src], land.at[src], r.land_recv, base + src).wait()

    hidden_in, grad_hidden, gains = r.hidden_v, r.grad_hidden, r.gains_v
    own_loads = [
        local(r.cot_all.at[span(2 * dp + core, tokens)], r.cot_own, r.in_sem, 4), local(r.hidden_in, hidden_in, r.in_sem, 5), local(r.gains, gains, r.in_sem, 6), local(r.own_x, r.own_x_v, r.in_sem, 7),
    ]
    start(own_loads)
    wait(own_loads)
    landed(r.dn2_land, 0)
    gain_acc = r.gain_acc
    gain_acc[...] = jnp.zeros_like(gain_acc)

    @pl.loop(0, tokens // 32)
    def _(i):
        where = span(i, 32)
        grad = r.dn2_land[0, where].astype(F32)
        for src in range(1, dp_n):
            grad += r.dn2_land[src, where].astype(F32)
        hat, inverse = norm_rows(hidden_in[where])
        gain_acc[1:2] += jnp.sum(grad * hat, axis=0, keepdims=True)
        back = grad * gains[1:2]
        dy_own = r.cot_own
        total = dy_own[where].astype(F32) + inverse * (back - hat * jnp.mean(back * hat, axis=-1, keepdims=True))
        grad_hidden[where] = total
        r.dx_all[dp, where] = total.astype(BF16)

    dx_sends = []
    for shift in pairs:
        to = peer(shift)
        dx_sends.append(remote(r.dx_all.at[dp], r.dx_all.at[dp], r.dx_send, shift, r.dx_recv, dp, (to, z, core)))
    start(dx_sends)
    line.advance(2)

    kv_sum, grad_query, grad_qkv = r.kv_sum, r.grad_query, r.grad_qkv
    step = max(1, min(group, MIB // (4 * length * tokens)))

    def kv_copies(s):
        found = []
        for shift in range(1, lines):
            to = lax.rem(z + shift, lines)
            found.append(remote(kv_sum.at[s, to], r.kv_land.at[z, s], r.kv_send, dp_n + s * lines + shift,
                                r.kv_recv, dp_n + s * lines + z, (dp, to, core)))
        return found

    def sequences(w_out, query, keys_values, bias, grad_mixed, grad_kv):
        loads = [
            local(src, dst, r.in_sem, 8 + n)
            for n, (src, dst) in enumerate(((r.w_out, w_out), (r.query, query), (r.keys_values, keys_values), (r.bias, bias)))
        ]
        start(loads)
        wait(loads)

        def pair_copy(s):
            return remote(grad_kv.at[s, :, other], r.kv_pair.at[s], r.kv_send, s, r.kv_recv, s, partner)

        def one_sequence(turn):
            s = peer(turn)

            @pl.when(turn > 0)
            def _():
                local(r.dx_all.at[s], r.dx_all.at[s], r.dx_recv, s).wait()

            grad_mixed[...] = contract_cols(r.dx_all[s], w_out[...]).astype(BF16)
            both = keys_values[:, s].reshape(length, 2 * kv_cols)
            grads = [None] * (2 * kv_heads)
            mask = jnp.concatenate([bias[...]] * step, axis=1)
            for g in range(kv_heads):
                keys = both[:, g * head : (g + 1) * head]
                values = both[:, (kv_heads + g) * head : (kv_heads + g + 1) * head]
                key_grad = value_grad = None
                for first in range(g * group, (g + 1) * group, step):
                    names = [slice(h * head, (h + 1) * head) for h in range(first, first + step)]
                    queries = jnp.concatenate([query[s, :, n] for n in names], axis=0)
                    grad_out = jnp.concatenate([grad_mixed[:, n] for n in names], axis=0)
                    scores = contract_cols(keys, queries) * scale + mask
                    offset = (first - g * group) * tokens
                    probs = jnp.exp(scores - r.log_total[s, pl.ds(g, 1), offset : offset + step * tokens])
                    grad_probs = contract_cols(values, grad_out)
                    inner = jnp.sum(probs * grad_probs, axis=0, keepdims=True)
                    grad_scores = (probs * (grad_probs - inner)).astype(BF16)
                    key_part = dot(grad_scores, queries)
                    value_part = dot(probs.astype(BF16), grad_out)
                    key_grad = key_part if key_grad is None else key_grad + key_part
                    value_grad = value_part if value_grad is None else value_grad + value_part
                    back = (contract_rows(keys, grad_scores) * scale).T.astype(BF16)
                    grad_query[s, :, first * head : (first + step) * head] = jnp.concatenate(
                        [back[h * tokens : (h + 1) * tokens] for h in range(step)], axis=1)
                grads[g] = key_grad * scale
                grads[kv_heads + g] = value_grad
            grad_kv[s] = jnp.concatenate(grads, axis=1).astype(BF16).reshape(lines, 2, tokens, 2 * kv_cols)
            pair_copy(s).start()

        def pass_on(turn):
            s = peer(turn)
            pair_copy(s).wait_recv()

            @pl.loop(0, lines)
            def _(n):
                kv_sum[s, n] = (grad_kv[s, n, core].astype(F32) + r.kv_pair[s, n].astype(F32)).astype(BF16)

            start(kv_copies(s))

        @pl.loop(0, dp_n)
        def _(turn):
            one_sequence(turn)

            @pl.when(turn > 0)
            def _():
                pass_on(turn - 1)

            line.advance_at(line.position + turn * dims.pace, dims.pace)

        pass_on(dp_n - 1)

        @pl.loop(0, dp_n)
        def _(s):
            pair_copy(s).wait_send()

    seqs = lambda *shape: pltpu.VMEM((dp_n,) + shape, BF16)
    pl.run_scoped(
        sequences,
        pltpu.VMEM((rows, width), BF16), seqs(tokens, q_cols), pltpu.VMEM((2 * lines, dp_n, tokens, 2 * kv_cols), BF16),
        pltpu.VMEM((length, tokens), F32), pltpu.VMEM((tokens, q_cols), BF16), seqs(lines, 2, tokens, 2 * kv_cols),
    )
    line.position += dp_n * dims.pace
    assert line.position <= n_ffn

    def projections(w_qkv, normed_one, qk_pre, mixed, tables, out_part, qkv_part, dn1_part):
        loads = [
            local(src, dst, r.in_sem, 8 + n)
            for n, (src, dst) in enumerate((
                (r.qk_pre, qk_pre), (r.tables, tables), (r.mixed, mixed), (r.normed_one, normed_one), (r.w_qkv, w_qkv)))
        ]
        start(loads)
        wait(loads)

        @pl.loop(0, width // 512)
        def _(n):
            total = jnp.zeros((rows, 512), F32)
            for s in range(dp_n):
                total += contract_rows(mixed[s], r.dx_all[s, :, span(n, 512)])
            out_part[:, span(n, 512)] = total.astype(BF16)

        pair_o = remote(out_part.at[span(other, half)], r.pair_o, r.pair_send, 0, r.pair_land, 0, partner)
        pair_o.start()
        line.advance(1)

        q_gain, k_gain = gains[2:3, 0:head], gains[3:4, 0:head]
        zero = jnp.zeros((1, head), F32)

        def rotate(turn, carry):
            s = peer(turn)
            for shift in range(1, lines):
                src = lax.rem(z + shift, lines)
                land = r.kv_land.at[src, s]
                local(land, land, r.kv_recv, dp_n + s * lines + src).wait()
            kv = kv_sum[s, z].astype(F32)
            for shift in range(1, lines):
                kv += r.kv_land[lax.rem(z + shift, lines), s].astype(F32)
            kv = kv.astype(BF16)
            cosine, sine = tables[s, :, 0:head], tables[s, :, head : 2 * head]
            sums = list(carry)
            outs = []
            for h in range(kv_heads * (group + 1)):
                is_key = h >= kv_heads * group
                if is_key:
                    g = h - kv_heads * group
                    grad = kv[:, g * head : (g + 1) * head].astype(F32)
                else:
                    grad = grad_query[s, :, h * head : (h + 1) * head].astype(F32)
                turned = jnp.concatenate([grad[:, head // 2 :], grad[:, : head // 2]], axis=1)
                grad = grad * cosine - turned * sine
                hat, inverse = norm_rows(qk_pre[s, :, h * head : (h + 1) * head])
                sums[is_key] = sums[is_key] + jnp.sum(grad * hat, axis=0, keepdims=True)
                back = grad * (k_gain if is_key else q_gain)
                outs.append((inverse * (back - hat * jnp.mean(back * hat, axis=-1, keepdims=True))).astype(BF16))
            grad_qkv[s] = jnp.concatenate(outs + [kv[:, kv_cols:]], axis=1)
            return tuple(sums)

        q_sum, k_sum = lax.fori_loop(0, dp_n, rotate, (zero, zero))
        gain_acc[2:3, 0:head] = q_sum
        gain_acc[3:4, 0:head] = k_sum
        line.advance(1)

        @pl.loop(0, width // 512)
        def _(n):
            weights = w_qkv[span(n, 512)]
            for s in range(dp_n):
                dn1_part[s, :, span(n, 512)] = contract_cols(grad_qkv[s], weights).astype(BF16)

        dn1_sends = []
        for shift in pairs:
            to = peer(shift)
            dn1_sends.append(remote(dn1_part.at[to], r.dn1_land.at[dp], r.dn1_send, shift, r.dn1_recv, dp, (to, z, core)))
        start(dn1_sends)
        r.dn1_land[dp] = dn1_part[dp]

        @pl.loop(0, dp_n)
        def _(i):
            total = jnp.zeros((rows, cols), F32)
            for s in range(dp_n):
                total += contract_rows(normed_one[s, :, span(i, rows)], grad_qkv[s])
            qkv_part[i] = total.astype(BF16)

        pair_q = [
            remote(qkv_part.at[i, span(other, half)], r.pair_q.at[i], r.pair_send, 1 + i, r.pair_land, 1 + i, partner)
            for i in range(dp_n)
        ]
        start(pair_q)

        line.advance(1)

        slot = r.pair_slot
        pair_o.wait_recv()
        for j in range(2):
            for c in range(4):
                copy = local(r.pair_o.at[pl.ds(j * quarter, quarter), pl.ds(c * 512, 512)], slot.at[span(c, quarter), pl.ds(0, 512)], r.stage_sem, c)
                copy.start()
                copy.wait()
                mine = out_part[pl.ds(pl.multiple_of(core * half + j * quarter, quarter), quarter), pl.ds(c * 512, 512)]
                where = pl.ds(c * quarter, quarter)
                slot[where, 0:512] = (mine.astype(F32) + slot[where, 0:512].astype(F32)).astype(BF16)
            copy = local(slot.at[pl.ds(0, rows), pl.ds(0, 512)], own.at[n_ffn + j], r.stage_sem, 0)
            copy.start()
            copy.wait()
        piece = line.piece
        q_sends = []
        q_mine = []
        for i in range(dp_n):
            pair_q[i].wait_recv()
            copy = local(r.pair_q.at[i], r.pair_q_slot, r.stage_sem, 0)
            copy.start()
            copy.wait()
            mine = qkv_part.at[i, span(core, half)]
            mine[...] = (mine[...].astype(F32) + r.pair_q_slot[...].astype(F32)).astype(BF16)
        for shift in range(dp_n):
            to = peer(shift)
            for j in range(3):
                number = dp * 3 + j
                src = qkv_part.at[to, span(core, half), pl.ds(j * piece, piece)]
                if shift == 0:
                    q_mine.append(local(src, line.q_own(number), r.own_sem, number))
                else:
                    q_sends.append(remote(src, line.q_own(number), r.q_send, shift * 3 + j, r.own_sem, number, (to, z, core)))
        start(q_sends + q_mine)

        out_sends = [
            remote(r.out_keep.at[peer(shift)], r.out_land.at[dp], r.sum_send, 3 * dp_n + shift, r.land_recv, dp_n + dp, (peer(shift), z, core))
            for shift in pairs
        ]
        out_mine = local(r.out_keep.at[dp], r.out_land.at[dp], r.in_sem, 4)
        start(out_sends + [out_mine])
        line.advance(2)

        for shift in pairs:
            src = peer(shift)
            local(r.dn1_land.at[src], r.dn1_land.at[src], r.dn1_recv, src).wait()

        @pl.loop(0, tokens // 32)
        def _(i):
            where = span(i, 32)
            grad = r.dn1_land[0, where].astype(F32)
            for src in range(1, dp_n):
                grad += r.dn1_land[src, where].astype(F32)
            hat, inverse = norm_rows(r.own_x_v[where].astype(F32))
            gain_acc[0:1] += jnp.sum(grad * hat, axis=0, keepdims=True)
            back = grad * gains[0:1]
            total = grad_hidden[where] + inverse * (back - hat * jnp.mean(back * hat, axis=-1, keepdims=True))
            r.result[where] = total.astype(BF16)

        written = local(r.result, r.input_grad, r.in_sem, 0)
        written.start()
        written.wait()

        def gain_total(land, count, me):
            land[me] = gain_acc[...]
            total = land[0]
            for n in range(1, count):
                total = total + land[n]
            return total

        sends = [remote(gain_acc, r.gain_core.at[core], r.gain_send, 0, r.gain_recv, 0, partner)]
        start(sends)
        line.advance(1)
        wait(sends)
        gain_acc[...] = gain_total(r.gain_core, 2, core)
        sends = [
            remote(gain_acc, r.gain_dp.at[dp], r.gain_send, shift, r.gain_recv, shift, (peer(shift), z, core)) for shift in pairs
        ]
        start(sends)
        line.advance(1)
        wait(sends)
        gain_acc[...] = gain_total(r.gain_dp, dp_n, dp)
        sends = [
            remote(gain_acc, r.gain_z.at[z], r.gain_send, dp_n + shift, r.gain_recv, dp_n + shift,
                   (dp, lax.rem(z + shift, lines), core))
            for shift in range(1, lines)
        ]
        start(sends)
        line.advance(1)
        wait(sends)
        gain_acc[...] = gain_total(r.gain_z, lines, z)
        written = local(gain_acc, r.gain_sum, r.in_sem, 1)
        written.start()
        written.wait()

        landed(r.out_land, dp_n)
        wait([out_mine])

        @pl.loop(0, dp_n)
        def _(src):
            copy = local(r.out_land.at[src], r.land_slot, r.in_sem, 3)
            copy.start()
            copy.wait()

            @pl.loop(0, tokens // 32)
            def _(i):
                where = span(i, 32)
                hidden_in[where] += r.land_slot[where].astype(F32)

        r.result[...] = hidden_in[...].astype(BF16)
        done = local(r.result, r.output, r.in_sem, 0)
        done.start()
        done.wait()
        line.finish()

        for copy in out_sends + q_sends + dn1_sends + pair_q + [pair_o]:
            copy.wait_send()

        @pl.loop(0, dp_n)
        def _(s):
            for copy in kv_copies(s):
                copy.wait_send()

    pl.run_scoped(
        projections,
        pltpu.VMEM((width, cols), BF16), seqs(tokens, width), pltpu.VMEM((dp_n, tokens, q_cols + kv_cols), F32), seqs(tokens, q_cols),
        pltpu.VMEM((dp_n, tokens, 2 * head), F32), pltpu.VMEM((rows, width), BF16), seqs(rows, cols), seqs(tokens, width),
    )

    for copy in dx_sends:
        copy.wait_send()

    @pl.loop(1, n_blocks)
    def _(b):
        for copy in weight_copies(b)[1]:
            copy.wait_send()


def add_rows(into, left, right):
    @pl.loop(0, into.shape[0] // 32)
    def _(i):
        where = pl.ds(pl.multiple_of(i * 32, 32), 32)
        into[where] = (left[where].astype(F32) + right[where].astype(F32)).astype(BF16)


def backward(arrays, dp_n, lines, head, collective_id):
    x = arrays
    tokens, width = x.own_x.shape
    rows = width // dp_n
    f8 = x.w_down.shape[0] // 2
    n_blocks = f8 // 256
    down_block = 1024 // rows
    q_cols = x.query.shape[2]
    cols = x.w_qkv.shape[1]
    kv_cols = (cols - q_cols) // 2
    kv_heads = kv_cols // head
    per_block = down_block + dp_n
    chunks = n_blocks * per_block + 2 + dp_n * cols // 1024
    plane = 2 * dp_n * tokens
    dims = SimpleNamespace(
        dp_n=dp_n, lines=lines, tokens=tokens, width=width, rows=rows, f8=f8, n_blocks=n_blocks, per_block=per_block,
        down_block=down_block, head=head, group=q_cols // kv_cols, kv_heads=kv_heads, q_cols=q_cols, kv_cols=kv_cols,
        qkv_cols=cols, chunks=chunks, pace=1,
    )
    bf16 = lambda *shape: jax.ShapeDtypeStruct(shape, BF16)
    outs = BackOut(
        output=bf16(tokens, width), input_grad=bf16(tokens, width), gain_sum=jax.ShapeDtypeStruct((8, width), F32),
        totals=bf16(2, chunks, rows, 512), own=bf16(chunks, rows, 512), first=bf16(chunks, rows, 512),
        cross=bf16(chunks, rows, 512), w_land=bf16(n_blocks, width, 512), dn2_pair=bf16(dp_n, tokens, width), out_pair=bf16(dp_n, tokens, width), out_land=bf16(dp_n, tokens, width), out_keep=bf16(dp_n, tokens, width),
        pair_o=bf16(rows // 2, width), pair_q=bf16(dp_n, rows // 2, cols),
    )
    vmem = lambda *shape: pltpu.VMEM(shape, BF16)
    dma = lambda n: pltpu.SemaphoreType.DMA((n,))
    scratch = BackScratch(
        sum_slot=vmem(4, rows, 512), total_slot=vmem(4, rows, 512), in_slot=vmem(rows, 512),
        kv_sum=vmem(dp_n, lines, tokens, 2 * kv_cols), grad_query=vmem(dp_n, tokens, q_cols), grad_qkv=vmem(dp_n, tokens, cols),
        dn2_land=vmem(dp_n, tokens, width),
        land_slot=vmem(tokens, width), hidden_v=pltpu.VMEM((tokens, width), F32), grad_hidden=pltpu.VMEM((tokens, width), F32),
        own_x_v=vmem(tokens, width), cot_own=vmem(tokens, width), gains_v=pltpu.VMEM((8, width), F32), gain_acc=pltpu.VMEM((8, width), F32),
        dx_all=vmem(dp_n, tokens, width), kv_pair=vmem(dp_n, lines, tokens, 2 * kv_cols), kv_land=vmem(lines, dp_n, tokens, 2 * kv_cols),
        gain_core=pltpu.VMEM((2, 8, width), F32), gain_dp=pltpu.VMEM((dp_n, 8, width), F32), gain_z=pltpu.VMEM((lines, 8, width), F32),
        dn1_land=vmem(dp_n, tokens, width), result=vmem(tokens, width), pair_slot=vmem(rows, 512), pair_q_slot=vmem(rows // 2, cols),
        load_sem=dma(3), own_sem=dma(3 * dp_n), first_send=dma(chunks), first_recv=dma(chunks),
        second_send=dma(chunks), cross_recv=dma(chunks), owner_send=dma(chunks), across_send=dma(chunks), second_recv=dma(chunks), core_send=dma(chunks), core_recv=dma(chunks),
        w_send=dma(2 * n_blocks * dp_n), w_recv=dma(2 * n_blocks * dp_n), stage_sem=dma(per_block),
        in_sem=dma(8 + max(8, dp_n)), sum_send=dma(4 * dp_n), pair_recv=dma(2 * dp_n), land_recv=dma(2 * dp_n), dx_send=dma(dp_n), dx_recv=dma(dp_n),
        kv_send=dma(dp_n + dp_n * lines), kv_recv=dma(dp_n + dp_n * lines), pair_send=dma(1 + dp_n), pair_land=dma(1 + dp_n),
        dn1_send=dma(dp_n), dn1_recv=dma(dp_n), q_send=dma(3 * dp_n), gain_send=dma(dp_n + lines), gain_recv=dma(dp_n + lines),
    )
    hbm = pl.BlockSpec(memory_space=pl.ANY)
    in_vmem = pl.BlockSpec(memory_space=pltpu.VMEM)
    flops = 6 * plane * width * f8 * 3
    results = pl.pallas_call(
        partial(back_kernel, dims),
        out_shape=tuple(outs),
        in_specs=list(BackIn(*[hbm] * len(x))._replace(log_total=in_vmem)),
        out_specs=(hbm,) * len(outs),
        scratch_shapes=list(scratch),
        compiler_params=pltpu.CompilerParams(collective_id=collective_id, has_side_effects=True, vmem_limit_bytes=63 * MIB),
        cost_estimate=pl.CostEstimate(flops=flops, bytes_accessed=100 * MIB, transcendentals=0),
        name="backward",
    )(*x)
    return BackOut(*results)


def widen_piece_kernel(place, totals, out):
    out[...] = totals[0, 0].astype(F32)


def widen_halves_kernel(place, totals, left, right):
    middle = left.shape[1]
    left[...] = totals[0, 0, :, :middle].astype(F32)
    right[...] = totals[0, 0, :, middle:].astype(F32)


def widen_pair_kernel(place, totals, gate, up):
    gate[...] = totals[0, 0, :, 0:256].astype(F32)
    up[...] = totals[0, 0, :, 256:512].astype(F32)


def widen_rows_kernel(place, totals, out):
    quarter = out.shape[0]
    for c in range(4):
        out[:, c * 512 : (c + 1) * 512] = totals[0, 0, c * quarter : (c + 1) * quarter, :].astype(F32)


def widen(totals, place, dp_n, width, f8, cols, q_cols, kv_cols):
    _, chunks, rows, _ = totals.shape
    quarter, half = rows // 4, rows // 2
    down_block = 256 // quarter
    per_block = down_block + dp_n
    n_blocks = f8 // 256
    n_ffn = n_blocks * per_block
    f32 = lambda *shape: jax.ShapeDtypeStruct(shape, F32)
    params = pltpu.CompilerParams(vmem_limit_bytes=40 * MIB)

    def call(kernel, grid, in_map, out_specs, out_shape, name):
        return pl.pallas_call(
            kernel,
            grid_spec=pltpu.PrefetchScalarGridSpec(
                num_scalar_prefetch=1, grid=grid, in_specs=[pl.BlockSpec((1, 1, rows, 512), in_map)], out_specs=out_specs),
            out_shape=out_shape, compiler_params=params, name=name,
        )(place, totals)

    columns = lambda src, who, b, place: (0, (2 * src + who) * n_blocks + b)
    gate, up = call(
        widen_pair_kernel, (dp_n, 2, n_blocks),
        lambda src, who, b, place: (who, b * per_block + down_block + lax.rem(place[0] - src + dp_n, dp_n), 0, 0),
        (pl.BlockSpec((rows, 256), columns),) * 2, (f32(rows, 2 * dp_n * f8),) * 2, "widen_gate_up")
    down = call(
        widen_rows_kernel, (2, n_blocks, down_block),
        lambda who, b, j, place: (who, b * per_block + j, 0, 0),
        pl.BlockSpec((quarter, width), lambda who, b, j, place: ((who * n_blocks + b) * down_block + j, 0)),
        f32(2 * f8, width), "widen_down")
    out = call(
        widen_rows_kernel, (2, 2), lambda who, j, place: (who, n_ffn + j, 0, 0),
        pl.BlockSpec((quarter, width), lambda who, j, place: (2 * who + j, 0)), f32(rows, width), "widen_out")
    piece = cols // 3
    across = 512 // piece
    per_chunk = 2 * across

    def piece_map(number, who):
        spot = lax.rem(number, per_chunk)
        return (who, n_ffn + 2 + number // per_chunk, spot // across, lax.rem(spot, across))

    def pieces(kernel, grid, in_map, out_specs, out_shape, name):
        return pl.pallas_call(
            kernel,
            grid_spec=pltpu.PrefetchScalarGridSpec(
                num_scalar_prefetch=1, grid=grid, in_specs=[pl.BlockSpec((1, 1, half, piece), in_map)], out_specs=out_specs),
            out_shape=out_shape, compiler_params=params, name=name,
        )(place, totals)

    query = pieces(
        widen_piece_kernel, (dp_n, 2, 2), lambda src, who, j, place: piece_map(3 * src + j, who),
        pl.BlockSpec((half, piece), lambda src, who, j, place: (who, 2 * src + j)), f32(rows, dp_n * q_cols), "widen_query")
    kv_in = lambda src, who, place: piece_map(3 * src + 2, who)
    if kv_cols % 128 == 0:
        key, value = pieces(
            widen_halves_kernel, (dp_n, 2), kv_in, (pl.BlockSpec((half, kv_cols), lambda src, who, place: (who, src)),) * 2,
            (f32(rows, dp_n * kv_cols),) * 2, "widen_key_value")
    else:
        both = pieces(
            widen_piece_kernel, (dp_n, 2), kv_in, pl.BlockSpec((half, piece), lambda src, who, place: (who, src)),
            f32(rows, dp_n * piece), "widen_key_value").reshape(rows, dp_n, 2, kv_cols)
        key, value = (both[:, :, n].reshape(rows, dp_n * kv_cols) for n in range(2))
    return query, key, value, out, gate, up, down


class FrontIn(NamedTuple):
    own_x: Any
    own_cot: Any
    w_query: Any
    w_pair: Any
    gain_piece: Any
    own_tables: Any
    bias: Any
    w_out: Any
    w_gate: Any
    w_up: Any


class FrontOut(NamedTuple):
    normed_two: Any
    cot_all: Any
    w_first: Any
    hidden_in: Any
    w_qkv: Any
    normed_one: Any
    qk_pre: Any
    query: Any
    keys_values: Any
    log_total: Any
    mixed: Any
    tables: Any
    gains: Any


class FrontScratch(NamedTuple):
    x_all: Any
    n1: Any
    w_all: Any
    qk: Any
    value: Any
    q_rot: Any
    kv: Any
    log_v: Any
    mix: Any
    tables_v: Any
    gains_v: Any
    bias_v: Any
    w_out_v: Any
    part: Any
    land: Any
    hidden: Any
    n2: Any
    in_sem: Any
    out_sem: Any
    x_send: Any
    x_recv: Any
    w_send: Any
    w_recv: Any
    w_pass: Any
    w_passed: Any
    kv_send: Any
    kv_recv: Any
    kv_pass: Any
    kv_passed: Any
    part_send: Any
    part_recv: Any
    plane_send: Any
    plane_recv: Any
    plane_pass: Any
    plane_passed: Any
    first_send: Any
    first_recv: Any


def front_kernel(dims, *refs):
    r = SimpleNamespace()
    for kind, first in ((FrontIn, 0), (FrontOut, len(FrontIn._fields)), (FrontScratch, len(FrontIn._fields + FrontOut._fields))):
        vars(r).update(kind(*refs[first : first + len(kind._fields)])._asdict())
    dp_n, lines, tokens, width, rows, f8 = dims.dp_n, dims.lines, dims.tokens, dims.width, dims.rows, dims.f8
    head, group, kv_heads, q_cols, kv_cols = dims.head, dims.group, dims.kv_heads, dims.q_cols, dims.kv_cols
    length = 2 * lines * tokens
    half = rows // 2
    scale = head ** (-0.5)
    dp, z, core = places()
    other = 1 - core
    partner = (dp, z, other)
    pairs = range(1, dp_n)
    me = 2 * z + core

    def peer(shift):
        return lax.rem(dp + shift, dp_n)

    def local(src, dst, sem, n=0):
        return pltpu.make_async_copy(src, dst, sem.at[n])

    def remote(src, dst, send, n, recv, m, device):
        return pltpu.make_async_remote_copy(
            src, dst, send.at[n], recv.at[m], device_id=device, device_id_type=MESH)

    def span(index, size):
        return pl.ds(pl.multiple_of(index * size, size), size)

    def start(copies):
        for copy in copies:
            copy.start()

    def wait(copies):
        for copy in copies:
            copy.wait()

    def landed(ref, sem, n):
        local(ref, ref, sem, n).wait()

    barrier = pltpu.get_barrier_semaphore()
    for shift in pairs:
        pl.semaphore_signal(barrier, device_id=(peer(shift), z, core), device_id_type=MESH)
    pl.semaphore_signal(barrier, device_id=partner, device_id_type=MESH)
    for shift in range(1, lines):
        pl.semaphore_signal(barrier, device_id=(dp, lax.rem(z + shift, lines), core), device_id_type=MESH)

    mine = [
        local(r.own_x, r.x_all.at[dp], r.in_sem, 0), local(r.own_tables, r.tables_v.at[dp], r.in_sem, 1),
        local(r.gain_piece, r.gains_v.at[:, span(dp, rows)], r.in_sem, 2), local(r.bias, r.bias_v, r.in_sem, 3),
        local(r.w_out, r.w_out_v, r.in_sem, 4),
        local(r.w_query.at[:, span(dp, q_cols)], r.w_all.at[span(dp, rows), pl.ds(0, q_cols)], r.in_sem, 5),
        local(r.w_pair.at[dp], r.w_all.at[span(dp, rows), pl.ds(q_cols, 2 * kv_cols)], r.in_sem, 6),
    ]
    start(mine)
    pl.semaphore_wait(barrier, dp_n + lines - 1)

    small = []
    for shift in pairs:
        to = peer(shift)
        device = (to, z, core)
        small += [
            remote(r.own_x, r.x_all.at[dp], r.x_send, 3 * shift, r.x_recv, 3 * dp, device),
            remote(r.own_tables, r.tables_v.at[dp], r.x_send, 3 * shift + 1, r.x_recv, 3 * dp + 1, device),
            remote(r.gain_piece, r.gains_v.at[:, span(dp, rows)], r.x_send, 3 * shift + 2, r.x_recv, 3 * dp + 2, device),
        ]
    start(small)

    def weight_spot(src, side):
        where = pl.ds(pl.multiple_of(src * rows + side * half, half), half)
        return r.w_all.at[where, pl.ds(0, q_cols)], r.w_all.at[where, pl.ds(q_cols, 2 * kv_cols)]

    weights = []
    for shift in pairs:
        to = peer(shift)
        spots = weight_spot(dp, core)
        where = span(core, half)
        for n, src in enumerate((r.w_query.at[where, span(to, q_cols)], r.w_pair.at[to, where])):
            weights.append(remote(src, spots[n], r.w_send, 2 * shift + n, r.w_recv, 2 * dp + n, (to, z, core)))
    start(weights)

    wait(mine[1:3])
    for shift in pairs:
        landed(r.gains_v.at[:, span(peer(shift), rows)], r.x_recv, 3 * peer(shift) + 2)
    mine[0].wait()

    @pl.loop(0, dp_n)
    def _(turn):
        s = peer(turn)

        @pl.when(turn > 0)
        def _():
            landed(r.x_all.at[s], r.x_recv, 3 * s)

        @pl.loop(0, tokens // 32)
        def _(i):
            hat, _ = norm_rows(r.x_all[s, span(i, 32)].astype(F32))
            r.n1[pl.ds(pl.multiple_of(s * tokens + i * 32, 32), 32)] = (hat * r.gains_v[0:1]).astype(BF16)

    passes = []
    for shift in pairs:
        src = peer(shift)
        for n, spot in enumerate(weight_spot(src, core)):
            landed(spot, r.w_recv, 2 * src + n)
            copy = remote(spot, spot, r.w_pass, 2 * shift + n, r.w_passed, 2 * src + n, partner)
            copy.start()
            passes.append(copy)
    wait(mine[3:])
    for shift in pairs:
        src = peer(shift)
        for n, spot in enumerate(weight_spot(src, other)):
            landed(spot, r.w_passed, 2 * src + n)
        landed(r.tables_v.at[src], r.x_recv, 3 * src + 1)

    slot_of = lambda d, c: pl.ds(pl.multiple_of((2 * d + c) * tokens, tokens), tokens)

    def plane_copies(src, target, base):
        spot = target.at[slot_of(dp, core)]
        found = [remote(src, spot, r.plane_send, base + shift, r.plane_recv, base + dp, (peer(shift), z, core)) for shift in pairs]
        return found + [remote(src, spot, r.plane_send, base, r.plane_recv, base + dp_n, partner)]

    def plane_pass(target, base):
        found = []
        for shift in pairs:
            src = peer(shift)
            spot = target.at[slot_of(src, core)]
            landed(spot, r.plane_recv, base + src)
            copy = remote(spot, spot, r.plane_pass, base + shift, r.plane_passed, base + src, partner)
            copy.start()
            found.append(copy)
        return found

    def plane_done(target, base):
        landed(target.at[slot_of(dp, other)], r.plane_recv, base + dp_n)
        for shift in pairs:
            src = peer(shift)
            landed(target.at[slot_of(src, other)], r.plane_passed, base + src)

    cots = plane_copies(r.own_cot, r.cot_all, 0)
    firsts, first_mine = [], []
    for n, weight in enumerate((r.w_gate, r.w_up)):
        for shift in range(dp_n):
            to = peer(shift)
            src = weight.at[:, pl.ds(pl.multiple_of((2 * to + core) * f8, 256), 256)]
            dst = r.w_first.at[span(dp, rows), pl.ds(256 * n, 256)]
            if shift == 0:
                first_mine.append(local(src, dst, r.out_sem, n))
            else:
                firsts.append(remote(src, dst, r.first_send, 2 * shift + n, r.first_recv, 2 * dp + n, (to, z, core)))
    cot_mine = local(r.own_cot, r.cot_all.at[slot_of(dp, core)], r.out_sem, 2)
    start(cots + firsts + first_mine + [cot_mine])

    split = q_cols + kv_cols
    r.qk[:, 0:q_cols] = dot(r.n1[...], r.w_all[:, 0:q_cols])
    pair = dot(r.n1[...], r.w_all[:, q_cols : q_cols + 2 * kv_cols])
    r.qk[:, q_cols:split] = pair[:, :kv_cols]
    r.value[...] = pair[:, kv_cols:].astype(BF16)
    outs = [
        local(r.n1, r.normed_one, r.out_sem, 3), local(r.w_all, r.w_qkv, r.out_sem, 4), local(r.qk, r.qk_pre, r.out_sem, 5),
        local(r.tables_v, r.tables, r.out_sem, 6), local(r.gains_v, r.gains, r.out_sem, 7),
    ]
    start(outs)

    def kv_copies(s):
        spot = r.kv.at[me, s]
        found = [
            remote(spot, spot, r.kv_send, s * lines + shift, r.kv_recv, s * (lines + 1) + z, (dp, lax.rem(z + shift, lines), core))
            for shift in range(1, lines)
        ]
        return found + [remote(spot, spot, r.kv_send, s * lines, r.kv_recv, s * (lines + 1) + lines, partner)]

    def kv_pass(s):
        found = []
        for shift in range(1, lines):
            src = lax.rem(z + shift, lines)
            spot = r.kv.at[2 * src + core, s]
            found.append((spot, s * (lines + 1) + src,
                          remote(spot, spot, r.kv_pass, s * lines + shift, r.kv_passed, s * lines + src, partner)))
        return found

    @pl.loop(0, dp_n)
    def _(turn):
        s = peer(turn + 1)
        cosine, sine = r.tables_v[s, :, 0:head], r.tables_v[s, :, head : 2 * head]
        turned = []
        where = span(s, tokens)
        for h in range(kv_heads * (group + 1)):
            gain = r.gains_v[2:3, 0:head] if h < kv_heads * group else r.gains_v[3:4, 0:head]
            hat, _ = norm_rows(r.qk[where, h * head : (h + 1) * head])
            hat = hat * gain
            swapped = jnp.concatenate([hat[:, head // 2 :], hat[:, : head // 2]], axis=1)
            turned.append((hat * cosine + swapped * sine).astype(BF16))
        r.q_rot[s] = jnp.concatenate(turned[: kv_heads * group], axis=1)
        r.kv[me, s] = jnp.concatenate(turned[kv_heads * group :] + [r.value[where]], axis=1)
        start(kv_copies(s))

    step = max(1, min(group, MIB // (2 * length * tokens)))

    def part_copy(s, shift):
        return remote(r.part.at[s], r.land.at[dp], r.part_send, shift, r.part_recv, dp, (s, z, core))

    @pl.loop(0, dp_n)
    def _(turn):
        s = peer(turn + 1)
        for spot, n, copy in kv_pass(s):
            landed(spot, r.kv_recv, n)
            copy.start()
        landed(r.kv.at[2 * z + other, s], r.kv_recv, s * (lines + 1) + lines)
        for shift in range(1, lines):
            src = lax.rem(z + shift, lines)
            landed(r.kv.at[2 * src + other, s], r.kv_passed, s * lines + src)
        both = r.kv[:, s].reshape(length, 2 * kv_cols)
        mask = jnp.concatenate([r.bias_v[...]] * step, axis=1)
        for g in range(kv_heads):
            keys = both[:, g * head : (g + 1) * head]
            values = both[:, (kv_heads + g) * head : (kv_heads + g + 1) * head]
            for first in range(g * group, (g + 1) * group, step):
                queries = jnp.concatenate([r.q_rot[s, :, h * head : (h + 1) * head] for h in range(first, first + step)], axis=0)
                scores = contract_cols(keys, queries) * scale + mask
                top = jnp.max(scores, axis=0, keepdims=True)
                weight = jnp.exp(scores - top)
                total = jnp.sum(weight, axis=0, keepdims=True)
                probs = (weight * (1.0 / total)).astype(BF16)
                offset = (first - g * group) * tokens
                r.log_v[s, pl.ds(g, 1), offset : offset + step * tokens] = top + jnp.log(total)
                out = contract_rows(values, probs).T.astype(BF16)
                r.mix[s, :, first * head : (first + step) * head] = jnp.concatenate(
                    [out[h * tokens : (h + 1) * tokens] for h in range(step)], axis=1)
        r.part[s] = dot(r.mix[s], r.w_out_v[...]).astype(BF16)

        @pl.when(turn < dp_n - 1)
        def _():
            part_copy(s, turn + 1).start()

    outs += [
        local(r.q_rot, r.query, r.out_sem, 8), local(r.kv, r.keys_values, r.out_sem, 9),
        local(r.log_v, r.log_total, r.out_sem, 10), local(r.mix, r.mixed, r.out_sem, 11),
    ]
    start(outs[5:])

    for shift in pairs:
        landed(r.land.at[peer(shift)], r.part_recv, peer(shift))
    r.land[dp] = r.part[dp]

    @pl.loop(0, tokens // 32)
    def _(i):
        where = span(i, 32)
        total = r.land[0, where].astype(F32)
        for src in range(1, dp_n):
            total += r.land[src, where].astype(F32)
        total += r.x_all[dp, where].astype(F32)
        r.hidden[where] = total
        hat, _ = norm_rows(total)
        r.n2[where] = (hat * r.gains_v[1:2]).astype(BF16)

    n2_base = dp_n + 1
    n2_copies = plane_copies(r.n2, r.normed_two, n2_base)
    start(n2_copies)
    n2_mine = local(r.n2, r.normed_two.at[slot_of(dp, core)], r.out_sem, 12)
    outs += [local(r.hidden, r.hidden_in, r.out_sem, 13), n2_mine]
    start(outs[9:])
    passed = plane_pass(r.cot_all, 0)
    passed += plane_pass(r.normed_two, n2_base)
    plane_done(r.cot_all, 0)
    for shift in pairs:
        src = peer(shift)
        for n in range(2):
            landed(r.w_first.at[span(src, rows), pl.ds(256 * n, 256)], r.first_recv, 2 * src + n)
    plane_done(r.normed_two, n2_base)
    wait(outs + first_mine + [cot_mine])
    for copy in small + weights + passes + cots + firsts + n2_copies + passed:
        copy.wait_send()

    @pl.loop(0, dp_n)
    def _(s):
        for copy in kv_copies(s):
            copy.wait_send()
        for _, _, copy in kv_pass(s):
            copy.wait_send()

    @pl.loop(0, dp_n - 1)
    def _(turn):
        part_copy(peer(turn + 1), turn + 1).wait_send()


def forward(x, dp_n, lines, head, collective_id):
    tokens, width = x.own_x.shape
    rows = width // dp_n
    kv_cols = x.w_pair.shape[2] // 2
    q_cols = x.w_query.shape[1] // dp_n
    kv_heads = kv_cols // head
    f8 = x.w_gate.shape[1] // (2 * dp_n)
    cols = q_cols + 2 * kv_cols
    length = 2 * lines * tokens
    dims = SimpleNamespace(
        dp_n=dp_n, lines=lines, tokens=tokens, width=width, rows=rows, f8=f8, head=head, group=q_cols // kv_cols,
        kv_heads=kv_heads, q_cols=q_cols, kv_cols=kv_cols,
    )
    bf16 = lambda *shape: jax.ShapeDtypeStruct(shape, BF16)
    f32 = lambda *shape: jax.ShapeDtypeStruct(shape, F32)
    all_tokens = dp_n * tokens
    group_rows = q_cols // kv_cols * tokens
    outs = FrontOut(
        normed_two=bf16(2 * all_tokens, width), cot_all=bf16(2 * all_tokens, width), w_first=bf16(width, 512),
        hidden_in=f32(tokens, width), w_qkv=bf16(width, cols), normed_one=bf16(all_tokens, width), qk_pre=f32(all_tokens, q_cols + kv_cols),
        query=bf16(dp_n, tokens, q_cols), keys_values=bf16(2 * lines, dp_n, tokens, 2 * kv_cols), log_total=f32(dp_n, kv_heads, group_rows),
        mixed=bf16(dp_n, tokens, q_cols), tables=f32(dp_n, tokens, 2 * head), gains=f32(8, width),
    )
    vmem = lambda *shape: pltpu.VMEM(shape, BF16)
    wide = lambda *shape: pltpu.VMEM(shape, F32)
    dma = lambda n: pltpu.SemaphoreType.DMA((n,))
    scratch = FrontScratch(
        x_all=vmem(dp_n, tokens, width), n1=vmem(all_tokens, width), w_all=vmem(width, cols), qk=wide(all_tokens, q_cols + kv_cols),
        value=vmem(all_tokens, kv_cols), q_rot=vmem(dp_n, tokens, q_cols), kv=vmem(2 * lines, dp_n, tokens, 2 * kv_cols),
        log_v=wide(dp_n, kv_heads, group_rows), mix=vmem(dp_n, tokens, q_cols), tables_v=wide(dp_n, tokens, 2 * head), gains_v=wide(8, width),
        bias_v=wide(length, tokens), w_out_v=vmem(rows, width), part=vmem(dp_n, tokens, width), land=vmem(dp_n, tokens, width),
        hidden=wide(tokens, width), n2=vmem(tokens, width), in_sem=dma(7), out_sem=dma(14), x_send=dma(3 * dp_n), x_recv=dma(3 * dp_n),
        w_send=dma(2 * dp_n), w_recv=dma(2 * dp_n), w_pass=dma(2 * dp_n), w_passed=dma(2 * dp_n), kv_send=dma(dp_n * lines),
        kv_recv=dma(dp_n * (lines + 1)), kv_pass=dma(dp_n * lines), kv_passed=dma(dp_n * lines), part_send=dma(dp_n), part_recv=dma(dp_n),
        plane_send=dma(2 * dp_n + 2), plane_recv=dma(2 * dp_n + 2), plane_pass=dma(2 * dp_n + 2), plane_passed=dma(2 * dp_n + 2),
        first_send=dma(2 * dp_n), first_recv=dma(2 * dp_n),
    )
    hbm = pl.BlockSpec(memory_space=pl.ANY)
    results = pl.pallas_call(
        partial(front_kernel, dims),
        out_shape=tuple(outs),
        in_specs=[hbm] * len(x),
        out_specs=(hbm,) * len(outs),
        scratch_shapes=list(scratch),
        compiler_params=pltpu.CompilerParams(collective_id=collective_id, has_side_effects=True, vmem_limit_bytes=63 * MIB),
        cost_estimate=pl.CostEstimate(flops=10**10, bytes_accessed=50 * MIB, transcendentals=0),
        name="forward",
    )(*x)
    return FrontOut(*results)


def local(
    inputs, attn_gain, w_query, w_key, w_value, q_gain, key_norm_gain, w_out, ffn_gain,
    w_gate, w_up, w_down, stretch_map, pos_ids, cotangent,
):
    dp, lines, cores = lax.axis_size("dp"), lax.axis_size("z"), lax.axis_size("core")
    core = lax.axis_index("core")
    rows, width = inputs.shape[1], inputs.shape[2]
    head = q_gain.shape[0]
    query_width, key_width, hidden = w_query.shape[1], w_key.shape[1], w_gate.shape[1]
    half = rows // 2
    stretches = stretch_map.shape[0]
    length = stretches * half
    ctx = lax.axis_index("z") * cores + core

    index = jnp.arange(rows, dtype=jnp.int32)
    blocks = jnp.arange(stretches, dtype=jnp.int32)
    own = 2 * ctx + index // half
    query_places = jnp.sum(jnp.where(blocks[None, :] == own[:, None], stretch_map[None, :], 0), axis=1) * half + index % half
    key_places = jnp.repeat(stretch_map, half, total_repeat_length=length) * half + jnp.tile(
        jnp.arange(half, dtype=jnp.int32), stretches
    )
    bias = jnp.where(key_places[:, None] <= query_places[None, :], 0.0, MASKED_SCORE).astype(F32)
    frequency = jnp.power(F32(ROPE_BASE), -2.0 * jnp.arange(head // 2, dtype=F32) / head)
    angles = pos_ids[0].astype(F32)[:, None] * frequency[None, :]
    cosine, sine = jnp.cos(angles), jnp.sin(angles)
    tables = jnp.concatenate([cosine, cosine, -sine, sine], axis=1)
    piece = width // dp
    gain_piece = jnp.zeros((8, piece), F32).at[0].set(attn_gain.astype(F32)).at[1].set(ffn_gain.astype(F32))
    gain_piece = gain_piece.at[2, :head].set(q_gain.astype(F32)).at[3, :head].set(key_norm_gain.astype(F32))
    kv_cols, q_cols = key_width // dp, query_width // dp
    w_pair = jnp.stack(
        [jnp.concatenate([w[:, n * kv_cols : (n + 1) * kv_cols] for w in (w_key, w_value)], axis=1) for n in range(dp)]
    )
    front = forward(
        FrontIn(
            own_x=inputs[0], own_cot=cotangent[0], w_query=w_query, w_pair=w_pair, gain_piece=gain_piece, own_tables=tables,
            bias=bias, w_out=w_out, w_gate=w_gate, w_up=w_up,
        ),
        dp, lines, head, 2,
    )
    f8 = hidden // (2 * dp)
    made = backward(
        BackIn(
            normed_two=front.normed_two, cot_all=front.cot_all, w_first=front.w_first, w_gate=w_gate, w_up=w_up, w_down=w_down,
            hidden_in=front.hidden_in, w_out=w_out, w_qkv=front.w_qkv, normed_one=front.normed_one.reshape(dp, rows, width),
            qk_pre=front.qk_pre.reshape(dp, rows, q_cols + kv_cols), query=front.query, keys_values=front.keys_values,
            log_total=front.log_total, mixed=front.mixed, bias=bias, tables=front.tables, gains=front.gains, own_x=inputs[0],
        ),
        dp, lines, head, 1,
    )
    place = lax.axis_index("dp").reshape(1)
    query_grad, key_grad, value_grad, out_grad, gate_grad, up_grad, down_grad = widen(
        made.totals, place, dp, width, f8, q_cols + 2 * kv_cols, q_cols, kv_cols
    )
    gains = made.gain_sum
    return (
        made.output[None], made.input_grad[None], lax.dynamic_slice_in_dim(gains[0], place[0] * piece, piece, 0), query_grad, key_grad,
        value_grad, gains[2, :head], gains[3, :head], out_grad, lax.dynamic_slice_in_dim(gains[1], place[0] * piece, piece, 0),
        gate_grad, up_grad, down_grad,
    )


def solution(mesh):
    dp, ctx = mesh.shape["dp"], mesh.shape["ctx"]
    fine = Mesh(mesh.devices.reshape(dp, ctx // 2, 2), ("dp", "z", "core"))
    tokens = P("dp", ("z", "core"), None)
    rows = P("dp", None)
    in_specs = (
        tokens, P("dp"), rows, rows, rows, P(), P(), rows, P("dp"), rows, rows, rows, P(), P("dp", ("z", "core")), tokens,
    )
    out_specs = (tokens, tokens, P("dp"), rows, rows, rows, P(), P(), rows, P("dp"), rows, rows, rows)
    return jax.shard_map(local, mesh=fine, in_specs=in_specs, out_specs=out_specs, check_vma=False)
```

```python
from functools import partial
from types import SimpleNamespace
from typing import Any, NamedTuple

import jax
import jax.numpy as jnp
from jax import lax
from jax.experimental import pallas as pl
from jax.experimental.pallas import tpu as pltpu
from jax.sharding import Mesh, PartitionSpec as P

NORM_EPSILON = 1e-05
ROPE_BASE = 1000000.0
MASKED_SCORE = -1e30
BF16 = jnp.bfloat16
F32 = jnp.float32
MESH = pl.DeviceIdType.MESH
MIB = 2**20


def dot(left, right):
    return jnp.dot(left, right, preferred_element_type=F32)


def contract_rows(left, right):
    return lax.dot_general(left, right, (((0,), (0,)), ((), ())), preferred_element_type=F32)


def contract_cols(left, right):
    return lax.dot_general(left, right, (((1,), (1,)), ((), ())), preferred_element_type=F32)


def places():
    dp, z, core = lax.axis_index("dp"), lax.axis_index("z"), lax.axis_index("core")
    return dp, z, core


def line_of(z, lines):
    left = z < lines // 2
    step = jnp.where(left, 1, -1)
    place = jnp.where(left, z, lines - 1 - z)
    inner = z + step
    outer = jnp.clip(z - step, 0, lines - 1)
    return place, inner, outer


class Line:
    def __init__(self, refs, dims):
        vars(self).update(vars(refs))
        vars(self).update(vars(dims))
        self.dp, self.z, self.core = places()
        self.place, self.inner, self.outer = line_of(self.z, self.lines)
        self.middle = self.lines // 2 - 1
        self.side = self.z // (self.lines // 2)
        self.other = 1 - self.core
        self.second = self.totals.at[self.core]
        self.quarter = self.rows // 4
        self.half = self.rows // 2
        self.ahead = 4
        self.lag = 7 + 3 * (self.middle - self.place)
        self.most = 7 + 3 * self.middle + 3
        self.n_ffn = self.n_blocks * self.per_block
        self.q_first = self.n_ffn + 2
        self.piece = self.qkv_cols // 3
        self.across = 512 // self.piece
        self.per_chunk = 2 * self.across
        self.position = 0

    def ours(self, k):
        return lax.rem(k // self.per_block + lax.rem(k, self.per_block), 2) == self.side

    def shift_of(self, k):
        part = lax.rem(k, self.per_block) - self.down_block
        return jnp.where(k < self.n_ffn, jnp.maximum(part, 0), 0)

    def send_inner(self, k, src):
        return pltpu.make_async_remote_copy(
            src, self.first.at[k], self.first_send.at[k], self.first_recv.at[k],
            device_id=(self.dp, self.inner, self.core), device_id_type=MESH)

    def send_across(self, k, src):
        return pltpu.make_async_remote_copy(
            src, self.cross.at[k], self.first_send.at[k], self.cross_recv.at[k],
            device_id=(self.dp, self.inner, self.core), device_id_type=MESH)

    def send_owner(self, k):
        total = self.total_slot.at[lax.rem(k, 8)]
        shift = self.shift_of(k)
        local = pltpu.make_async_copy(total, self.second.at[k], self.second_recv.at[k])
        remote = pltpu.make_async_remote_copy(
            total, self.second.at[k], self.owner_send.at[k], self.second_recv.at[k],
            device_id=(lax.rem(self.dp + shift, self.dp_n), self.z, self.core), device_id_type=MESH)
        return shift, local, remote

    def spread_across(self, k):
        return pltpu.make_async_remote_copy(
            self.second.at[k], self.second.at[k], self.across_send.at[k], self.second_recv.at[k],
            device_id=(self.dp, self.inner, self.core), device_id_type=MESH)

    def spread_outer(self, k):
        return pltpu.make_async_remote_copy(
            self.second.at[k], self.second.at[k], self.second_send.at[k], self.second_recv.at[k],
            device_id=(self.dp, self.outer, self.core), device_id_type=MESH)

    def load(self, src, dst, n):
        return pltpu.make_async_copy(src, dst, self.load_sem.at[n])

    def ready(self, k):
        @pl.when(k >= self.q_first)
        def _():
            for c in range(self.per_chunk):
                number = (k - self.q_first) * self.per_chunk + c
                spot = self.q_own(number)
                pltpu.make_async_copy(spot, spot, self.own_sem.at[number]).wait()

    def stage_one(self, k):
        self.ready(k)
        mine = self.sum_slot.at[lax.rem(k, 8)]

        @pl.when(self.place == 0)
        def _():
            @pl.when(k >= self.ahead)
            def _():
                self.send_inner(k - self.ahead, self.own.at[k - self.ahead]).wait_send()

            self.send_inner(k, self.own.at[k]).start()

        @pl.when(self.place > 0)
        def _():
            self.load(self.own.at[k], mine, 0).start()
            self.send_inner(k, mine).wait_recv()
            self.load(self.first.at[k], self.in_slot, 1).start()
            self.load(self.own.at[k], mine, 0).wait()
            self.load(self.first.at[k], self.in_slot, 1).wait()
            add_chunk(mine, mine, self.in_slot)

            @pl.when(self.place < self.middle)
            def _():
                self.send_inner(k, mine).start()

            @pl.when((self.place == self.middle) & jnp.logical_not(self.ours(k)))
            def _():
                self.send_across(k, mine).start()

    def stage_sum(self, k):
        @pl.when((self.place == self.middle) & self.ours(k))
        def _():
            mine = self.sum_slot.at[lax.rem(k, 8)]
            self.send_across(k, mine).wait_recv()
            arrived = self.load(self.cross.at[k], self.in_slot, 2)
            arrived.start()
            arrived.wait()
            add_chunk(self.total_slot.at[lax.rem(k, 8)], mine, self.in_slot)
            shift, local, remote = self.send_owner(k)

            @pl.when(shift == 0)
            def _():
                local.start()

            @pl.when(shift > 0)
            def _():
                remote.start()

    def stage_sent(self, k):
        @pl.when((self.place > 0) & ((self.place < self.middle) | jnp.logical_not(self.ours(k))))
        def _():
            self.send_inner(k, self.own.at[k]).wait_send()

    def stage_handed(self, k):
        shift, _, remote = self.send_owner(k)

        @pl.when((self.place == self.middle) & self.ours(k) & (shift > 0))
        def _():
            remote.wait_send()

    def stage_two(self, k):
        self.spread_outer(k).wait_recv()

        @pl.when((self.place == self.middle) & self.ours(k))
        def _():
            self.spread_across(k).start()

        @pl.when(self.place > 0)
        def _():
            self.spread_outer(k).start()

        self.deliver(k).start()

    def stage_three(self, k):
        @pl.when((self.place == self.middle) & self.ours(k))
        def _():
            self.spread_across(k).wait_send()

        @pl.when(self.place > 0)
        def _():
            self.spread_outer(k).wait_send()

        @pl.when((self.place == 0) & (k >= self.chunks - self.ahead))
        def _():
            self.send_inner(k, self.own.at[k]).wait_send()

        self.deliver(k).wait_send()

    def q_place(self, number):
        spot = lax.rem(number, self.per_chunk)
        column = lax.rem(spot, self.across) * self.piece
        if not isinstance(column, int):
            column = pl.multiple_of(column, 128)
        return number // self.per_chunk, pl.ds((spot // self.across) * self.half, self.half), pl.ds(column, self.piece)

    def q_own(self, number):
        chunk, where, columns = self.q_place(number)
        return self.own.at[self.q_first + chunk, where, columns]

    def deliver(self, k):
        return pltpu.make_async_remote_copy(
            self.second.at[k], self.second.at[k], self.core_send.at[k], self.core_recv.at[k],
            device_id=(self.dp, self.z, self.other), device_id_type=MESH)

    def advance(self, count):
        start = self.position
        self.position += count

        @pl.loop(start, start + count)
        def _(t):
            self.slot(t)

    def slot(self, t):
        @pl.when(t < self.chunks)
        def _():
            self.stage_one(t)

        at_middle = self.place == self.middle

        def upto(most, least):
            begin = self.n_ffn - 2

            def last(n):
                caught = jnp.minimum(n - least, 2 * n - begin - most)
                return jnp.clip(jnp.where(n < begin, n - most, caught), -1, self.chunks - 1)

            return pl.loop(last(t - 1) + 1, last(t) + 1)

        def fixed(k, act):
            @pl.when((k >= 0) & (k < self.chunks))
            def _():
                act(k)

        fixed(t - 9, self.stage_handed)

        @upto(2, 1)
        def _(k):
            self.stage_sum(k)

        fixed(t - 7, self.stage_sent)

        @upto(4, 2)
        def _(k):
            @pl.when(at_middle & self.ours(k))
            def _():
                self.stage_two(k)

        steps = self.middle - self.place

        @upto(7 + 3 * steps, 3 + 2 * steps)
        def _(k):
            @pl.when(jnp.logical_not(at_middle & self.ours(k)))
            def _():
                self.stage_two(k)

        fixed(t - self.lag - 3, self.stage_three)

    def advance_at(self, first, count):
        for j in range(count):
            self.slot(first + j)

    def finish(self):
        self.advance(self.chunks + self.most - self.position)

        @pl.loop(0, self.chunks)
        def _(k):
            self.deliver(k).wait_recv()


def add_chunk(into, left, right):
    rows = into.shape[0]

    @pl.loop(0, rows // 64)
    def _(i):
        part = pl.ds(i * 64, 64)
        into[part] = (left[part].astype(F32) + right[part].astype(F32)).astype(BF16)


class BackIn(NamedTuple):
    normed_two: Any
    cot_all: Any
    w_first: Any
    w_gate: Any
    w_up: Any
    w_down: Any
    hidden_in: Any
    w_out: Any
    w_qkv: Any
    normed_one: Any
    qk_pre: Any
    query: Any
    keys_values: Any
    log_total: Any
    mixed: Any
    bias: Any
    tables: Any
    gains: Any
    own_x: Any


class BackOut(NamedTuple):
    output: Any
    input_grad: Any
    gain_sum: Any
    totals: Any
    own: Any
    first: Any
    cross: Any
    w_land: Any
    dn2_pair: Any
    out_pair: Any
    out_land: Any
    out_keep: Any


class BackScratch(NamedTuple):
    sum_slot: Any
    total_slot: Any
    in_slot: Any
    kv_sum: Any
    grad_query: Any
    grad_qkv: Any
    dn2_land: Any
    land_slot: Any
    hidden_v: Any
    grad_hidden: Any
    own_x_v: Any
    cot_own: Any
    gains_v: Any
    gain_acc: Any
    dx_all: Any
    kv_pair: Any
    kv_land: Any
    gain_core: Any
    gain_dp: Any
    gain_z: Any
    dn1_land: Any
    result: Any
    pair_slot: Any
    pair_o: Any
    pair_q: Any
    load_sem: Any
    own_sem: Any
    first_send: Any
    first_recv: Any
    second_send: Any
    cross_recv: Any
    owner_send: Any
    across_send: Any
    second_recv: Any
    core_send: Any
    core_recv: Any
    w_send: Any
    w_recv: Any
    stage_sem: Any
    in_sem: Any
    sum_send: Any
    pair_recv: Any
    land_recv: Any
    dx_send: Any
    dx_recv: Any
    kv_send: Any
    kv_recv: Any
    pair_send: Any
    pair_land: Any
    dn1_send: Any
    dn1_recv: Any
    q_send: Any
    gain_send: Any
    gain_recv: Any


def norm_rows(values):
    inverse = lax.rsqrt(jnp.mean(values * values, axis=-1, keepdims=True) + NORM_EPSILON)
    return values * inverse, inverse


def back_kernel(dims, *refs):
    r = SimpleNamespace()
    for kind, first in ((BackIn, 0), (BackOut, len(BackIn._fields)), (BackScratch, len(BackIn._fields + BackOut._fields))):
        vars(r).update(kind(*refs[first : first + len(kind._fields)])._asdict())
    dp_n, lines, tokens, width = dims.dp_n, dims.lines, dims.tokens, dims.width
    rows, f8, n_blocks, per_block, down_block = dims.rows, dims.f8, dims.n_blocks, dims.per_block, dims.down_block
    head, group, kv_heads = dims.head, dims.group, dims.kv_heads
    q_cols, kv_cols, cols = dims.q_cols, dims.kv_cols, dims.qkv_cols
    plane = 2 * dp_n * tokens
    seq_tokens = dp_n * tokens
    length = lines * 2 * tokens
    scale = head ** (-0.5)
    line = Line(r, dims)
    dp, z, core, other = line.dp, line.z, line.core, line.other
    own = r.own
    half, quarter = rows // 2, rows // 4
    partner = (dp, z, other)
    n_ffn = line.n_ffn
    pairs = range(1, dp_n)

    def peer(shift):
        return lax.rem(dp + shift, dp_n)

    def local(src, dst, sem, n=0):
        return pltpu.make_async_copy(src, dst, sem.at[n])

    def remote(src, dst, send, n, recv, m, device):
        return pltpu.make_async_remote_copy(
            src, dst, send.at[n], recv.at[m], device_id=device, device_id_type=MESH)

    def span(index, size):
        return pl.ds(pl.multiple_of(index * size, size), size)

    def start(copies):
        for copy in copies:
            copy.start()

    def wait(copies):
        for copy in copies:
            copy.wait()

    barrier = pltpu.get_barrier_semaphore()
    for shift in pairs:
        pl.semaphore_signal(barrier, device_id=(peer(shift), z, core), device_id_type=MESH)
    for shift in range(1, 2 * lines):
        spot = lax.rem(2 * z + core + shift, 2 * lines)
        pl.semaphore_signal(barrier, device_id=(dp, spot // 2, lax.rem(spot, 2)), device_id_type=MESH)

    w_land = r.w_land

    def weight_copies(b):
        mine, sent = [], []
        for c, weight in enumerate((r.w_gate, r.w_up)):
            for shift in range(dp_n):
                to = peer(shift)
                src = weight.at[:, pl.ds(pl.multiple_of((2 * to + core) * f8 + b * 256, 256), 256)]
                dst = w_land.at[b, span(dp, rows), pl.ds(c * 256, 256)]
                slot = (b * dp_n + dp) * 2 + c
                if shift == 0:
                    mine.append(local(src, dst, r.w_recv, slot))
                else:
                    sent.append(remote(src, dst, r.w_send, (b * dp_n + shift) * 2 + c, r.w_recv, slot, (to, z, core)))
        return mine, sent

    def feed_forward(act, grads, wd, w_gu, stage):
        def blocks(n2, dy):
            loads = [
                local(r.normed_two, n2, r.in_sem, 0), local(r.cot_all, dy, r.in_sem, 1),
                local(r.w_down.at[span(core, f8)], wd, r.in_sem, 2),
            ]
            start(loads)

            first_weights = local(r.w_first, w_gu.at[0], r.in_sem, 3)
            first_weights.start()

            @pl.loop(1, n_blocks)
            def _(b):
                start(weight_copies(b)[0])

            pl.semaphore_wait(barrier, dp_n - 1 + 2 * lines - 1)

            start(weight_copies(1)[1])
            wait(loads)
            first_weights.wait()

            @pl.loop(0, n_blocks)
            def _(b):
                @pl.when(b > 0)
                def _():
                    @pl.loop(0, dp_n)
                    def _(src):
                        for c in range(2):
                            dst = w_land.at[b, pl.ds(0, rows), pl.ds(c * 256, 256)]
                            local(dst, dst, r.w_recv, (b * dp_n + src) * 2 + c).wait()

                    weights = local(w_land.at[b], w_gu.at[b], r.in_sem, 3)
                    weights.start()

                    @pl.when(b + 1 < n_blocks)
                    def _():
                        start(weight_copies(b + 1)[1])

                    weights.wait()

                @pl.loop(0, plane // 256)
                def _(i):
                    where = span(i, 256)
                    both = dot(n2[where], w_gu[b])
                    gate, up = both[:, :256], both[:, 256:]
                    grad_act = contract_cols(dy[where], wd[span(b, 256)])
                    sig = jax.nn.sigmoid(gate)
                    silu = gate * sig
                    act[b, where] = (silu * up).astype(BF16)
                    grads[b, where, 0:256] = (grad_act * up * sig * (1.0 + gate * (1.0 - sig))).astype(BF16)
                    grads[b, where, 256:512] = (grad_act * silu).astype(BF16)

                def to_own(j):
                    return local(stage.at[j], own.at[b * per_block + j], r.stage_sem, j)

                @pl.loop(0, 4)
                def _(c):
                    grad = contract_rows(act[b], dy[:, span(c, 512)]).astype(BF16)
                    for j in range(down_block):
                        stage[j, span(c, quarter), :] = grad[j * quarter : (j + 1) * quarter]

                for j in range(down_block):
                    to_own(j).start()

                @pl.loop(0, dp_n)
                def _(shift):
                    stage[down_block + shift] = contract_rows(n2[:, span(peer(shift), rows)], grads[b]).astype(BF16)
                    to_own(down_block + shift).start()

                @pl.loop(0, per_block)
                def _(j):
                    to_own(j).wait()


                line.advance_at(b * 2, 2)

        pl.run_scoped(blocks, pltpu.VMEM((plane, width), BF16), pltpu.VMEM((plane, width), BF16))
        line.position = n_blocks * 2

        def sums(part):
            def own_sum(turn):
                to = peer(turn)
                return remote(part.at[to, span(core, tokens)], r.dn2_land.at[dp], r.sum_send, 2 * dp_n + turn, r.land_recv, dp, (to, z, core))

            def plane_sum(hidden, product, every):
                def to_pair(i):
                    base = 0 if hidden else dp_n
                    pair = r.dn2_pair if hidden else r.out_pair
                    return remote(part.at[i, span(other, tokens)], pair.at[i], r.sum_send, base + i, r.pair_recv, base + i, partner), pair

                @pl.loop(0, dp_n + 1)
                def _(turn):
                    @pl.when(turn < dp_n)
                    def _():
                        i = peer(turn + 1)

                        @pl.loop(0, width // 512)
                        def _(n):
                            part[i, :, span(n, 512)] = product(span(i, 2 * tokens), span(n, 512)).astype(BF16)

                        to_pair(i)[0].start()

                    @pl.when(turn > 0)
                    def _():
                        i = peer(turn)
                        copy, pair = to_pair(i)
                        copy.wait_recv()
                        copy = local(pair.at[i], r.land_slot, r.in_sem, 3)
                        copy.start()
                        copy.wait()
                        mine = part.at[i, span(core, tokens)]
                        add_rows(mine, mine, r.land_slot)
                        if hidden:
                            @pl.when(turn < dp_n)
                            def _():
                                own_sum(turn).start()
                        else:
                            local(mine, r.out_keep.at[i], r.in_sem, 7 + turn).start()

                        @pl.when(lax.rem(turn, every) == 0)
                        def _():
                            line.advance_at(line.position + turn // every - 1, 1)

                line.position += dp_n // every

            def hidden_grad(where, columns):
                total = contract_cols(grads[0, where], w_gu[0, columns])
                for b in range(1, n_blocks):
                    total += contract_cols(grads[b, where], w_gu[b, columns])
                return total

            def ffn_out(where, columns):
                total = dot(act[0, where], wd[pl.ds(0, 256), columns])
                for b in range(1, n_blocks):
                    total += dot(act[b, where], wd[pl.ds(b * 256, 256), columns])
                return total

            def pair_sent(base):
                for i in range(dp_n):
                    remote(part.at[i, span(other, tokens)], r.dn2_pair.at[i], r.sum_send, base + i, r.pair_recv, base + i, partner).wait_send()

            plane_sum(True, hidden_grad, max(1, dp_n // 4))
            mine = local(part.at[dp, span(core, tokens)], r.dn2_land.at[dp], r.in_sem, 4)
            mine.start()
            mine.wait()
            pair_sent(0)
            for shift in pairs:
                own_sum(shift).wait_send()
            plane_sum(False, ffn_out, max(1, dp_n // 2))
            for turn in range(1, dp_n + 1):
                local(part.at[0, span(core, tokens)], r.out_keep.at[0], r.in_sem, 7 + turn).wait()
            pair_sent(dp_n)

        pl.run_scoped(sums, pltpu.VMEM((dp_n, 2 * tokens, width), BF16))

    pl.run_scoped(
        feed_forward,
        pltpu.VMEM((n_blocks, plane, 256), BF16), pltpu.VMEM((n_blocks, plane, 512), BF16), pltpu.VMEM((f8, width), BF16),
        pltpu.VMEM((n_blocks, width, 512), BF16), pltpu.VMEM((per_block, rows, 512), BF16),
    )

    def landed(land, base):
        for shift in pairs:
            src = peer(shift)
            local(land.at[src], land.at[src], r.land_recv, base + src).wait()

    hidden_in, grad_hidden, gains = r.hidden_v, r.grad_hidden, r.gains_v
    own_loads = [
        local(r.cot_all.at[span(2 * dp + core, tokens)], r.cot_own, r.in_sem, 4), local(r.hidden_in, hidden_in, r.in_sem, 5), local(r.gains, gains, r.in_sem, 6), local(r.own_x, r.own_x_v, r.in_sem, 7),
    ]
    start(own_loads)
    wait(own_loads)
    landed(r.dn2_land, 0)
    gain_acc = r.gain_acc
    gain_acc[...] = jnp.zeros_like(gain_acc)

    @pl.loop(0, tokens // 32)
    def _(i):
        where = span(i, 32)
        grad = r.dn2_land[0, where].astype(F32)
        for src in range(1, dp_n):
            grad += r.dn2_land[src, where].astype(F32)
        hat, inverse = norm_rows(hidden_in[where])
        gain_acc[1:2] += jnp.sum(grad * hat, axis=0, keepdims=True)
        back = grad * gains[1:2]
        dy_own = r.cot_own
        total = dy_own[where].astype(F32) + inverse * (back - hat * jnp.mean(back * hat, axis=-1, keepdims=True))
        grad_hidden[where] = total
        r.dx_all[dp, where] = total.astype(BF16)

    dx_sends = []
    for shift in pairs:
        to = peer(shift)
        dx_sends.append(remote(r.dx_all.at[dp], r.dx_all.at[dp], r.dx_send, shift, r.dx_recv, dp, (to, z, core)))
    start(dx_sends)
    line.advance(2)

    kv_sum, grad_query, grad_qkv = r.kv_sum, r.grad_query, r.grad_qkv
    step = max(1, min(group, MIB // (4 * length * tokens)))

    def kv_copies(s):
        found = []
        for shift in range(1, lines):
            to = lax.rem(z + shift, lines)
            found.append(remote(kv_sum.at[s, to], r.kv_land.at[z, s], r.kv_send, dp_n + s * lines + shift,
                                r.kv_recv, dp_n + s * lines + z, (dp, to, core)))
        return found

    every = max(1, dp_n // 4)

    def sequences(w_out, query, keys_values, bias, grad_mixed, grad_kv):
        loads = [
            local(src, dst, r.in_sem, 8 + n)
            for n, (src, dst) in enumerate(((r.w_out, w_out), (r.query, query), (r.keys_values, keys_values), (r.bias, bias)))
        ]
        start(loads)
        wait(loads)

        def pair_copy(s):
            return remote(grad_kv.at[s, :, other], r.kv_pair.at[s], r.kv_send, s, r.kv_recv, s, partner)

        def one_sequence(turn):
            s = peer(turn)

            @pl.when(turn > 0)
            def _():
                local(r.dx_all.at[s], r.dx_all.at[s], r.dx_recv, s).wait()

            grad_mixed[...] = contract_cols(r.dx_all[s], w_out[...]).astype(BF16)
            both = keys_values[:, s].reshape(length, 2 * kv_cols)
            grads = [None] * (2 * kv_heads)
            mask = jnp.concatenate([bias[...]] * step, axis=1)
            for g in range(kv_heads):
                keys = both[:, g * head : (g + 1) * head]
                values = both[:, (kv_heads + g) * head : (kv_heads + g + 1) * head]
                key_grad = value_grad = None
                for first in range(g * group, (g + 1) * group, step):
                    names = [slice(h * head, (h + 1) * head) for h in range(first, first + step)]
                    queries = jnp.concatenate([query[s, :, n] for n in names], axis=0)
                    grad_out = jnp.concatenate([grad_mixed[:, n] for n in names], axis=0)
                    scores = contract_cols(keys, queries) * scale + mask
                    offset = (first - g * group) * tokens
                    probs = jnp.exp(scores - r.log_total[s, pl.ds(g, 1), offset : offset + step * tokens])
                    grad_probs = contract_cols(values, grad_out)
                    inner = jnp.sum(probs * grad_probs, axis=0, keepdims=True)
                    grad_scores = (probs * (grad_probs - inner)).astype(BF16)
                    key_part = dot(grad_scores, queries)
                    value_part = dot(probs.astype(BF16), grad_out)
                    key_grad = key_part if key_grad is None else key_grad + key_part
                    value_grad = value_part if value_grad is None else value_grad + value_part
                    back = (contract_rows(keys, grad_scores) * scale).T.astype(BF16)
                    grad_query[s, :, first * head : (first + step) * head] = jnp.concatenate(
                        [back[h * tokens : (h + 1) * tokens] for h in range(step)], axis=1)
                grads[g] = key_grad * scale
                grads[kv_heads + g] = value_grad
            grad_kv[s] = jnp.concatenate(grads, axis=1).astype(BF16).reshape(lines, 2, tokens, 2 * kv_cols)
            pair_copy(s).start()

        def pass_on(turn):
            s = peer(turn)
            pair_copy(s).wait_recv()

            @pl.loop(0, lines)
            def _(n):
                kv_sum[s, n] = (grad_kv[s, n, core].astype(F32) + r.kv_pair[s, n].astype(F32)).astype(BF16)

            start(kv_copies(s))

        @pl.loop(0, dp_n)
        def _(turn):
            one_sequence(turn)

            @pl.when(turn > 0)
            def _():
                pass_on(turn - 1)

            @pl.when(lax.rem(turn, every) == 0)
            def _():
                line.advance_at(line.position + turn // every, 1)

        pass_on(dp_n - 1)

        @pl.loop(0, dp_n)
        def _(s):
            pair_copy(s).wait_send()

    seqs = lambda *shape: pltpu.VMEM((dp_n,) + shape, BF16)
    pl.run_scoped(
        sequences,
        pltpu.VMEM((rows, width), BF16), seqs(tokens, q_cols), pltpu.VMEM((2 * lines, dp_n, tokens, 2 * kv_cols), BF16),
        pltpu.VMEM((length, tokens), F32), pltpu.VMEM((tokens, q_cols), BF16), seqs(lines, 2, tokens, 2 * kv_cols),
    )
    line.position += dp_n // every
    assert line.position <= n_ffn

    def projections(w_qkv, normed_one, qk_pre, mixed, tables, out_part, qkv_part, dn1_part):
        loads = [
            local(src, dst, r.in_sem, 8 + n)
            for n, (src, dst) in enumerate((
                (r.qk_pre, qk_pre), (r.tables, tables), (r.mixed, mixed), (r.normed_one, normed_one), (r.w_qkv, w_qkv)))
        ]
        start(loads)
        wait(loads)

        @pl.loop(0, width // 512)
        def _(n):
            total = jnp.zeros((rows, 512), F32)
            for s in range(dp_n):
                total += contract_rows(mixed[s], r.dx_all[s, :, span(n, 512)])
            out_part[:, span(n, 512)] = total.astype(BF16)

            @pl.when(n == 1)
            def _():
                line.advance_at(line.position, 1)

        line.position += 1

        pair_o = remote(out_part.at[span(other, half)], r.pair_o, r.pair_send, 0, r.pair_land, 0, partner)
        pair_o.start()

        q_gain, k_gain = gains[2:3, 0:head], gains[3:4, 0:head]
        zero = jnp.zeros((1, head), F32)

        def rotate(turn, carry):
            s = peer(turn)
            for shift in range(1, lines):
                src = lax.rem(z + shift, lines)
                land = r.kv_land.at[src, s]
                local(land, land, r.kv_recv, dp_n + s * lines + src).wait()
            kv = kv_sum[s, z].astype(F32)
            for shift in range(1, lines):
                kv += r.kv_land[lax.rem(z + shift, lines), s].astype(F32)
            kv = kv.astype(BF16)
            cosine, sine = tables[s, :, 0:head], tables[s, :, head : 2 * head]
            sums = list(carry)
            outs = []
            for h in range(kv_heads * (group + 1)):
                is_key = h >= kv_heads * group
                if is_key:
                    g = h - kv_heads * group
                    grad = kv[:, g * head : (g + 1) * head].astype(F32)
                else:
                    grad = grad_query[s, :, h * head : (h + 1) * head].astype(F32)
                turned = jnp.concatenate([grad[:, head // 2 :], grad[:, : head // 2]], axis=1)
                grad = grad * cosine - turned * sine
                hat, inverse = norm_rows(qk_pre[s, :, h * head : (h + 1) * head])
                sums[is_key] = sums[is_key] + jnp.sum(grad * hat, axis=0, keepdims=True)
                back = grad * (k_gain if is_key else q_gain)
                outs.append((inverse * (back - hat * jnp.mean(back * hat, axis=-1, keepdims=True))).astype(BF16))
            grad_qkv[s] = jnp.concatenate(outs + [kv[:, kv_cols:]], axis=1)

            @pl.when(lax.rem(turn, max(1, dp_n // 2)) == 0)
            def _():
                line.advance_at(line.position + turn // max(1, dp_n // 2), 1)

            return tuple(sums)

        q_sum, k_sum = lax.fori_loop(0, dp_n, rotate, (zero, zero))
        line.position += 2
        assert line.position <= n_ffn
        slot = r.pair_slot
        pair_o.wait_recv()
        for j in range(2):
            for c in range(4):
                mine = out_part[pl.ds(pl.multiple_of(core * half + j * quarter, quarter), quarter), pl.ds(c * 512, 512)]
                arrived = r.pair_o[pl.ds(j * quarter, quarter), pl.ds(c * 512, 512)]
                slot[j, pl.ds(c * quarter, quarter), :] = (mine.astype(F32) + arrived.astype(F32)).astype(BF16)
        copies = [local(slot.at[j], own.at[n_ffn + j], r.stage_sem, j) for j in range(2)]
        start(copies)
        wait(copies)
        gain_acc[2:3, 0:head] = q_sum
        gain_acc[3:4, 0:head] = k_sum
        line.advance(1)

        @pl.loop(0, dp_n)
        def _(i):
            total = jnp.zeros((rows, cols), F32)
            for s in range(dp_n):
                total += contract_rows(normed_one[s, :, span(i, rows)], grad_qkv[s])
            qkv_part[i] = total.astype(BF16)

        pair_q = [
            remote(qkv_part.at[i, span(other, half)], r.pair_q.at[i], r.pair_send, 1 + i, r.pair_land, 1 + i, partner)
            for i in range(dp_n)
        ]
        start(pair_q)
        line.advance(1)

        @pl.loop(0, width // 512)
        def _(n):
            weights = w_qkv[span(n, 512)]
            for s in range(dp_n):
                dn1_part[s, :, span(n, 512)] = contract_cols(grad_qkv[s], weights).astype(BF16)

        dn1_sends = []
        for shift in pairs:
            to = peer(shift)
            dn1_sends.append(remote(dn1_part.at[to], r.dn1_land.at[dp], r.dn1_send, shift, r.dn1_recv, dp, (to, z, core)))
        r.dn1_land[dp] = dn1_part[dp]
        line.advance(1)

        piece = line.piece
        q_sends = []
        q_mine = []
        for i in range(dp_n):
            pair_q[i].wait_recv()
            mine = qkv_part.at[i, span(core, half)]
            mine[...] = (mine[...].astype(F32) + r.pair_q[i].astype(F32)).astype(BF16)
        for shift in range(dp_n):
            to = peer(shift)
            for j in range(3):
                number = dp * 3 + j
                src = qkv_part.at[to, span(core, half), pl.ds(j * piece, piece)]
                if shift == 0:
                    q_mine.append(local(src, line.q_own(number), r.own_sem, number))
                else:
                    q_sends.append(remote(src, line.q_own(number), r.q_send, shift * 3 + j, r.own_sem, number, (to, z, core)))
        start(q_sends + q_mine)
        assert line.position <= line.q_first
        start(dn1_sends)
        line.advance(1)
        out_sends = [
            remote(r.out_keep.at[peer(shift)], r.out_land.at[dp], r.sum_send, 3 * dp_n + shift, r.land_recv, dp_n + dp, (peer(shift), z, core))
            for shift in pairs
        ]
        out_mine = local(r.out_keep.at[dp], r.out_land.at[dp], r.in_sem, 4)
        start(out_sends + [out_mine])
        line.advance(1)

        for shift in pairs:
            src = peer(shift)
            local(r.dn1_land.at[src], r.dn1_land.at[src], r.dn1_recv, src).wait()

        @pl.loop(0, tokens // 32)
        def _(i):
            where = span(i, 32)
            grad = r.dn1_land[0, where].astype(F32)
            for src in range(1, dp_n):
                grad += r.dn1_land[src, where].astype(F32)
            hat, inverse = norm_rows(r.own_x_v[where].astype(F32))
            gain_acc[0:1] += jnp.sum(grad * hat, axis=0, keepdims=True)
            back = grad * gains[0:1]
            total = grad_hidden[where] + inverse * (back - hat * jnp.mean(back * hat, axis=-1, keepdims=True))
            r.result[where] = total.astype(BF16)

        written = local(r.result, r.input_grad, r.in_sem, 0)
        written.start()
        written.wait()

        def gain_total(land, count, me):
            land[me] = gain_acc[...]
            total = land[0]
            for n in range(1, count):
                total = total + land[n]
            return total

        sends = [remote(gain_acc, r.gain_core.at[core], r.gain_send, 0, r.gain_recv, 0, partner)]
        start(sends)
        line.advance(1)
        wait(sends)
        gain_acc[...] = gain_total(r.gain_core, 2, core)
        sends = [
            remote(gain_acc, r.gain_dp.at[dp], r.gain_send, shift, r.gain_recv, shift, (peer(shift), z, core)) for shift in pairs
        ]
        start(sends)
        line.advance(1)
        wait(sends)
        gain_acc[...] = gain_total(r.gain_dp, dp_n, dp)
        sends = [
            remote(gain_acc, r.gain_z.at[z], r.gain_send, dp_n + shift, r.gain_recv, dp_n + shift,
                   (dp, lax.rem(z + shift, lines), core))
            for shift in range(1, lines)
        ]
        start(sends)
        line.advance(1)
        wait(sends)
        gain_acc[...] = gain_total(r.gain_z, lines, z)
        written = local(gain_acc, r.gain_sum, r.in_sem, 1)
        written.start()
        written.wait()

        landed(r.out_land, dp_n)
        wait([out_mine])

        @pl.loop(0, dp_n)
        def _(src):
            copy = local(r.out_land.at[src], r.land_slot, r.in_sem, 3)
            copy.start()
            copy.wait()

            @pl.loop(0, tokens // 32)
            def _(i):
                where = span(i, 32)
                hidden_in[where] += r.land_slot[where].astype(F32)

        r.result[...] = hidden_in[...].astype(BF16)
        done = local(r.result, r.output, r.in_sem, 0)
        done.start()
        done.wait()
        line.finish()

        for copy in out_sends + q_sends + dn1_sends + pair_q + [pair_o]:
            copy.wait_send()

        @pl.loop(0, dp_n)
        def _(s):
            for copy in kv_copies(s):
                copy.wait_send()

    pl.run_scoped(
        projections,
        pltpu.VMEM((width, cols), BF16), seqs(tokens, width), pltpu.VMEM((dp_n, tokens, q_cols + kv_cols), F32), seqs(tokens, q_cols),
        pltpu.VMEM((dp_n, tokens, 2 * head), F32), pltpu.VMEM((rows, width), BF16), seqs(rows, cols), seqs(tokens, width),
    )

    for copy in dx_sends:
        copy.wait_send()

    @pl.loop(1, n_blocks)
    def _(b):
        for copy in weight_copies(b)[1]:
            copy.wait_send()


def add_rows(into, left, right):
    @pl.loop(0, into.shape[0] // 32)
    def _(i):
        where = pl.ds(pl.multiple_of(i * 32, 32), 32)
        into[where] = (left[where].astype(F32) + right[where].astype(F32)).astype(BF16)


def backward(arrays, dp_n, lines, head, collective_id):
    x = arrays
    tokens, width = x.own_x.shape
    rows = width // dp_n
    f8 = x.w_down.shape[0] // 2
    n_blocks = f8 // 256
    down_block = 1024 // rows
    q_cols = x.query.shape[2]
    cols = x.w_qkv.shape[1]
    kv_cols = (cols - q_cols) // 2
    kv_heads = kv_cols // head
    per_block = down_block + dp_n
    chunks = n_blocks * per_block + 2 + dp_n * cols // 1024
    plane = 2 * dp_n * tokens
    dims = SimpleNamespace(
        dp_n=dp_n, lines=lines, tokens=tokens, width=width, rows=rows, f8=f8, n_blocks=n_blocks, per_block=per_block,
        down_block=down_block, head=head, group=q_cols // kv_cols, kv_heads=kv_heads, q_cols=q_cols, kv_cols=kv_cols,
        qkv_cols=cols, chunks=chunks,
    )
    bf16 = lambda *shape: jax.ShapeDtypeStruct(shape, BF16)
    outs = BackOut(
        output=bf16(tokens, width), input_grad=bf16(tokens, width), gain_sum=jax.ShapeDtypeStruct((8, width), F32),
        totals=bf16(2, chunks, rows, 512), own=bf16(chunks, rows, 512), first=bf16(chunks, rows, 512),
        cross=bf16(chunks, rows, 512), w_land=bf16(n_blocks, width, 512), dn2_pair=bf16(dp_n, tokens, width), out_pair=bf16(dp_n, tokens, width), out_land=bf16(dp_n, tokens, width), out_keep=bf16(dp_n, tokens, width),
    )
    vmem = lambda *shape: pltpu.VMEM(shape, BF16)
    dma = lambda n: pltpu.SemaphoreType.DMA((n,))
    scratch = BackScratch(
        sum_slot=vmem(8, rows, 512), total_slot=vmem(8, rows, 512), in_slot=vmem(rows, 512),
        kv_sum=vmem(dp_n, lines, tokens, 2 * kv_cols), grad_query=vmem(dp_n, tokens, q_cols), grad_qkv=vmem(dp_n, tokens, cols),
        dn2_land=vmem(dp_n, tokens, width),
        land_slot=vmem(tokens, width), hidden_v=pltpu.VMEM((tokens, width), F32), grad_hidden=pltpu.VMEM((tokens, width), F32),
        own_x_v=vmem(tokens, width), cot_own=vmem(tokens, width), gains_v=pltpu.VMEM((8, width), F32), gain_acc=pltpu.VMEM((8, width), F32),
        dx_all=vmem(dp_n, tokens, width), kv_pair=vmem(dp_n, lines, tokens, 2 * kv_cols), kv_land=vmem(lines, dp_n, tokens, 2 * kv_cols),
        gain_core=pltpu.VMEM((2, 8, width), F32), gain_dp=pltpu.VMEM((dp_n, 8, width), F32), gain_z=pltpu.VMEM((lines, 8, width), F32),
        dn1_land=vmem(dp_n, tokens, width), result=vmem(tokens, width), pair_slot=vmem(2, rows, 512), pair_o=vmem(rows // 2, width), pair_q=vmem(dp_n, rows // 2, cols),
        load_sem=dma(3), own_sem=dma(3 * dp_n), first_send=dma(chunks), first_recv=dma(chunks),
        second_send=dma(chunks), cross_recv=dma(chunks), owner_send=dma(chunks), across_send=dma(chunks), second_recv=dma(chunks), core_send=dma(chunks), core_recv=dma(chunks),
        w_send=dma(2 * n_blocks * dp_n), w_recv=dma(2 * n_blocks * dp_n), stage_sem=dma(per_block),
        in_sem=dma(8 + max(8, dp_n)), sum_send=dma(4 * dp_n), pair_recv=dma(2 * dp_n), land_recv=dma(2 * dp_n), dx_send=dma(dp_n), dx_recv=dma(dp_n),
        kv_send=dma(dp_n + dp_n * lines), kv_recv=dma(dp_n + dp_n * lines), pair_send=dma(1 + dp_n), pair_land=dma(1 + dp_n),
        dn1_send=dma(dp_n), dn1_recv=dma(dp_n), q_send=dma(3 * dp_n), gain_send=dma(dp_n + lines), gain_recv=dma(dp_n + lines),
    )
    hbm = pl.BlockSpec(memory_space=pl.ANY)
    in_vmem = pl.BlockSpec(memory_space=pltpu.VMEM)
    flops = 6 * plane * width * f8 * 3
    results = pl.pallas_call(
        partial(back_kernel, dims),
        out_shape=tuple(outs),
        in_specs=list(BackIn(*[hbm] * len(x))._replace(log_total=in_vmem)),
        out_specs=(hbm,) * len(outs),
        scratch_shapes=list(scratch),
        compiler_params=pltpu.CompilerParams(collective_id=collective_id, has_side_effects=True, vmem_limit_bytes=63 * MIB),
        cost_estimate=pl.CostEstimate(flops=flops, bytes_accessed=100 * MIB, transcendentals=0),
        name="backward",
    )(*x)
    return BackOut(*results)


def widen_pair_kernel(n_blocks, place, *refs):
    gate, up = refs[n_blocks:]
    for b in range(n_blocks):
        columns = slice(b * 256, (b + 1) * 256)
        gate[:, columns] = refs[b][0, 0, :, 0:256].astype(F32)
        up[:, columns] = refs[b][0, 0, :, 256:512].astype(F32)


def widen_rows(out, chunks):
    quarter = chunks[0].shape[2] // 4
    for j, chunk in enumerate(chunks):
        for c in range(4):
            out[j * quarter : (j + 1) * quarter, c * 512 : (c + 1) * 512] = chunk[0, 0, c * quarter : (c + 1) * quarter, :].astype(F32)


def widen_rows_kernel(place, *refs):
    widen_rows(refs[-1], refs[:-1])


def widen_heads_kernel(dp_n, q_cols, kv_cols, place, *refs):
    out, query, key, value = refs[-4:]
    widen_rows(out, refs[:2])
    chunks = refs[2:-4]
    half = query.shape[0]
    piece = (q_cols + 2 * kv_cols) // 3
    across = 512 // piece
    for src in range(dp_n):
        for j in range(3):
            chunk, spot = divmod(3 * src + j, 2 * across)
            row, column = spot // across * half, spot % across * piece
            part = chunks[chunk][0, 0, row : row + half, column : column + piece].astype(F32)
            if j < 2:
                query[:, src * q_cols + j * piece : src * q_cols + (j + 1) * piece] = part
            else:
                key[:, src * kv_cols : (src + 1) * kv_cols] = part[:, :kv_cols]
                value[:, src * kv_cols : (src + 1) * kv_cols] = part[:, kv_cols:]


def widen(totals, place, dp_n, width, f8, q_cols, kv_cols):
    _, chunks, rows, _ = totals.shape
    half = rows // 2
    down_block = 1024 // rows
    per_block = down_block + dp_n
    n_blocks = f8 // 256
    n_ffn = n_blocks * per_block
    f32 = lambda *shape: jax.ShapeDtypeStruct(shape, F32)

    def call(kernel, grid, in_maps, out_specs, out_shape, name):
        return pl.pallas_call(
            kernel,
            grid_spec=pltpu.PrefetchScalarGridSpec(
                num_scalar_prefetch=1, grid=grid, in_specs=[pl.BlockSpec((1, 1, rows, 512), m) for m in in_maps], out_specs=out_specs),
            out_shape=out_shape, compiler_params=pltpu.CompilerParams(vmem_limit_bytes=48 * MIB), name=name,
        )(place, *[totals] * len(in_maps))

    def gate_map(b):
        return lambda src, who, place: (who, b * per_block + down_block + lax.rem(place[0] - src + dp_n, dp_n), 0, 0)

    gate, up = call(
        partial(widen_pair_kernel, n_blocks), (dp_n, 2), [gate_map(b) for b in range(n_blocks)],
        (pl.BlockSpec((rows, f8), lambda src, who, place: (0, 2 * src + who)),) * 2, (f32(rows, 2 * dp_n * f8),) * 2, "widen_gate_up")

    def down_map(j):
        return lambda who, b, place: (who, b * per_block + j, 0, 0)

    down = call(
        widen_rows_kernel, (2, n_blocks), [down_map(j) for j in range(down_block)],
        pl.BlockSpec((256, width), lambda who, b, place: (who * n_blocks + b, 0)), f32(2 * f8, width), "widen_down")

    def tail_map(k):
        return lambda who, place: (who, k, 0, 0)

    half_rows = lambda columns: pl.BlockSpec((half, columns), lambda who, place: (who, 0))
    widths = (width, dp_n * q_cols, dp_n * kv_cols, dp_n * kv_cols)
    out, query, key, value = call(
        partial(widen_heads_kernel, dp_n, q_cols, kv_cols), (2,), [tail_map(k) for k in range(n_ffn, chunks)],
        tuple(half_rows(columns) for columns in widths), tuple(f32(rows, columns) for columns in widths), "widen_heads")
    return query, key, value, out, gate, up, down


class FrontIn(NamedTuple):
    own_x: Any
    own_cot: Any
    w_query: Any
    w_key: Any
    w_value: Any
    gain_piece: Any
    own_tables: Any
    bias: Any
    w_out: Any
    w_gate: Any
    w_up: Any


class FrontOut(NamedTuple):
    normed_two: Any
    cot_all: Any
    w_first: Any
    hidden_in: Any
    w_qkv: Any
    normed_one: Any
    qk_pre: Any
    query: Any
    keys_values: Any
    log_total: Any
    mixed: Any
    tables: Any
    gains: Any


class FrontScratch(NamedTuple):
    x_all: Any
    n1: Any
    w_all: Any
    qk: Any
    value: Any
    q_rot: Any
    kv: Any
    log_v: Any
    mix: Any
    tables_v: Any
    gains_v: Any
    bias_v: Any
    w_out_v: Any
    part: Any
    land: Any
    hidden: Any
    n2: Any
    in_sem: Any
    out_sem: Any
    x_send: Any
    x_recv: Any
    w_send: Any
    w_recv: Any
    w_pass: Any
    w_passed: Any
    kv_send: Any
    kv_recv: Any
    kv_pass: Any
    kv_passed: Any
    part_send: Any
    part_recv: Any
    plane_send: Any
    plane_recv: Any
    plane_pass: Any
    plane_passed: Any
    first_send: Any
    first_recv: Any


def front_kernel(dims, *refs):
    r = SimpleNamespace()
    for kind, first in ((FrontIn, 0), (FrontOut, len(FrontIn._fields)), (FrontScratch, len(FrontIn._fields + FrontOut._fields))):
        vars(r).update(kind(*refs[first : first + len(kind._fields)])._asdict())
    dp_n, lines, tokens, width, rows, f8 = dims.dp_n, dims.lines, dims.tokens, dims.width, dims.rows, dims.f8
    head, group, kv_heads, q_cols, kv_cols = dims.head, dims.group, dims.kv_heads, dims.q_cols, dims.kv_cols
    length = 2 * lines * tokens
    half = rows // 2
    scale = head ** (-0.5)
    dp, z, core = places()
    other = 1 - core
    partner = (dp, z, other)
    pairs = range(1, dp_n)
    me = 2 * z + core

    def peer(shift):
        return lax.rem(dp + shift, dp_n)

    def local(src, dst, sem, n=0):
        return pltpu.make_async_copy(src, dst, sem.at[n])

    def remote(src, dst, send, n, recv, m, device):
        return pltpu.make_async_remote_copy(
            src, dst, send.at[n], recv.at[m], device_id=device, device_id_type=MESH)

    def span(index, size):
        return pl.ds(pl.multiple_of(index * size, size), size)

    def start(copies):
        for copy in copies:
            copy.start()

    def wait(copies):
        for copy in copies:
            copy.wait()

    def landed(ref, sem, n):
        local(ref, ref, sem, n).wait()

    barrier = pltpu.get_barrier_semaphore()
    for shift in pairs:
        pl.semaphore_signal(barrier, device_id=(peer(shift), z, core), device_id_type=MESH)
    pl.semaphore_signal(barrier, device_id=partner, device_id_type=MESH)
    for shift in range(1, lines):
        pl.semaphore_signal(barrier, device_id=(dp, lax.rem(z + shift, lines), core), device_id_type=MESH)

    mine = [
        local(r.own_x, r.x_all.at[dp], r.in_sem, 0), local(r.own_tables, r.tables_v.at[dp], r.in_sem, 1),
        local(r.gain_piece, r.gains_v.at[:, span(dp, rows)], r.in_sem, 2), local(r.bias, r.bias_v, r.in_sem, 3),
        local(r.w_out, r.w_out_v, r.in_sem, 4),
    ]
    ends = (0, q_cols, q_cols + kv_cols, q_cols + 2 * kv_cols) if kv_cols % 128 == 0 else (0, q_cols, q_cols + 2 * kv_cols)
    n_pieces = len(ends) - 1

    def weight_from(to, where):
        if n_pieces == 3:
            return [r.w_query.at[where, span(to, q_cols)], r.w_key.at[where, span(to, kv_cols)], r.w_value.at[where, span(to, kv_cols)]]
        return [r.w_query.at[where, span(to, q_cols)], r.w_key.at[to, where]]

    def weight_to(where):
        return [r.w_all.at[where, pl.ds(a, b - a)] for a, b in zip(ends, ends[1:])]

    whole = pl.ds(0, rows)
    mine += [local(src, dst, r.in_sem, 5 + n) for n, (src, dst) in enumerate(zip(weight_from(dp, whole), weight_to(span(dp, rows))))]
    start(mine)
    pl.semaphore_wait(barrier, dp_n + lines - 1)

    small = []
    for shift in pairs:
        to = peer(shift)
        device = (to, z, core)
        small += [
            remote(r.own_x, r.x_all.at[dp], r.x_send, 3 * shift, r.x_recv, 3 * dp, device),
            remote(r.own_tables, r.tables_v.at[dp], r.x_send, 3 * shift + 1, r.x_recv, 3 * dp + 1, device),
            remote(r.gain_piece, r.gains_v.at[:, span(dp, rows)], r.x_send, 3 * shift + 2, r.x_recv, 3 * dp + 2, device),
        ]
    start(small)

    def weight_spot(src, side):
        return weight_to(pl.ds(pl.multiple_of(src * rows + side * half, half), half))

    weights = []
    for shift in pairs:
        to = peer(shift)
        for n, (src, dst) in enumerate(zip(weight_from(to, span(core, half)), weight_spot(dp, core))):
            weights.append(remote(src, dst, r.w_send, 3 * shift + n, r.w_recv, 3 * dp + n, (to, z, core)))
    start(weights)

    wait(mine[1:3])
    for shift in pairs:
        landed(r.gains_v.at[:, span(peer(shift), rows)], r.x_recv, 3 * peer(shift) + 2)
    mine[0].wait()

    @pl.loop(0, dp_n)
    def _(turn):
        s = peer(turn)

        @pl.when(turn > 0)
        def _():
            landed(r.x_all.at[s], r.x_recv, 3 * s)

        @pl.loop(0, tokens // 32)
        def _(i):
            hat, _ = norm_rows(r.x_all[s, span(i, 32)].astype(F32))
            r.n1[pl.ds(pl.multiple_of(s * tokens + i * 32, 32), 32)] = (hat * r.gains_v[0:1]).astype(BF16)

    passes = []
    for shift in pairs:
        src = peer(shift)
        for n, spot in enumerate(weight_spot(src, core)):
            landed(spot, r.w_recv, 3 * src + n)
            copy = remote(spot, spot, r.w_pass, 3 * shift + n, r.w_passed, 3 * src + n, partner)
            copy.start()
            passes.append(copy)
    wait(mine[3:])
    for shift in pairs:
        src = peer(shift)
        for n, spot in enumerate(weight_spot(src, other)):
            landed(spot, r.w_passed, 3 * src + n)
        landed(r.tables_v.at[src], r.x_recv, 3 * src + 1)

    slot_of = lambda d, c: pl.ds(pl.multiple_of((2 * d + c) * tokens, tokens), tokens)

    def plane_copies(src, target, base):
        spot = target.at[slot_of(dp, core)]
        found = [remote(src, spot, r.plane_send, base + shift, r.plane_recv, base + dp, (peer(shift), z, core)) for shift in pairs]
        return found + [remote(src, spot, r.plane_send, base, r.plane_recv, base + dp_n, partner)]

    def plane_pass(target, base):
        found = []
        for shift in pairs:
            src = peer(shift)
            spot = target.at[slot_of(src, core)]
            landed(spot, r.plane_recv, base + src)
            copy = remote(spot, spot, r.plane_pass, base + shift, r.plane_passed, base + src, partner)
            copy.start()
            found.append(copy)
        return found

    def plane_done(target, base):
        landed(target.at[slot_of(dp, other)], r.plane_recv, base + dp_n)
        for shift in pairs:
            src = peer(shift)
            landed(target.at[slot_of(src, other)], r.plane_passed, base + src)

    cots = plane_copies(r.own_cot, r.cot_all, 0)
    firsts, first_mine = [], []
    for n, weight in enumerate((r.w_gate, r.w_up)):
        for shift in range(dp_n):
            to = peer(shift)
            src = weight.at[:, pl.ds(pl.multiple_of((2 * to + core) * f8, 256), 256)]
            dst = r.w_first.at[span(dp, rows), pl.ds(256 * n, 256)]
            if shift == 0:
                first_mine.append(local(src, dst, r.out_sem, n))
            else:
                firsts.append(remote(src, dst, r.first_send, 2 * shift + n, r.first_recv, 2 * dp + n, (to, z, core)))
    cot_mine = local(r.own_cot, r.cot_all.at[slot_of(dp, core)], r.out_sem, 2)
    start(cots + firsts + first_mine + [cot_mine])

    split = q_cols + kv_cols
    r.qk[:, 0:q_cols] = dot(r.n1[...], r.w_all[:, 0:q_cols])
    pair = dot(r.n1[...], r.w_all[:, q_cols : q_cols + 2 * kv_cols])
    r.qk[:, q_cols:split] = pair[:, :kv_cols]
    r.value[...] = pair[:, kv_cols:].astype(BF16)
    outs = [
        local(r.n1, r.normed_one, r.out_sem, 3), local(r.w_all, r.w_qkv, r.out_sem, 4), local(r.qk, r.qk_pre, r.out_sem, 5),
        local(r.tables_v, r.tables, r.out_sem, 6), local(r.gains_v, r.gains, r.out_sem, 7),
    ]
    start(outs)

    def kv_copies(s):
        spot = r.kv.at[me, s]
        found = [
            remote(spot, spot, r.kv_send, s * lines + shift, r.kv_recv, s * (lines + 1) + z, (dp, lax.rem(z + shift, lines), core))
            for shift in range(1, lines)
        ]
        return found + [remote(spot, spot, r.kv_send, s * lines, r.kv_recv, s * (lines + 1) + lines, partner)]

    def kv_pass(s):
        found = []
        for shift in range(1, lines):
            src = lax.rem(z + shift, lines)
            spot = r.kv.at[2 * src + core, s]
            found.append((spot, s * (lines + 1) + src,
                          remote(spot, spot, r.kv_pass, s * lines + shift, r.kv_passed, s * lines + src, partner)))
        return found

    @pl.loop(0, dp_n)
    def _(turn):
        s = peer(turn + 1)
        cosine, sine = r.tables_v[s, :, 0:head], r.tables_v[s, :, head : 2 * head]
        turned = []
        where = span(s, tokens)
        for h in range(kv_heads * (group + 1)):
            gain = r.gains_v[2:3, 0:head] if h < kv_heads * group else r.gains_v[3:4, 0:head]
            hat, _ = norm_rows(r.qk[where, h * head : (h + 1) * head])
            hat = hat * gain
            swapped = jnp.concatenate([hat[:, head // 2 :], hat[:, : head // 2]], axis=1)
            turned.append((hat * cosine + swapped * sine).astype(BF16))
        r.q_rot[s] = jnp.concatenate(turned[: kv_heads * group], axis=1)
        r.kv[me, s] = jnp.concatenate(turned[kv_heads * group :] + [r.value[where]], axis=1)
        start(kv_copies(s))

    step = max(1, min(group, MIB // (2 * length * tokens)))

    def part_copy(s, shift):
        return remote(r.part.at[s], r.land.at[dp], r.part_send, shift, r.part_recv, dp, (s, z, core))

    @pl.loop(0, dp_n)
    def _(turn):
        s = peer(turn + 1)
        for spot, n, copy in kv_pass(s):
            landed(spot, r.kv_recv, n)
            copy.start()
        landed(r.kv.at[2 * z + other, s], r.kv_recv, s * (lines + 1) + lines)
        for shift in range(1, lines):
            src = lax.rem(z + shift, lines)
            landed(r.kv.at[2 * src + other, s], r.kv_passed, s * lines + src)
        both = r.kv[:, s].reshape(length, 2 * kv_cols)
        mask = jnp.concatenate([r.bias_v[...]] * step, axis=1)
        for g in range(kv_heads):
            keys = both[:, g * head : (g + 1) * head]
            values = both[:, (kv_heads + g) * head : (kv_heads + g + 1) * head]
            for first in range(g * group, (g + 1) * group, step):
                queries = jnp.concatenate([r.q_rot[s, :, h * head : (h + 1) * head] for h in range(first, first + step)], axis=0)
                scores = contract_cols(keys, queries) * scale + mask
                top = jnp.max(scores, axis=0, keepdims=True)
                weight = jnp.exp(scores - top)
                total = jnp.sum(weight, axis=0, keepdims=True)
                probs = (weight * (1.0 / total)).astype(BF16)
                offset = (first - g * group) * tokens
                r.log_v[s, pl.ds(g, 1), offset : offset + step * tokens] = top + jnp.log(total)
                out = contract_rows(values, probs).T.astype(BF16)
                r.mix[s, :, first * head : (first + step) * head] = jnp.concatenate(
                    [out[h * tokens : (h + 1) * tokens] for h in range(step)], axis=1)
        r.part[s] = dot(r.mix[s], r.w_out_v[...]).astype(BF16)

        @pl.when(turn < dp_n - 1)
        def _():
            part_copy(s, turn + 1).start()

    outs += [
        local(r.q_rot, r.query, r.out_sem, 8), local(r.kv, r.keys_values, r.out_sem, 9),
        local(r.log_v, r.log_total, r.out_sem, 10), local(r.mix, r.mixed, r.out_sem, 11),
    ]
    start(outs[5:])

    for shift in pairs:
        landed(r.land.at[peer(shift)], r.part_recv, peer(shift))
    r.land[dp] = r.part[dp]

    @pl.loop(0, tokens // 32)
    def _(i):
        where = span(i, 32)
        total = r.land[0, where].astype(F32)
        for src in range(1, dp_n):
            total += r.land[src, where].astype(F32)
        total += r.x_all[dp, where].astype(F32)
        r.hidden[where] = total
        hat, _ = norm_rows(total)
        r.n2[where] = (hat * r.gains_v[1:2]).astype(BF16)

    n2_base = dp_n + 1
    n2_copies = plane_copies(r.n2, r.normed_two, n2_base)
    start(n2_copies)
    n2_mine = local(r.n2, r.normed_two.at[slot_of(dp, core)], r.out_sem, 12)
    outs += [local(r.hidden, r.hidden_in, r.out_sem, 13), n2_mine]
    start(outs[9:])
    passed = plane_pass(r.cot_all, 0)
    passed += plane_pass(r.normed_two, n2_base)
    plane_done(r.cot_all, 0)
    for shift in pairs:
        src = peer(shift)
        for n in range(2):
            landed(r.w_first.at[span(src, rows), pl.ds(256 * n, 256)], r.first_recv, 2 * src + n)
    plane_done(r.normed_two, n2_base)
    wait(outs + first_mine + [cot_mine])
    for copy in small + weights + passes + cots + firsts + n2_copies + passed:
        copy.wait_send()

    @pl.loop(0, dp_n)
    def _(s):
        for copy in kv_copies(s):
            copy.wait_send()
        for _, _, copy in kv_pass(s):
            copy.wait_send()

    @pl.loop(0, dp_n - 1)
    def _(turn):
        part_copy(peer(turn + 1), turn + 1).wait_send()


def forward(x, dp_n, lines, head, collective_id):
    tokens, width = x.own_x.shape
    rows = width // dp_n
    q_cols = x.w_query.shape[1] // dp_n
    kv_cols = x.w_value.shape[1] // dp_n
    kv_heads = kv_cols // head
    f8 = x.w_gate.shape[1] // (2 * dp_n)
    cols = q_cols + 2 * kv_cols
    length = 2 * lines * tokens
    dims = SimpleNamespace(
        dp_n=dp_n, lines=lines, tokens=tokens, width=width, rows=rows, f8=f8, head=head, group=q_cols // kv_cols,
        kv_heads=kv_heads, q_cols=q_cols, kv_cols=kv_cols,
    )
    bf16 = lambda *shape: jax.ShapeDtypeStruct(shape, BF16)
    f32 = lambda *shape: jax.ShapeDtypeStruct(shape, F32)
    all_tokens = dp_n * tokens
    group_rows = q_cols // kv_cols * tokens
    outs = FrontOut(
        normed_two=bf16(2 * all_tokens, width), cot_all=bf16(2 * all_tokens, width), w_first=bf16(width, 512),
        hidden_in=f32(tokens, width), w_qkv=bf16(width, cols), normed_one=bf16(all_tokens, width), qk_pre=f32(all_tokens, q_cols + kv_cols),
        query=bf16(dp_n, tokens, q_cols), keys_values=bf16(2 * lines, dp_n, tokens, 2 * kv_cols), log_total=f32(dp_n, kv_heads, group_rows),
        mixed=bf16(dp_n, tokens, q_cols), tables=f32(dp_n, tokens, 2 * head), gains=f32(8, width),
    )
    vmem = lambda *shape: pltpu.VMEM(shape, BF16)
    wide = lambda *shape: pltpu.VMEM(shape, F32)
    dma = lambda n: pltpu.SemaphoreType.DMA((n,))
    scratch = FrontScratch(
        x_all=vmem(dp_n, tokens, width), n1=vmem(all_tokens, width), w_all=vmem(width, cols), qk=wide(all_tokens, q_cols + kv_cols),
        value=vmem(all_tokens, kv_cols), q_rot=vmem(dp_n, tokens, q_cols), kv=vmem(2 * lines, dp_n, tokens, 2 * kv_cols),
        log_v=wide(dp_n, kv_heads, group_rows), mix=vmem(dp_n, tokens, q_cols), tables_v=wide(dp_n, tokens, 2 * head), gains_v=wide(8, width),
        bias_v=wide(length, tokens), w_out_v=vmem(rows, width), part=vmem(dp_n, tokens, width), land=vmem(dp_n, tokens, width),
        hidden=wide(tokens, width), n2=vmem(tokens, width), in_sem=dma(8), out_sem=dma(14), x_send=dma(3 * dp_n), x_recv=dma(3 * dp_n),
        w_send=dma(3 * dp_n), w_recv=dma(3 * dp_n), w_pass=dma(3 * dp_n), w_passed=dma(3 * dp_n), kv_send=dma(dp_n * lines),
        kv_recv=dma(dp_n * (lines + 1)), kv_pass=dma(dp_n * lines), kv_passed=dma(dp_n * lines), part_send=dma(dp_n), part_recv=dma(dp_n),
        plane_send=dma(2 * dp_n + 2), plane_recv=dma(2 * dp_n + 2), plane_pass=dma(2 * dp_n + 2), plane_passed=dma(2 * dp_n + 2),
        first_send=dma(2 * dp_n), first_recv=dma(2 * dp_n),
    )
    hbm = pl.BlockSpec(memory_space=pl.ANY)
    results = pl.pallas_call(
        partial(front_kernel, dims),
        out_shape=tuple(outs),
        in_specs=[hbm] * len(x),
        out_specs=(hbm,) * len(outs),
        scratch_shapes=list(scratch),
        compiler_params=pltpu.CompilerParams(collective_id=collective_id, has_side_effects=True, vmem_limit_bytes=63 * MIB),
        cost_estimate=pl.CostEstimate(flops=10**10, bytes_accessed=50 * MIB, transcendentals=0),
        name="forward",
    )(*x)
    return FrontOut(*results)


def local(
    inputs, attn_gain, w_query, w_key, w_value, q_gain, key_norm_gain, w_out, ffn_gain,
    w_gate, w_up, w_down, stretch_map, pos_ids, cotangent,
):
    dp, lines, cores = lax.axis_size("dp"), lax.axis_size("z"), lax.axis_size("core")
    core = lax.axis_index("core")
    rows, width = inputs.shape[1], inputs.shape[2]
    head = q_gain.shape[0]
    query_width, key_width, hidden = w_query.shape[1], w_key.shape[1], w_gate.shape[1]
    half = rows // 2
    stretches = stretch_map.shape[0]
    length = stretches * half
    ctx = lax.axis_index("z") * cores + core

    within = jnp.arange(half, dtype=jnp.int32)
    key_places = (stretch_map[:, None] * half + within[None, :]).reshape(length)
    query_places = lax.dynamic_slice_in_dim(key_places, ctx * rows, rows, 0)
    bias = jnp.where(key_places[:, None] <= query_places[None, :], 0.0, MASKED_SCORE).astype(F32)
    frequency = jnp.power(F32(ROPE_BASE), -2.0 * jnp.arange(head // 2, dtype=F32) / head)
    angles = pos_ids[0].astype(F32)[:, None] * frequency[None, :]
    cosine, sine = jnp.cos(angles), jnp.sin(angles)
    tables = jnp.concatenate([cosine, cosine, -sine, sine], axis=1)
    piece = width // dp
    gain_piece = jnp.zeros((8, piece), F32).at[0].set(attn_gain.astype(F32)).at[1].set(ffn_gain.astype(F32))
    gain_piece = gain_piece.at[2, :head].set(q_gain.astype(F32)).at[3, :head].set(key_norm_gain.astype(F32))
    kv_cols, q_cols = key_width // dp, query_width // dp
    if kv_cols % 128 == 0:
        pair = (w_key, w_value)
    else:
        cut = [jnp.concatenate([w[:, n * kv_cols : (n + 1) * kv_cols] for w in (w_key, w_value)], axis=1) for n in range(dp)]
        pair = (jnp.stack(cut), w_value)
    front = forward(
        FrontIn(
            own_x=inputs[0], own_cot=cotangent[0], w_query=w_query, w_key=pair[0], w_value=pair[1], gain_piece=gain_piece, own_tables=tables,
            bias=bias, w_out=w_out, w_gate=w_gate, w_up=w_up,
        ),
        dp, lines, head, 2,
    )
    f8 = hidden // (2 * dp)
    made = backward(
        BackIn(
            normed_two=front.normed_two, cot_all=front.cot_all, w_first=front.w_first, w_gate=w_gate, w_up=w_up, w_down=w_down,
            hidden_in=front.hidden_in, w_out=w_out, w_qkv=front.w_qkv, normed_one=front.normed_one.reshape(dp, rows, width),
            qk_pre=front.qk_pre.reshape(dp, rows, q_cols + kv_cols), query=front.query, keys_values=front.keys_values,
            log_total=front.log_total, mixed=front.mixed, bias=bias, tables=front.tables, gains=front.gains, own_x=inputs[0],
        ),
        dp, lines, head, 1,
    )
    place = lax.axis_index("dp").reshape(1)
    query_grad, key_grad, value_grad, out_grad, gate_grad, up_grad, down_grad = widen(
        made.totals, place, dp, width, f8, q_cols, kv_cols
    )
    gains = made.gain_sum
    return (
        made.output[None], made.input_grad[None], lax.dynamic_slice_in_dim(gains[0], place[0] * piece, piece, 0), query_grad, key_grad,
        value_grad, gains[2, :head], gains[3, :head], out_grad, lax.dynamic_slice_in_dim(gains[1], place[0] * piece, piece, 0),
        gate_grad, up_grad, down_grad,
    )


def solution(mesh):
    dp, ctx = mesh.shape["dp"], mesh.shape["ctx"]
    fine = Mesh(mesh.devices.reshape(dp, ctx // 2, 2), ("dp", "z", "core"))
    tokens = P("dp", ("z", "core"), None)
    rows = P("dp", None)
    in_specs = (
        tokens, P("dp"), rows, rows, rows, P(), P(), rows, P("dp"), rows, rows, rows, P(), P("dp", ("z", "core")), tokens,
    )
    out_specs = (tokens, tokens, P("dp"), rows, rows, rows, P(), P(), rows, P("dp"), rows, rows, rows)
    return jax.shard_map(local, mesh=fine, in_specs=in_specs, out_specs=out_specs, check_vma=False)
```

```python
from functools import partial
from types import SimpleNamespace
from typing import Any, NamedTuple

import jax
import jax.numpy as jnp
from jax import lax
from jax.experimental import pallas as pl
from jax.experimental.pallas import tpu as pltpu
from jax.sharding import Mesh, PartitionSpec as P

NORM_EPSILON = 1e-05
ROPE_BASE = 1000000.0
MASKED_SCORE = -1e30
BF16 = jnp.bfloat16
F32 = jnp.float32
MESH = pl.DeviceIdType.MESH
MIB = 2**20


def dot(left, right):
    return jnp.dot(left, right, preferred_element_type=F32)


def contract_rows(left, right):
    return lax.dot_general(left, right, (((0,), (0,)), ((), ())), preferred_element_type=F32)


def contract_cols(left, right):
    return lax.dot_general(left, right, (((1,), (1,)), ((), ())), preferred_element_type=F32)


def places():
    dp, z, core = lax.axis_index("dp"), lax.axis_index("z"), lax.axis_index("core")
    return dp, z, core


def line_of(z, lines):
    left = z < lines // 2
    step = jnp.where(left, 1, -1)
    place = jnp.where(left, z, lines - 1 - z)
    inner = z + step
    outer = jnp.clip(z - step, 0, lines - 1)
    return place, inner, outer


class Line:
    def __init__(self, refs, dims):
        vars(self).update(vars(refs))
        vars(self).update(vars(dims))
        self.dp, self.z, self.core = places()
        self.place, self.inner, self.outer = line_of(self.z, self.lines)
        self.middle = self.lines // 2 - 1
        self.side = self.z // (self.lines // 2)
        self.other = 1 - self.core
        self.second = self.totals.at[self.core]
        self.quarter = self.rows // 4
        self.half = self.rows // 2
        self.ahead = 4
        self.lag = 7 + 4 * (self.middle - self.place)
        self.most = 7 + 4 * self.middle + 3
        self.n_ffn = self.n_blocks * self.per_block
        self.q_first = self.n_ffn + 2
        self.piece = self.qkv_cols // 3
        self.across = 512 // self.piece
        self.per_chunk = 2 * self.across
        self.position = 0

    def ours(self, k):
        return lax.rem(k // self.per_block + lax.rem(k, self.per_block), 2) == self.side

    def shift_of(self, k):
        part = lax.rem(k, self.per_block) - self.down_block
        return jnp.where(k < self.n_ffn, jnp.maximum(part, 0), 0)

    def send_inner(self, k, src):
        return pltpu.make_async_remote_copy(
            src, self.first.at[k], self.first_send.at[k], self.first_recv.at[k],
            device_id=(self.dp, self.inner, self.core), device_id_type=MESH)

    def send_across(self, k, src):
        return pltpu.make_async_remote_copy(
            src, self.cross.at[k], self.first_send.at[k], self.cross_recv.at[k],
            device_id=(self.dp, self.inner, self.core), device_id_type=MESH)

    def send_owner(self, k):
        total = self.total_slot.at[lax.rem(k, 8)]
        shift = self.shift_of(k)
        local = pltpu.make_async_copy(total, self.second.at[k], self.second_recv.at[k])
        remote = pltpu.make_async_remote_copy(
            total, self.second.at[k], self.owner_send.at[k], self.second_recv.at[k],
            device_id=(lax.rem(self.dp + shift, self.dp_n), self.z, self.core), device_id_type=MESH)
        return shift, local, remote

    def spread_across(self, k):
        return pltpu.make_async_remote_copy(
            self.second.at[k], self.second.at[k], self.across_send.at[k], self.second_recv.at[k],
            device_id=(self.dp, self.inner, self.core), device_id_type=MESH)

    def spread_outer(self, k):
        return pltpu.make_async_remote_copy(
            self.second.at[k], self.second.at[k], self.second_send.at[k], self.second_recv.at[k],
            device_id=(self.dp, self.outer, self.core), device_id_type=MESH)

    def load(self, src, dst, n):
        return pltpu.make_async_copy(src, dst, self.load_sem.at[n])

    def ready(self, k):
        @pl.when(k >= self.q_first)
        def _():
            for c in range(self.per_chunk):
                number = (k - self.q_first) * self.per_chunk + c
                spot = self.q_own(number)
                pltpu.make_async_copy(spot, spot, self.own_sem.at[number]).wait()

    def stage_one(self, k):
        self.ready(k)
        mine = self.sum_slot.at[lax.rem(k, 8)]

        @pl.when(self.place == 0)
        def _():
            @pl.when(k >= self.ahead)
            def _():
                self.send_inner(k - self.ahead, self.own.at[k - self.ahead]).wait_send()

            self.send_inner(k, self.own.at[k]).start()

        @pl.when(self.place > 0)
        def _():
            self.load(self.own.at[k], mine, 0).start()
            self.send_inner(k, mine).wait_recv()
            self.load(self.first.at[k], self.in_slot, 1).start()
            self.load(self.own.at[k], mine, 0).wait()
            self.load(self.first.at[k], self.in_slot, 1).wait()
            add_chunk(mine, mine, self.in_slot)

            @pl.when(self.place < self.middle)
            def _():
                self.send_inner(k, mine).start()

            @pl.when((self.place == self.middle) & jnp.logical_not(self.ours(k)))
            def _():
                self.send_across(k, mine).start()

    def stage_sum(self, k):
        @pl.when((self.place == self.middle) & self.ours(k))
        def _():
            mine = self.sum_slot.at[lax.rem(k, 8)]
            self.send_across(k, mine).wait_recv()
            arrived = self.load(self.cross.at[k], self.in_slot, 2)
            arrived.start()
            arrived.wait()
            add_chunk(self.total_slot.at[lax.rem(k, 8)], mine, self.in_slot)
            shift, local, remote = self.send_owner(k)

            @pl.when(shift == 0)
            def _():
                local.start()

            @pl.when(shift > 0)
            def _():
                remote.start()

    def stage_sent(self, k):
        @pl.when((self.place > 0) & ((self.place < self.middle) | jnp.logical_not(self.ours(k))))
        def _():
            self.send_inner(k, self.own.at[k]).wait_send()

    def stage_handed(self, k):
        shift, _, remote = self.send_owner(k)

        @pl.when((self.place == self.middle) & self.ours(k) & (shift > 0))
        def _():
            remote.wait_send()

    def stage_two(self, k):
        self.spread_outer(k).wait_recv()

        @pl.when((self.place == self.middle) & self.ours(k))
        def _():
            self.spread_across(k).start()

        @pl.when(self.place > 0)
        def _():
            self.spread_outer(k).start()

        self.deliver(k).start()

    def stage_three(self, k):
        @pl.when((self.place == self.middle) & self.ours(k))
        def _():
            self.spread_across(k).wait_send()

        @pl.when(self.place > 0)
        def _():
            self.spread_outer(k).wait_send()

        @pl.when((self.place == 0) & (k >= self.chunks - self.ahead))
        def _():
            self.send_inner(k, self.own.at[k]).wait_send()

        self.deliver(k).wait_send()

    def q_place(self, number):
        spot = lax.rem(number, self.per_chunk)
        column = lax.rem(spot, self.across) * self.piece
        if not isinstance(column, int):
            column = pl.multiple_of(column, 128)
        return number // self.per_chunk, pl.ds((spot // self.across) * self.half, self.half), pl.ds(column, self.piece)

    def q_own(self, number):
        chunk, where, columns = self.q_place(number)
        return self.own.at[self.q_first + chunk, where, columns]

    def deliver(self, k):
        return pltpu.make_async_remote_copy(
            self.second.at[k], self.second.at[k], self.core_send.at[k], self.core_recv.at[k],
            device_id=(self.dp, self.z, self.other), device_id_type=MESH)

    def advance(self, count):
        start = self.position
        self.position += count

        @pl.loop(start, start + count)
        def _(t):
            self.slot(t)

    def slot(self, t):
        @pl.when(t < self.chunks)
        def _():
            self.stage_one(t)

        at_middle = self.place == self.middle

        def upto(most, least):
            begin = self.n_ffn - 2

            def last(n):
                caught = jnp.minimum(n - least, 2 * n - begin - most)
                return jnp.clip(jnp.where(n < begin, n - most, caught), -1, self.chunks - 1)

            return pl.loop(last(t - 1) + 1, last(t) + 1)

        def fixed(k, act):
            @pl.when((k >= 0) & (k < self.chunks))
            def _():
                act(k)

        fixed(t - 9, self.stage_handed)

        @upto(2, 1)
        def _(k):
            self.stage_sum(k)

        fixed(t - 7, self.stage_sent)

        @upto(4, 2)
        def _(k):
            @pl.when(at_middle & self.ours(k))
            def _():
                self.stage_two(k)

        steps = self.middle - self.place

        @upto(7 + 4 * steps, 3 + 2 * steps)
        def _(k):
            @pl.when(jnp.logical_not(at_middle & self.ours(k)))
            def _():
                self.stage_two(k)

        fixed(t - self.lag - 3, self.stage_three)

    def advance_at(self, first, count):
        for j in range(count):
            self.slot(first + j)

    def finish(self):
        self.advance(self.chunks + self.most - self.position)

        @pl.loop(0, self.chunks)
        def _(k):
            self.deliver(k).wait_recv()


def add_chunk(into, left, right):
    rows = into.shape[0]

    @pl.loop(0, rows // 64)
    def _(i):
        part = pl.ds(i * 64, 64)
        into[part] = (left[part].astype(F32) + right[part].astype(F32)).astype(BF16)


class BackIn(NamedTuple):
    normed_two: Any
    cot_all: Any
    w_first: Any
    w_gate: Any
    w_up: Any
    w_down: Any
    hidden_in: Any
    w_out: Any
    w_qkv: Any
    normed_one: Any
    qk_pre: Any
    query: Any
    keys_values: Any
    log_total: Any
    mixed: Any
    bias: Any
    tables: Any
    gains: Any
    own_x: Any


class BackOut(NamedTuple):
    output: Any
    input_grad: Any
    gain_sum: Any
    totals: Any
    own: Any
    first: Any
    cross: Any
    w_land: Any
    dn2_pair: Any
    out_pair: Any
    out_land: Any
    out_keep: Any


class BackScratch(NamedTuple):
    sum_slot: Any
    total_slot: Any
    in_slot: Any
    kv_sum: Any
    grad_query: Any
    grad_qkv: Any
    dn2_land: Any
    land_slot: Any
    hidden_v: Any
    grad_hidden: Any
    own_x_v: Any
    cot_own: Any
    gains_v: Any
    gain_acc: Any
    dx_all: Any
    kv_pair: Any
    kv_land: Any
    gain_core: Any
    gain_dp: Any
    gain_z: Any
    dn1_land: Any
    result: Any
    pair_slot: Any
    pair_o: Any
    pair_q: Any
    load_sem: Any
    own_sem: Any
    first_send: Any
    first_recv: Any
    second_send: Any
    cross_recv: Any
    owner_send: Any
    across_send: Any
    second_recv: Any
    core_send: Any
    core_recv: Any
    w_send: Any
    w_recv: Any
    stage_sem: Any
    in_sem: Any
    sum_send: Any
    pair_recv: Any
    land_recv: Any
    dx_send: Any
    dx_recv: Any
    kv_send: Any
    kv_recv: Any
    pair_send: Any
    pair_land: Any
    dn1_send: Any
    dn1_recv: Any
    q_send: Any
    gain_send: Any
    gain_recv: Any


def norm_rows(values):
    inverse = lax.rsqrt(jnp.mean(values * values, axis=-1, keepdims=True) + NORM_EPSILON)
    return values * inverse, inverse


def back_kernel(dims, *refs):
    r = SimpleNamespace()
    for kind, first in ((BackIn, 0), (BackOut, len(BackIn._fields)), (BackScratch, len(BackIn._fields + BackOut._fields))):
        vars(r).update(kind(*refs[first : first + len(kind._fields)])._asdict())
    dp_n, lines, tokens, width = dims.dp_n, dims.lines, dims.tokens, dims.width
    rows, f8, n_blocks, per_block, down_block = dims.rows, dims.f8, dims.n_blocks, dims.per_block, dims.down_block
    head, group, kv_heads = dims.head, dims.group, dims.kv_heads
    q_cols, kv_cols, cols = dims.q_cols, dims.kv_cols, dims.qkv_cols
    plane = 2 * dp_n * tokens
    seq_tokens = dp_n * tokens
    length = lines * 2 * tokens
    scale = head ** (-0.5)
    line = Line(r, dims)
    dp, z, core, other = line.dp, line.z, line.core, line.other
    own = r.own
    half, quarter = rows // 2, rows // 4
    partner = (dp, z, other)
    n_ffn = line.n_ffn
    pairs = range(1, dp_n)

    def peer(shift):
        return lax.rem(dp + shift, dp_n)

    def local(src, dst, sem, n=0):
        return pltpu.make_async_copy(src, dst, sem.at[n])

    def remote(src, dst, send, n, recv, m, device):
        return pltpu.make_async_remote_copy(
            src, dst, send.at[n], recv.at[m], device_id=device, device_id_type=MESH)

    def span(index, size):
        return pl.ds(pl.multiple_of(index * size, size), size)

    def start(copies):
        for copy in copies:
            copy.start()

    def wait(copies):
        for copy in copies:
            copy.wait()

    barrier = pltpu.get_barrier_semaphore()
    for shift in pairs:
        pl.semaphore_signal(barrier, device_id=(peer(shift), z, core), device_id_type=MESH)
    for shift in range(1, 2 * lines):
        spot = lax.rem(2 * z + core + shift, 2 * lines)
        pl.semaphore_signal(barrier, device_id=(dp, spot // 2, lax.rem(spot, 2)), device_id_type=MESH)

    w_land = r.w_land

    def weight_copies(b):
        mine, sent = [], []
        for c, weight in enumerate((r.w_gate, r.w_up)):
            for shift in range(dp_n):
                to = peer(shift)
                src = weight.at[:, pl.ds(pl.multiple_of((2 * to + core) * f8 + b * 256, 256), 256)]
                dst = w_land.at[b, span(dp, rows), pl.ds(c * 256, 256)]
                slot = (b * dp_n + dp) * 2 + c
                if shift == 0:
                    mine.append(local(src, dst, r.w_recv, slot))
                else:
                    sent.append(remote(src, dst, r.w_send, (b * dp_n + shift) * 2 + c, r.w_recv, slot, (to, z, core)))
        return mine, sent

    def feed_forward(act, grads, wd, w_gu, stage):
        def blocks(n2, dy):
            loads = [
                local(r.normed_two, n2, r.in_sem, 0), local(r.cot_all, dy, r.in_sem, 1),
                local(r.w_down.at[span(core, f8)], wd, r.in_sem, 2),
            ]
            start(loads)

            first_weights = local(r.w_first, w_gu.at[0], r.in_sem, 3)
            first_weights.start()

            @pl.loop(1, n_blocks)
            def _(b):
                start(weight_copies(b)[0])

            pl.semaphore_wait(barrier, dp_n - 1 + 2 * lines - 1)

            start(weight_copies(1)[1])
            wait(loads)
            first_weights.wait()

            @pl.loop(0, n_blocks)
            def _(b):
                @pl.when(b > 0)
                def _():
                    @pl.loop(0, dp_n)
                    def _(src):
                        for c in range(2):
                            dst = w_land.at[b, pl.ds(0, rows), pl.ds(c * 256, 256)]
                            local(dst, dst, r.w_recv, (b * dp_n + src) * 2 + c).wait()

                    weights = local(w_land.at[b], w_gu.at[b], r.in_sem, 3)
                    weights.start()

                    @pl.when(b + 1 < n_blocks)
                    def _():
                        start(weight_copies(b + 1)[1])

                    weights.wait()

                @pl.loop(0, plane // 256)
                def _(i):
                    where = span(i, 256)
                    both = dot(n2[where], w_gu[b])
                    gate, up = both[:, :256], both[:, 256:]
                    grad_act = contract_cols(dy[where], wd[span(b, 256)])
                    sig = jax.nn.sigmoid(gate)
                    silu = gate * sig
                    act[b, where] = (silu * up).astype(BF16)
                    grads[b, where, 0:256] = (grad_act * up * sig * (1.0 + gate * (1.0 - sig))).astype(BF16)
                    grads[b, where, 256:512] = (grad_act * silu).astype(BF16)

                def to_own(j):
                    return local(stage.at[j], own.at[b * per_block + j], r.stage_sem, j)

                @pl.loop(0, 4)
                def _(c):
                    grad = contract_rows(act[b], dy[:, span(c, 512)]).astype(BF16)
                    for j in range(down_block):
                        stage[j, span(c, quarter), :] = grad[j * quarter : (j + 1) * quarter]

                for j in range(down_block):
                    to_own(j).start()
                for j in range(down_block):
                    to_own(j).wait()
                line.advance_at(b * 2, 1)

                @pl.loop(0, dp_n)
                def _(shift):
                    stage[down_block + shift] = contract_rows(n2[:, span(peer(shift), rows)], grads[b]).astype(BF16)
                    to_own(down_block + shift).start()

                @pl.loop(down_block, per_block)
                def _(j):
                    to_own(j).wait()


                line.advance_at(b * 2 + 1, 1)

        pl.run_scoped(blocks, pltpu.VMEM((plane, width), BF16), pltpu.VMEM((plane, width), BF16))
        line.position = n_blocks * 2

        def sums(part):
            def own_sum(turn):
                to = peer(turn)
                return remote(part.at[to, span(core, tokens)], r.dn2_land.at[dp], r.sum_send, 2 * dp_n + turn, r.land_recv, dp, (to, z, core))

            def plane_sum(hidden, product, every):
                def to_pair(i):
                    base = 0 if hidden else dp_n
                    pair = r.dn2_pair if hidden else r.out_pair
                    return remote(part.at[i, span(other, tokens)], pair.at[i], r.sum_send, base + i, r.pair_recv, base + i, partner), pair

                @pl.loop(0, dp_n + 1)
                def _(turn):
                    @pl.when(turn < dp_n)
                    def _():
                        i = peer(turn + 1)

                        @pl.loop(0, width // 512)
                        def _(n):
                            part[i, :, span(n, 512)] = product(span(i, 2 * tokens), span(n, 512)).astype(BF16)

                        to_pair(i)[0].start()

                    @pl.when(turn > 0)
                    def _():
                        i = peer(turn)
                        copy, pair = to_pair(i)
                        copy.wait_recv()
                        copy = local(pair.at[i], r.land_slot, r.in_sem, 3)
                        copy.start()
                        copy.wait()
                        mine = part.at[i, span(core, tokens)]
                        add_rows(mine, mine, r.land_slot)
                        if hidden:
                            @pl.when(turn < dp_n)
                            def _():
                                own_sum(turn).start()
                        else:
                            local(mine, r.out_keep.at[i], r.in_sem, 7 + turn).start()

                        @pl.when(lax.rem(turn, every) == 0)
                        def _():
                            line.advance_at(line.position + turn // every - 1, 1)

                line.position += dp_n // every

            def hidden_grad(where, columns):
                total = contract_cols(grads[0, where], w_gu[0, columns])
                for b in range(1, n_blocks):
                    total += contract_cols(grads[b, where], w_gu[b, columns])
                return total

            def ffn_out(where, columns):
                total = dot(act[0, where], wd[pl.ds(0, 256), columns])
                for b in range(1, n_blocks):
                    total += dot(act[b, where], wd[pl.ds(b * 256, 256), columns])
                return total

            def pair_sent(base):
                for i in range(dp_n):
                    remote(part.at[i, span(other, tokens)], r.dn2_pair.at[i], r.sum_send, base + i, r.pair_recv, base + i, partner).wait_send()

            plane_sum(True, hidden_grad, max(1, dp_n // 4))
            mine = local(part.at[dp, span(core, tokens)], r.dn2_land.at[dp], r.in_sem, 4)
            mine.start()
            mine.wait()
            pair_sent(0)
            for shift in pairs:
                own_sum(shift).wait_send()
            plane_sum(False, ffn_out, max(1, dp_n // 2))
            for turn in range(1, dp_n + 1):
                local(part.at[0, span(core, tokens)], r.out_keep.at[0], r.in_sem, 7 + turn).wait()
            pair_sent(dp_n)

        pl.run_scoped(sums, pltpu.VMEM((dp_n, 2 * tokens, width), BF16))

    pl.run_scoped(
        feed_forward,
        pltpu.VMEM((n_blocks, plane, 256), BF16), pltpu.VMEM((n_blocks, plane, 512), BF16), pltpu.VMEM((f8, width), BF16),
        pltpu.VMEM((n_blocks, width, 512), BF16), pltpu.VMEM((per_block, rows, 512), BF16),
    )

    def landed(land, base):
        for shift in pairs:
            src = peer(shift)
            local(land.at[src], land.at[src], r.land_recv, base + src).wait()

    hidden_in, grad_hidden, gains = r.hidden_v, r.grad_hidden, r.gains_v
    own_loads = [
        local(r.cot_all.at[span(2 * dp + core, tokens)], r.cot_own, r.in_sem, 4), local(r.hidden_in, hidden_in, r.in_sem, 5), local(r.gains, gains, r.in_sem, 6), local(r.own_x, r.own_x_v, r.in_sem, 7),
    ]
    start(own_loads)
    wait(own_loads)
    landed(r.dn2_land, 0)
    gain_acc = r.gain_acc
    gain_acc[...] = jnp.zeros_like(gain_acc)

    @pl.loop(0, tokens // 32)
    def _(i):
        where = span(i, 32)
        grad = r.dn2_land[0, where].astype(F32)
        for src in range(1, dp_n):
            grad += r.dn2_land[src, where].astype(F32)
        hat, inverse = norm_rows(hidden_in[where])
        gain_acc[1:2] += jnp.sum(grad * hat, axis=0, keepdims=True)
        back = grad * gains[1:2]
        dy_own = r.cot_own
        total = dy_own[where].astype(F32) + inverse * (back - hat * jnp.mean(back * hat, axis=-1, keepdims=True))
        grad_hidden[where] = total
        r.dx_all[dp, where] = total.astype(BF16)

    dx_sends = []
    for shift in pairs:
        to = peer(shift)
        dx_sends.append(remote(r.dx_all.at[dp], r.dx_all.at[dp], r.dx_send, shift, r.dx_recv, dp, (to, z, core)))
    start(dx_sends)
    line.advance(2)

    kv_sum, grad_query, grad_qkv = r.kv_sum, r.grad_query, r.grad_qkv
    step = max(1, min(group, MIB // (4 * length * tokens)))

    def kv_copies(s):
        found = []
        for shift in range(1, lines):
            to = lax.rem(z + shift, lines)
            found.append(remote(kv_sum.at[s, to], r.kv_land.at[z, s], r.kv_send, dp_n + s * lines + shift,
                                r.kv_recv, dp_n + s * lines + z, (dp, to, core)))
        return found

    every = max(1, dp_n // 4)

    def sequences(w_out, query, keys_values, bias, grad_mixed, grad_kv):
        loads = [
            local(src, dst, r.in_sem, 8 + n)
            for n, (src, dst) in enumerate(((r.w_out, w_out), (r.query, query), (r.keys_values, keys_values), (r.bias, bias)))
        ]
        start(loads)
        wait(loads)

        def pair_copy(s):
            return remote(grad_kv.at[s, :, other], r.kv_pair.at[s], r.kv_send, s, r.kv_recv, s, partner)

        def one_sequence(turn):
            s = peer(turn)

            @pl.when(turn > 0)
            def _():
                local(r.dx_all.at[s], r.dx_all.at[s], r.dx_recv, s).wait()

            grad_mixed[...] = contract_cols(r.dx_all[s], w_out[...]).astype(BF16)
            both = keys_values[:, s].reshape(length, 2 * kv_cols)
            grads = [None] * (2 * kv_heads)
            mask = jnp.concatenate([bias[...]] * step, axis=1)
            for g in range(kv_heads):
                keys = both[:, g * head : (g + 1) * head]
                values = both[:, (kv_heads + g) * head : (kv_heads + g + 1) * head]
                key_grad = value_grad = None
                for first in range(g * group, (g + 1) * group, step):
                    names = [slice(h * head, (h + 1) * head) for h in range(first, first + step)]
                    queries = jnp.concatenate([query[s, :, n] for n in names], axis=0)
                    grad_out = jnp.concatenate([grad_mixed[:, n] for n in names], axis=0)
                    scores = contract_cols(keys, queries) * scale + mask
                    offset = (first - g * group) * tokens
                    probs = jnp.exp(scores - r.log_total[s, pl.ds(g, 1), offset : offset + step * tokens])
                    grad_probs = contract_cols(values, grad_out)
                    inner = jnp.sum(probs * grad_probs, axis=0, keepdims=True)
                    grad_scores = (probs * (grad_probs - inner)).astype(BF16)
                    key_part = dot(grad_scores, queries)
                    value_part = dot(probs.astype(BF16), grad_out)
                    key_grad = key_part if key_grad is None else key_grad + key_part
                    value_grad = value_part if value_grad is None else value_grad + value_part
                    back = (contract_rows(keys, grad_scores) * scale).T.astype(BF16)
                    grad_query[s, :, first * head : (first + step) * head] = jnp.concatenate(
                        [back[h * tokens : (h + 1) * tokens] for h in range(step)], axis=1)
                grads[g] = key_grad * scale
                grads[kv_heads + g] = value_grad
            grad_kv[s] = jnp.concatenate(grads, axis=1).astype(BF16).reshape(lines, 2, tokens, 2 * kv_cols)
            pair_copy(s).start()

        def pass_on(turn):
            s = peer(turn)
            pair_copy(s).wait_recv()

            @pl.loop(0, lines)
            def _(n):
                kv_sum[s, n] = (grad_kv[s, n, core].astype(F32) + r.kv_pair[s, n].astype(F32)).astype(BF16)

            start(kv_copies(s))

        @pl.loop(0, dp_n)
        def _(turn):
            one_sequence(turn)

            @pl.when(turn > 0)
            def _():
                pass_on(turn - 1)

            @pl.when(lax.rem(turn, every) == 0)
            def _():
                line.advance_at(line.position + turn // every, 1)

        pass_on(dp_n - 1)

        @pl.loop(0, dp_n)
        def _(s):
            pair_copy(s).wait_send()

    seqs = lambda *shape: pltpu.VMEM((dp_n,) + shape, BF16)
    pl.run_scoped(
        sequences,
        pltpu.VMEM((rows, width), BF16), seqs(tokens, q_cols), pltpu.VMEM((2 * lines, dp_n, tokens, 2 * kv_cols), BF16),
        pltpu.VMEM((length, tokens), F32), pltpu.VMEM((tokens, q_cols), BF16), seqs(lines, 2, tokens, 2 * kv_cols),
    )
    line.position += dp_n // every
    assert line.position <= n_ffn

    def projections(w_qkv, normed_one, qk_pre, mixed, tables, out_part, qkv_part, dn1_part):
        loads = [
            local(src, dst, r.in_sem, 8 + n)
            for n, (src, dst) in enumerate((
                (r.qk_pre, qk_pre), (r.tables, tables), (r.mixed, mixed), (r.normed_one, normed_one), (r.w_qkv, w_qkv)))
        ]
        start(loads)
        wait(loads)

        @pl.loop(0, width // 512)
        def _(n):
            total = jnp.zeros((rows, 512), F32)
            for s in range(dp_n):
                total += contract_rows(mixed[s], r.dx_all[s, :, span(n, 512)])
            out_part[:, span(n, 512)] = total.astype(BF16)

            @pl.when(n == 1)
            def _():
                line.advance_at(line.position, 1)

        line.position += 1

        pair_o = remote(out_part.at[span(other, half)], r.pair_o, r.pair_send, 0, r.pair_land, 0, partner)
        pair_o.start()

        q_gain, k_gain = gains[2:3, 0:head], gains[3:4, 0:head]
        zero = jnp.zeros((1, head), F32)

        def rotate(turn, carry):
            s = peer(turn)
            for shift in range(1, lines):
                src = lax.rem(z + shift, lines)
                land = r.kv_land.at[src, s]
                local(land, land, r.kv_recv, dp_n + s * lines + src).wait()
            kv = kv_sum[s, z].astype(F32)
            for shift in range(1, lines):
                kv += r.kv_land[lax.rem(z + shift, lines), s].astype(F32)
            kv = kv.astype(BF16)
            cosine, sine = tables[s, :, 0:head], tables[s, :, head : 2 * head]
            sums = list(carry)
            outs = []
            for h in range(kv_heads * (group + 1)):
                is_key = h >= kv_heads * group
                if is_key:
                    g = h - kv_heads * group
                    grad = kv[:, g * head : (g + 1) * head].astype(F32)
                else:
                    grad = grad_query[s, :, h * head : (h + 1) * head].astype(F32)
                turned = jnp.concatenate([grad[:, head // 2 :], grad[:, : head // 2]], axis=1)
                grad = grad * cosine - turned * sine
                hat, inverse = norm_rows(qk_pre[s, :, h * head : (h + 1) * head])
                sums[is_key] = sums[is_key] + jnp.sum(grad * hat, axis=0, keepdims=True)
                back = grad * (k_gain if is_key else q_gain)
                outs.append((inverse * (back - hat * jnp.mean(back * hat, axis=-1, keepdims=True))).astype(BF16))
            grad_qkv[s] = jnp.concatenate(outs + [kv[:, kv_cols:]], axis=1)

            @pl.when(lax.rem(turn, max(1, dp_n // 2)) == 0)
            def _():
                line.advance_at(line.position + turn // max(1, dp_n // 2), 1)

            return tuple(sums)

        q_sum, k_sum = lax.fori_loop(0, dp_n, rotate, (zero, zero))
        line.position += 2
        assert line.position <= n_ffn
        slot = r.pair_slot
        pair_o.wait_recv()
        for j in range(2):
            for c in range(4):
                mine = out_part[pl.ds(pl.multiple_of(core * half + j * quarter, quarter), quarter), pl.ds(c * 512, 512)]
                arrived = r.pair_o[pl.ds(j * quarter, quarter), pl.ds(c * 512, 512)]
                slot[j, pl.ds(c * quarter, quarter), :] = (mine.astype(F32) + arrived.astype(F32)).astype(BF16)
        copies = [local(slot.at[j], own.at[n_ffn + j], r.stage_sem, j) for j in range(2)]
        start(copies)
        wait(copies)
        gain_acc[2:3, 0:head] = q_sum
        gain_acc[3:4, 0:head] = k_sum
        line.advance(1)

        @pl.loop(0, dp_n)
        def _(i):
            total = jnp.zeros((rows, cols), F32)
            for s in range(dp_n):
                total += contract_rows(normed_one[s, :, span(i, rows)], grad_qkv[s])
            qkv_part[i] = total.astype(BF16)

        pair_q = [
            remote(qkv_part.at[i, span(other, half)], r.pair_q.at[i], r.pair_send, 1 + i, r.pair_land, 1 + i, partner)
            for i in range(dp_n)
        ]
        start(pair_q)
        line.advance(1)

        @pl.loop(0, width // 512)
        def _(n):
            weights = w_qkv[span(n, 512)]
            for s in range(dp_n):
                dn1_part[s, :, span(n, 512)] = contract_cols(grad_qkv[s], weights).astype(BF16)

        dn1_sends = []
        for shift in pairs:
            to = peer(shift)
            dn1_sends.append(remote(dn1_part.at[to], r.dn1_land.at[dp], r.dn1_send, shift, r.dn1_recv, dp, (to, z, core)))
        r.dn1_land[dp] = dn1_part[dp]
        line.advance(1)

        piece = line.piece
        q_sends = []
        q_mine = []
        for i in range(dp_n):
            pair_q[i].wait_recv()
            mine = qkv_part.at[i, span(core, half)]
            mine[...] = (mine[...].astype(F32) + r.pair_q[i].astype(F32)).astype(BF16)
        for shift in range(dp_n):
            to = peer(shift)
            for j in range(3):
                number = dp * 3 + j
                src = qkv_part.at[to, span(core, half), pl.ds(j * piece, piece)]
                if shift == 0:
                    q_mine.append(local(src, line.q_own(number), r.own_sem, number))
                else:
                    q_sends.append(remote(src, line.q_own(number), r.q_send, shift * 3 + j, r.own_sem, number, (to, z, core)))
        start(q_sends + q_mine)
        assert line.position <= line.q_first
        start(dn1_sends)
        line.advance(1)
        out_sends = [
            remote(r.out_keep.at[peer(shift)], r.out_land.at[dp], r.sum_send, 3 * dp_n + shift, r.land_recv, dp_n + dp, (peer(shift), z, core))
            for shift in pairs
        ]
        out_mine = local(r.out_keep.at[dp], r.out_land.at[dp], r.in_sem, 4)
        start(out_sends + [out_mine])
        line.advance(1)

        for shift in pairs:
            src = peer(shift)
            local(r.dn1_land.at[src], r.dn1_land.at[src], r.dn1_recv, src).wait()

        @pl.loop(0, tokens // 32)
        def _(i):
            where = span(i, 32)
            grad = r.dn1_land[0, where].astype(F32)
            for src in range(1, dp_n):
                grad += r.dn1_land[src, where].astype(F32)
            hat, inverse = norm_rows(r.own_x_v[where].astype(F32))
            gain_acc[0:1] += jnp.sum(grad * hat, axis=0, keepdims=True)
            back = grad * gains[0:1]
            total = grad_hidden[where] + inverse * (back - hat * jnp.mean(back * hat, axis=-1, keepdims=True))
            r.result[where] = total.astype(BF16)

        written = local(r.result, r.input_grad, r.in_sem, 0)
        written.start()
        written.wait()

        def gain_total(land, count, me):
            land[me] = gain_acc[...]
            total = land[0]
            for n in range(1, count):
                total = total + land[n]
            return total

        sends = [remote(gain_acc, r.gain_core.at[core], r.gain_send, 0, r.gain_recv, 0, partner)]
        start(sends)
        line.advance(1)
        wait(sends)
        gain_acc[...] = gain_total(r.gain_core, 2, core)
        sends = [
            remote(gain_acc, r.gain_dp.at[dp], r.gain_send, shift, r.gain_recv, shift, (peer(shift), z, core)) for shift in pairs
        ]
        start(sends)
        line.advance(1)
        wait(sends)
        gain_acc[...] = gain_total(r.gain_dp, dp_n, dp)
        sends = [
            remote(gain_acc, r.gain_z.at[z], r.gain_send, dp_n + shift, r.gain_recv, dp_n + shift,
                   (dp, lax.rem(z + shift, lines), core))
            for shift in range(1, lines)
        ]
        start(sends)
        line.advance(1)
        wait(sends)
        gain_acc[...] = gain_total(r.gain_z, lines, z)
        written = local(gain_acc, r.gain_sum, r.in_sem, 1)
        written.start()
        written.wait()

        landed(r.out_land, dp_n)
        wait([out_mine])

        @pl.loop(0, dp_n)
        def _(src):
            copy = local(r.out_land.at[src], r.land_slot, r.in_sem, 3)
            copy.start()
            copy.wait()

            @pl.loop(0, tokens // 32)
            def _(i):
                where = span(i, 32)
                hidden_in[where] += r.land_slot[where].astype(F32)

        r.result[...] = hidden_in[...].astype(BF16)
        done = local(r.result, r.output, r.in_sem, 0)
        done.start()
        done.wait()
        line.finish()

        for copy in out_sends + q_sends + dn1_sends + pair_q + [pair_o]:
            copy.wait_send()

        @pl.loop(0, dp_n)
        def _(s):
            for copy in kv_copies(s):
                copy.wait_send()

    pl.run_scoped(
        projections,
        pltpu.VMEM((width, cols), BF16), seqs(tokens, width), pltpu.VMEM((dp_n, tokens, q_cols + kv_cols), F32), seqs(tokens, q_cols),
        pltpu.VMEM((dp_n, tokens, 2 * head), F32), pltpu.VMEM((rows, width), BF16), seqs(rows, cols), seqs(tokens, width),
    )

    for copy in dx_sends:
        copy.wait_send()

    @pl.loop(1, n_blocks)
    def _(b):
        for copy in weight_copies(b)[1]:
            copy.wait_send()


def add_rows(into, left, right):
    @pl.loop(0, into.shape[0] // 32)
    def _(i):
        where = pl.ds(pl.multiple_of(i * 32, 32), 32)
        into[where] = (left[where].astype(F32) + right[where].astype(F32)).astype(BF16)


def backward(arrays, dp_n, lines, head, collective_id):
    x = arrays
    tokens, width = x.own_x.shape
    rows = width // dp_n
    f8 = x.w_down.shape[0] // 2
    n_blocks = f8 // 256
    down_block = 1024 // rows
    q_cols = x.query.shape[2]
    cols = x.w_qkv.shape[1]
    kv_cols = (cols - q_cols) // 2
    kv_heads = kv_cols // head
    per_block = down_block + dp_n
    chunks = n_blocks * per_block + 2 + dp_n * cols // 1024
    plane = 2 * dp_n * tokens
    dims = SimpleNamespace(
        dp_n=dp_n, lines=lines, tokens=tokens, width=width, rows=rows, f8=f8, n_blocks=n_blocks, per_block=per_block,
        down_block=down_block, head=head, group=q_cols // kv_cols, kv_heads=kv_heads, q_cols=q_cols, kv_cols=kv_cols,
        qkv_cols=cols, chunks=chunks,
    )
    bf16 = lambda *shape: jax.ShapeDtypeStruct(shape, BF16)
    outs = BackOut(
        output=bf16(tokens, width), input_grad=bf16(tokens, width), gain_sum=jax.ShapeDtypeStruct((8, width), F32),
        totals=bf16(2, chunks, rows, 512), own=bf16(chunks, rows, 512), first=bf16(chunks, rows, 512),
        cross=bf16(chunks, rows, 512), w_land=bf16(n_blocks, width, 512), dn2_pair=bf16(dp_n, tokens, width), out_pair=bf16(dp_n, tokens, width), out_land=bf16(dp_n, tokens, width), out_keep=bf16(dp_n, tokens, width),
    )
    vmem = lambda *shape: pltpu.VMEM(shape, BF16)
    dma = lambda n: pltpu.SemaphoreType.DMA((n,))
    scratch = BackScratch(
        sum_slot=vmem(8, rows, 512), total_slot=vmem(8, rows, 512), in_slot=vmem(rows, 512),
        kv_sum=vmem(dp_n, lines, tokens, 2 * kv_cols), grad_query=vmem(dp_n, tokens, q_cols), grad_qkv=vmem(dp_n, tokens, cols),
        dn2_land=vmem(dp_n, tokens, width),
        land_slot=vmem(tokens, width), hidden_v=pltpu.VMEM((tokens, width), F32), grad_hidden=pltpu.VMEM((tokens, width), F32),
        own_x_v=vmem(tokens, width), cot_own=vmem(tokens, width), gains_v=pltpu.VMEM((8, width), F32), gain_acc=pltpu.VMEM((8, width), F32),
        dx_all=vmem(dp_n, tokens, width), kv_pair=vmem(dp_n, lines, tokens, 2 * kv_cols), kv_land=vmem(lines, dp_n, tokens, 2 * kv_cols),
        gain_core=pltpu.VMEM((2, 8, width), F32), gain_dp=pltpu.VMEM((dp_n, 8, width), F32), gain_z=pltpu.VMEM((lines, 8, width), F32),
        dn1_land=vmem(dp_n, tokens, width), result=vmem(tokens, width), pair_slot=vmem(2, rows, 512), pair_o=vmem(rows // 2, width), pair_q=vmem(dp_n, rows // 2, cols),
        load_sem=dma(3), own_sem=dma(3 * dp_n), first_send=dma(chunks), first_recv=dma(chunks),
        second_send=dma(chunks), cross_recv=dma(chunks), owner_send=dma(chunks), across_send=dma(chunks), second_recv=dma(chunks), core_send=dma(chunks), core_recv=dma(chunks),
        w_send=dma(2 * n_blocks * dp_n), w_recv=dma(2 * n_blocks * dp_n), stage_sem=dma(per_block),
        in_sem=dma(8 + max(8, dp_n)), sum_send=dma(4 * dp_n), pair_recv=dma(2 * dp_n), land_recv=dma(2 * dp_n), dx_send=dma(dp_n), dx_recv=dma(dp_n),
        kv_send=dma(dp_n + dp_n * lines), kv_recv=dma(dp_n + dp_n * lines), pair_send=dma(1 + dp_n), pair_land=dma(1 + dp_n),
        dn1_send=dma(dp_n), dn1_recv=dma(dp_n), q_send=dma(3 * dp_n), gain_send=dma(dp_n + lines), gain_recv=dma(dp_n + lines),
    )
    hbm = pl.BlockSpec(memory_space=pl.ANY)
    in_vmem = pl.BlockSpec(memory_space=pltpu.VMEM)
    flops = 6 * plane * width * f8 * 3
    results = pl.pallas_call(
        partial(back_kernel, dims),
        out_shape=tuple(outs),
        in_specs=list(BackIn(*[hbm] * len(x))._replace(log_total=in_vmem)),
        out_specs=(hbm,) * len(outs),
        scratch_shapes=list(scratch),
        compiler_params=pltpu.CompilerParams(collective_id=collective_id, has_side_effects=True, vmem_limit_bytes=63 * MIB),
        cost_estimate=pl.CostEstimate(flops=flops, bytes_accessed=100 * MIB, transcendentals=0),
        name="backward",
    )(*x)
    return BackOut(*results)


def widen_pair_kernel(n_blocks, place, *refs):
    gate, up = refs[n_blocks:]
    for b in range(n_blocks):
        columns = slice(b * 256, (b + 1) * 256)
        gate[:, columns] = refs[b][0, 0, :, 0:256].astype(F32)
        up[:, columns] = refs[b][0, 0, :, 256:512].astype(F32)


def widen_rows(out, chunks):
    quarter = chunks[0].shape[2] // 4
    for j, chunk in enumerate(chunks):
        for c in range(4):
            out[j * quarter : (j + 1) * quarter, c * 512 : (c + 1) * 512] = chunk[0, 0, c * quarter : (c + 1) * quarter, :].astype(F32)


def widen_rows_kernel(place, *refs):
    widen_rows(refs[-1], refs[:-1])


def widen_heads_kernel(dp_n, q_cols, kv_cols, place, *refs):
    out, query, key, value = refs[-4:]
    widen_rows(out, refs[:2])
    chunks = refs[2:-4]
    half = query.shape[0]
    piece = (q_cols + 2 * kv_cols) // 3
    across = 512 // piece
    for src in range(dp_n):
        for j in range(3):
            chunk, spot = divmod(3 * src + j, 2 * across)
            row, column = spot // across * half, spot % across * piece
            part = chunks[chunk][0, 0, row : row + half, column : column + piece].astype(F32)
            if j < 2:
                query[:, src * q_cols + j * piece : src * q_cols + (j + 1) * piece] = part
            else:
                key[:, src * kv_cols : (src + 1) * kv_cols] = part[:, :kv_cols]
                value[:, src * kv_cols : (src + 1) * kv_cols] = part[:, kv_cols:]


def widen(totals, place, dp_n, width, f8, q_cols, kv_cols):
    _, chunks, rows, _ = totals.shape
    half = rows // 2
    down_block = 1024 // rows
    per_block = down_block + dp_n
    n_blocks = f8 // 256
    n_ffn = n_blocks * per_block
    f32 = lambda *shape: jax.ShapeDtypeStruct(shape, F32)

    def call(kernel, grid, in_maps, out_specs, out_shape, name):
        return pl.pallas_call(
            kernel,
            grid_spec=pltpu.PrefetchScalarGridSpec(
                num_scalar_prefetch=1, grid=grid, in_specs=[pl.BlockSpec((1, 1, rows, 512), m) for m in in_maps], out_specs=out_specs),
            out_shape=out_shape, compiler_params=pltpu.CompilerParams(vmem_limit_bytes=48 * MIB), name=name,
        )(place, *[totals] * len(in_maps))

    def gate_map(b):
        return lambda src, who, place: (who, b * per_block + down_block + lax.rem(place[0] - src + dp_n, dp_n), 0, 0)

    gate, up = call(
        partial(widen_pair_kernel, n_blocks), (dp_n, 2), [gate_map(b) for b in range(n_blocks)],
        (pl.BlockSpec((rows, f8), lambda src, who, place: (0, 2 * src + who)),) * 2, (f32(rows, 2 * dp_n * f8),) * 2, "widen_gate_up")

    def down_map(j):
        return lambda who, b, place: (who, b * per_block + j, 0, 0)

    down = call(
        widen_rows_kernel, (2, n_blocks), [down_map(j) for j in range(down_block)],
        pl.BlockSpec((256, width), lambda who, b, place: (who * n_blocks + b, 0)), f32(2 * f8, width), "widen_down")

    def tail_map(k):
        return lambda who, place: (who, k, 0, 0)

    half_rows = lambda columns: pl.BlockSpec((half, columns), lambda who, place: (who, 0))
    widths = (width, dp_n * q_cols, dp_n * kv_cols, dp_n * kv_cols)
    out, query, key, value = call(
        partial(widen_heads_kernel, dp_n, q_cols, kv_cols), (2,), [tail_map(k) for k in range(n_ffn, chunks)],
        tuple(half_rows(columns) for columns in widths), tuple(f32(rows, columns) for columns in widths), "widen_heads")
    return query, key, value, out, gate, up, down


class FrontIn(NamedTuple):
    own_x: Any
    own_cot: Any
    w_query: Any
    w_key: Any
    w_value: Any
    gain_piece: Any
    own_tables: Any
    bias: Any
    w_out: Any
    w_gate: Any
    w_up: Any


class FrontOut(NamedTuple):
    normed_two: Any
    cot_all: Any
    w_first: Any
    hidden_in: Any
    w_qkv: Any
    normed_one: Any
    qk_pre: Any
    query: Any
    keys_values: Any
    log_total: Any
    mixed: Any
    tables: Any
    gains: Any


class FrontScratch(NamedTuple):
    x_all: Any
    n1: Any
    w_all: Any
    qk: Any
    value: Any
    q_rot: Any
    kv: Any
    log_v: Any
    mix: Any
    tables_v: Any
    gains_v: Any
    bias_v: Any
    w_out_v: Any
    part: Any
    land: Any
    hidden: Any
    n2: Any
    in_sem: Any
    out_sem: Any
    x_send: Any
    x_recv: Any
    w_send: Any
    w_recv: Any
    w_pass: Any
    w_passed: Any
    kv_send: Any
    kv_recv: Any
    kv_pass: Any
    kv_passed: Any
    part_send: Any
    part_recv: Any
    plane_send: Any
    plane_recv: Any
    plane_pass: Any
    plane_passed: Any
    first_send: Any
    first_recv: Any


def front_kernel(dims, *refs):
    r = SimpleNamespace()
    for kind, first in ((FrontIn, 0), (FrontOut, len(FrontIn._fields)), (FrontScratch, len(FrontIn._fields + FrontOut._fields))):
        vars(r).update(kind(*refs[first : first + len(kind._fields)])._asdict())
    dp_n, lines, tokens, width, rows, f8 = dims.dp_n, dims.lines, dims.tokens, dims.width, dims.rows, dims.f8
    head, group, kv_heads, q_cols, kv_cols = dims.head, dims.group, dims.kv_heads, dims.q_cols, dims.kv_cols
    length = 2 * lines * tokens
    half = rows // 2
    scale = head ** (-0.5)
    dp, z, core = places()
    other = 1 - core
    partner = (dp, z, other)
    pairs = range(1, dp_n)
    me = 2 * z + core

    def peer(shift):
        return lax.rem(dp + shift, dp_n)

    def local(src, dst, sem, n=0):
        return pltpu.make_async_copy(src, dst, sem.at[n])

    def remote(src, dst, send, n, recv, m, device):
        return pltpu.make_async_remote_copy(
            src, dst, send.at[n], recv.at[m], device_id=device, device_id_type=MESH)

    def span(index, size):
        return pl.ds(pl.multiple_of(index * size, size), size)

    def start(copies):
        for copy in copies:
            copy.start()

    def wait(copies):
        for copy in copies:
            copy.wait()

    def landed(ref, sem, n):
        local(ref, ref, sem, n).wait()

    barrier = pltpu.get_barrier_semaphore()
    for shift in pairs:
        pl.semaphore_signal(barrier, device_id=(peer(shift), z, core), device_id_type=MESH)
    pl.semaphore_signal(barrier, device_id=partner, device_id_type=MESH)
    for shift in range(1, lines):
        pl.semaphore_signal(barrier, device_id=(dp, lax.rem(z + shift, lines), core), device_id_type=MESH)

    mine = [
        local(r.own_x, r.x_all.at[dp], r.in_sem, 0), local(r.own_tables, r.tables_v.at[dp], r.in_sem, 1),
        local(r.gain_piece, r.gains_v.at[:, span(dp, rows)], r.in_sem, 2), local(r.bias, r.bias_v, r.in_sem, 3),
        local(r.w_out, r.w_out_v, r.in_sem, 4),
    ]
    ends = (0, q_cols, q_cols + kv_cols, q_cols + 2 * kv_cols) if kv_cols % 128 == 0 else (0, q_cols, q_cols + 2 * kv_cols)
    n_pieces = len(ends) - 1

    def weight_from(to, where):
        if n_pieces == 3:
            return [r.w_query.at[where, span(to, q_cols)], r.w_key.at[where, span(to, kv_cols)], r.w_value.at[where, span(to, kv_cols)]]
        return [r.w_query.at[where, span(to, q_cols)], r.w_key.at[to, where]]

    def weight_to(where):
        return [r.w_all.at[where, pl.ds(a, b - a)] for a, b in zip(ends, ends[1:])]

    whole = pl.ds(0, rows)
    mine += [local(src, dst, r.in_sem, 5 + n) for n, (src, dst) in enumerate(zip(weight_from(dp, whole), weight_to(span(dp, rows))))]
    start(mine)
    pl.semaphore_wait(barrier, dp_n + lines - 1)

    small = []
    for shift in pairs:
        to = peer(shift)
        device = (to, z, core)
        small += [
            remote(r.own_x, r.x_all.at[dp], r.x_send, 3 * shift, r.x_recv, 3 * dp, device),
            remote(r.own_tables, r.tables_v.at[dp], r.x_send, 3 * shift + 1, r.x_recv, 3 * dp + 1, device),
            remote(r.gain_piece, r.gains_v.at[:, span(dp, rows)], r.x_send, 3 * shift + 2, r.x_recv, 3 * dp + 2, device),
        ]
    start(small)

    def weight_spot(src, side):
        return weight_to(pl.ds(pl.multiple_of(src * rows + side * half, half), half))

    weights = []
    for shift in pairs:
        to = peer(shift)
        for n, (src, dst) in enumerate(zip(weight_from(to, span(core, half)), weight_spot(dp, core))):
            weights.append(remote(src, dst, r.w_send, 3 * shift + n, r.w_recv, 3 * dp + n, (to, z, core)))
    start(weights)

    wait(mine[1:3])
    for shift in pairs:
        landed(r.gains_v.at[:, span(peer(shift), rows)], r.x_recv, 3 * peer(shift) + 2)
    mine[0].wait()

    @pl.loop(0, dp_n)
    def _(turn):
        s = peer(turn)

        @pl.when(turn > 0)
        def _():
            landed(r.x_all.at[s], r.x_recv, 3 * s)

        @pl.loop(0, tokens // 32)
        def _(i):
            hat, _ = norm_rows(r.x_all[s, span(i, 32)].astype(F32))
            r.n1[pl.ds(pl.multiple_of(s * tokens + i * 32, 32), 32)] = (hat * r.gains_v[0:1]).astype(BF16)

    passes = []
    for shift in pairs:
        src = peer(shift)
        for n, spot in enumerate(weight_spot(src, core)):
            landed(spot, r.w_recv, 3 * src + n)
            copy = remote(spot, spot, r.w_pass, 3 * shift + n, r.w_passed, 3 * src + n, partner)
            copy.start()
            passes.append(copy)
    wait(mine[3:])
    for shift in pairs:
        src = peer(shift)
        for n, spot in enumerate(weight_spot(src, other)):
            landed(spot, r.w_passed, 3 * src + n)
        landed(r.tables_v.at[src], r.x_recv, 3 * src + 1)

    slot_of = lambda d, c: pl.ds(pl.multiple_of((2 * d + c) * tokens, tokens), tokens)

    def plane_copies(src, target, base):
        spot = target.at[slot_of(dp, core)]
        found = [remote(src, spot, r.plane_send, base + shift, r.plane_recv, base + dp, (peer(shift), z, core)) for shift in pairs]
        return found + [remote(src, spot, r.plane_send, base, r.plane_recv, base + dp_n, partner)]

    def plane_pass(target, base):
        found = []
        for shift in pairs:
            src = peer(shift)
            spot = target.at[slot_of(src, core)]
            landed(spot, r.plane_recv, base + src)
            copy = remote(spot, spot, r.plane_pass, base + shift, r.plane_passed, base + src, partner)
            copy.start()
            found.append(copy)
        return found

    def plane_done(target, base):
        landed(target.at[slot_of(dp, other)], r.plane_recv, base + dp_n)
        for shift in pairs:
            src = peer(shift)
            landed(target.at[slot_of(src, other)], r.plane_passed, base + src)

    cots = plane_copies(r.own_cot, r.cot_all, 0)
    firsts, first_mine = [], []
    for n, weight in enumerate((r.w_gate, r.w_up)):
        for shift in range(dp_n):
            to = peer(shift)
            src = weight.at[:, pl.ds(pl.multiple_of((2 * to + core) * f8, 256), 256)]
            dst = r.w_first.at[span(dp, rows), pl.ds(256 * n, 256)]
            if shift == 0:
                first_mine.append(local(src, dst, r.out_sem, n))
            else:
                firsts.append(remote(src, dst, r.first_send, 2 * shift + n, r.first_recv, 2 * dp + n, (to, z, core)))
    cot_mine = local(r.own_cot, r.cot_all.at[slot_of(dp, core)], r.out_sem, 2)
    start(cots + firsts + first_mine + [cot_mine])

    split = q_cols + kv_cols
    r.qk[:, 0:q_cols] = dot(r.n1[...], r.w_all[:, 0:q_cols])
    pair = dot(r.n1[...], r.w_all[:, q_cols : q_cols + 2 * kv_cols])
    r.qk[:, q_cols:split] = pair[:, :kv_cols]
    r.value[...] = pair[:, kv_cols:].astype(BF16)
    outs = [
        local(r.n1, r.normed_one, r.out_sem, 3), local(r.w_all, r.w_qkv, r.out_sem, 4), local(r.qk, r.qk_pre, r.out_sem, 5),
        local(r.tables_v, r.tables, r.out_sem, 6), local(r.gains_v, r.gains, r.out_sem, 7),
    ]
    start(outs)

    def kv_copies(s):
        spot = r.kv.at[me, s]
        found = [
            remote(spot, spot, r.kv_send, s * lines + shift, r.kv_recv, s * (lines + 1) + z, (dp, lax.rem(z + shift, lines), core))
            for shift in range(1, lines)
        ]
        return found + [remote(spot, spot, r.kv_send, s * lines, r.kv_recv, s * (lines + 1) + lines, partner)]

    def kv_pass(s):
        found = []
        for shift in range(1, lines):
            src = lax.rem(z + shift, lines)
            spot = r.kv.at[2 * src + core, s]
            found.append((spot, s * (lines + 1) + src,
                          remote(spot, spot, r.kv_pass, s * lines + shift, r.kv_passed, s * lines + src, partner)))
        return found

    @pl.loop(0, dp_n)
    def _(turn):
        s = peer(turn + 1)
        cosine, sine = r.tables_v[s, :, 0:head], r.tables_v[s, :, head : 2 * head]
        turned = []
        where = span(s, tokens)
        for h in range(kv_heads * (group + 1)):
            gain = r.gains_v[2:3, 0:head] if h < kv_heads * group else r.gains_v[3:4, 0:head]
            hat, _ = norm_rows(r.qk[where, h * head : (h + 1) * head])
            hat = hat * gain
            swapped = jnp.concatenate([hat[:, head // 2 :], hat[:, : head // 2]], axis=1)
            turned.append((hat * cosine + swapped * sine).astype(BF16))
        r.q_rot[s] = jnp.concatenate(turned[: kv_heads * group], axis=1)
        r.kv[me, s] = jnp.concatenate(turned[kv_heads * group :] + [r.value[where]], axis=1)
        start(kv_copies(s))

    step = max(1, min(group, MIB // (2 * length * tokens)))

    def part_copy(s, shift):
        return remote(r.part.at[s], r.land.at[dp], r.part_send, shift, r.part_recv, dp, (s, z, core))

    @pl.loop(0, dp_n)
    def _(turn):
        s = peer(turn + 1)
        for spot, n, copy in kv_pass(s):
            landed(spot, r.kv_recv, n)
            copy.start()
        landed(r.kv.at[2 * z + other, s], r.kv_recv, s * (lines + 1) + lines)
        for shift in range(1, lines):
            src = lax.rem(z + shift, lines)
            landed(r.kv.at[2 * src + other, s], r.kv_passed, s * lines + src)
        both = r.kv[:, s].reshape(length, 2 * kv_cols)
        mask = jnp.concatenate([r.bias_v[...]] * step, axis=1)
        for g in range(kv_heads):
            keys = both[:, g * head : (g + 1) * head]
            values = both[:, (kv_heads + g) * head : (kv_heads + g + 1) * head]
            for first in range(g * group, (g + 1) * group, step):
                queries = jnp.concatenate([r.q_rot[s, :, h * head : (h + 1) * head] for h in range(first, first + step)], axis=0)
                scores = contract_cols(keys, queries) * scale + mask
                top = jnp.max(scores, axis=0, keepdims=True)
                weight = jnp.exp(scores - top)
                total = jnp.sum(weight, axis=0, keepdims=True)
                probs = (weight * (1.0 / total)).astype(BF16)
                offset = (first - g * group) * tokens
                r.log_v[s, pl.ds(g, 1), offset : offset + step * tokens] = top + jnp.log(total)
                out = contract_rows(values, probs).T.astype(BF16)
                r.mix[s, :, first * head : (first + step) * head] = jnp.concatenate(
                    [out[h * tokens : (h + 1) * tokens] for h in range(step)], axis=1)
        r.part[s] = dot(r.mix[s], r.w_out_v[...]).astype(BF16)

        @pl.when(turn < dp_n - 1)
        def _():
            part_copy(s, turn + 1).start()

    outs += [
        local(r.q_rot, r.query, r.out_sem, 8), local(r.kv, r.keys_values, r.out_sem, 9),
        local(r.log_v, r.log_total, r.out_sem, 10), local(r.mix, r.mixed, r.out_sem, 11),
    ]
    start(outs[5:])

    for shift in pairs:
        landed(r.land.at[peer(shift)], r.part_recv, peer(shift))
    r.land[dp] = r.part[dp]

    @pl.loop(0, tokens // 32)
    def _(i):
        where = span(i, 32)
        total = r.land[0, where].astype(F32)
        for src in range(1, dp_n):
            total += r.land[src, where].astype(F32)
        total += r.x_all[dp, where].astype(F32)
        r.hidden[where] = total
        hat, _ = norm_rows(total)
        r.n2[where] = (hat * r.gains_v[1:2]).astype(BF16)

    n2_base = dp_n + 1
    n2_copies = plane_copies(r.n2, r.normed_two, n2_base)
    start(n2_copies)
    n2_mine = local(r.n2, r.normed_two.at[slot_of(dp, core)], r.out_sem, 12)
    outs += [local(r.hidden, r.hidden_in, r.out_sem, 13), n2_mine]
    start(outs[9:])
    passed = plane_pass(r.cot_all, 0)
    passed += plane_pass(r.normed_two, n2_base)
    plane_done(r.cot_all, 0)
    for shift in pairs:
        src = peer(shift)
        for n in range(2):
            landed(r.w_first.at[span(src, rows), pl.ds(256 * n, 256)], r.first_recv, 2 * src + n)
    plane_done(r.normed_two, n2_base)
    wait(outs + first_mine + [cot_mine])
    for copy in small + weights + passes + cots + firsts + n2_copies + passed:
        copy.wait_send()

    @pl.loop(0, dp_n)
    def _(s):
        for copy in kv_copies(s):
            copy.wait_send()
        for _, _, copy in kv_pass(s):
            copy.wait_send()

    @pl.loop(0, dp_n - 1)
    def _(turn):
        part_copy(peer(turn + 1), turn + 1).wait_send()


def forward(x, dp_n, lines, head, collective_id):
    tokens, width = x.own_x.shape
    rows = width // dp_n
    q_cols = x.w_query.shape[1] // dp_n
    kv_cols = x.w_value.shape[1] // dp_n
    kv_heads = kv_cols // head
    f8 = x.w_gate.shape[1] // (2 * dp_n)
    cols = q_cols + 2 * kv_cols
    length = 2 * lines * tokens
    dims = SimpleNamespace(
        dp_n=dp_n, lines=lines, tokens=tokens, width=width, rows=rows, f8=f8, head=head, group=q_cols // kv_cols,
        kv_heads=kv_heads, q_cols=q_cols, kv_cols=kv_cols,
    )
    bf16 = lambda *shape: jax.ShapeDtypeStruct(shape, BF16)
    f32 = lambda *shape: jax.ShapeDtypeStruct(shape, F32)
    all_tokens = dp_n * tokens
    group_rows = q_cols // kv_cols * tokens
    outs = FrontOut(
        normed_two=bf16(2 * all_tokens, width), cot_all=bf16(2 * all_tokens, width), w_first=bf16(width, 512),
        hidden_in=f32(tokens, width), w_qkv=bf16(width, cols), normed_one=bf16(all_tokens, width), qk_pre=f32(all_tokens, q_cols + kv_cols),
        query=bf16(dp_n, tokens, q_cols), keys_values=bf16(2 * lines, dp_n, tokens, 2 * kv_cols), log_total=f32(dp_n, kv_heads, group_rows),
        mixed=bf16(dp_n, tokens, q_cols), tables=f32(dp_n, tokens, 2 * head), gains=f32(8, width),
    )
    vmem = lambda *shape: pltpu.VMEM(shape, BF16)
    wide = lambda *shape: pltpu.VMEM(shape, F32)
    dma = lambda n: pltpu.SemaphoreType.DMA((n,))
    scratch = FrontScratch(
        x_all=vmem(dp_n, tokens, width), n1=vmem(all_tokens, width), w_all=vmem(width, cols), qk=wide(all_tokens, q_cols + kv_cols),
        value=vmem(all_tokens, kv_cols), q_rot=vmem(dp_n, tokens, q_cols), kv=vmem(2 * lines, dp_n, tokens, 2 * kv_cols),
        log_v=wide(dp_n, kv_heads, group_rows), mix=vmem(dp_n, tokens, q_cols), tables_v=wide(dp_n, tokens, 2 * head), gains_v=wide(8, width),
        bias_v=wide(length, tokens), w_out_v=vmem(rows, width), part=vmem(dp_n, tokens, width), land=vmem(dp_n, tokens, width),
        hidden=wide(tokens, width), n2=vmem(tokens, width), in_sem=dma(8), out_sem=dma(14), x_send=dma(3 * dp_n), x_recv=dma(3 * dp_n),
        w_send=dma(3 * dp_n), w_recv=dma(3 * dp_n), w_pass=dma(3 * dp_n), w_passed=dma(3 * dp_n), kv_send=dma(dp_n * lines),
        kv_recv=dma(dp_n * (lines + 1)), kv_pass=dma(dp_n * lines), kv_passed=dma(dp_n * lines), part_send=dma(dp_n), part_recv=dma(dp_n),
        plane_send=dma(2 * dp_n + 2), plane_recv=dma(2 * dp_n + 2), plane_pass=dma(2 * dp_n + 2), plane_passed=dma(2 * dp_n + 2),
        first_send=dma(2 * dp_n), first_recv=dma(2 * dp_n),
    )
    hbm = pl.BlockSpec(memory_space=pl.ANY)
    results = pl.pallas_call(
        partial(front_kernel, dims),
        out_shape=tuple(outs),
        in_specs=[hbm] * len(x),
        out_specs=(hbm,) * len(outs),
        scratch_shapes=list(scratch),
        compiler_params=pltpu.CompilerParams(collective_id=collective_id, has_side_effects=True, vmem_limit_bytes=63 * MIB),
        cost_estimate=pl.CostEstimate(flops=10**10, bytes_accessed=50 * MIB, transcendentals=0),
        name="forward",
    )(*x)
    return FrontOut(*results)


def local(
    inputs, attn_gain, w_query, w_key, w_value, q_gain, key_norm_gain, w_out, ffn_gain,
    w_gate, w_up, w_down, stretch_map, pos_ids, cotangent,
):
    dp, lines, cores = lax.axis_size("dp"), lax.axis_size("z"), lax.axis_size("core")
    core = lax.axis_index("core")
    rows, width = inputs.shape[1], inputs.shape[2]
    head = q_gain.shape[0]
    query_width, key_width, hidden = w_query.shape[1], w_key.shape[1], w_gate.shape[1]
    half = rows // 2
    stretches = stretch_map.shape[0]
    length = stretches * half
    ctx = lax.axis_index("z") * cores + core

    within = jnp.arange(half, dtype=jnp.int32)
    key_places = (stretch_map[:, None] * half + within[None, :]).reshape(length)
    query_places = lax.dynamic_slice_in_dim(key_places, ctx * rows, rows, 0)
    bias = jnp.where(key_places[:, None] <= query_places[None, :], 0.0, MASKED_SCORE).astype(F32)
    frequency = jnp.power(F32(ROPE_BASE), -2.0 * jnp.arange(head // 2, dtype=F32) / head)
    angles = pos_ids[0].astype(F32)[:, None] * frequency[None, :]
    cosine, sine = jnp.cos(angles), jnp.sin(angles)
    tables = jnp.concatenate([cosine, cosine, -sine, sine], axis=1)
    piece = width // dp
    gain_piece = jnp.zeros((8, piece), F32).at[0].set(attn_gain.astype(F32)).at[1].set(ffn_gain.astype(F32))
    gain_piece = gain_piece.at[2, :head].set(q_gain.astype(F32)).at[3, :head].set(key_norm_gain.astype(F32))
    kv_cols, q_cols = key_width // dp, query_width // dp
    if kv_cols % 128 == 0:
        pair = (w_key, w_value)
    else:
        cut = [jnp.concatenate([w[:, n * kv_cols : (n + 1) * kv_cols] for w in (w_key, w_value)], axis=1) for n in range(dp)]
        pair = (jnp.stack(cut), w_value)
    front = forward(
        FrontIn(
            own_x=inputs[0], own_cot=cotangent[0], w_query=w_query, w_key=pair[0], w_value=pair[1], gain_piece=gain_piece, own_tables=tables,
            bias=bias, w_out=w_out, w_gate=w_gate, w_up=w_up,
        ),
        dp, lines, head, 2,
    )
    f8 = hidden // (2 * dp)
    made = backward(
        BackIn(
            normed_two=front.normed_two, cot_all=front.cot_all, w_first=front.w_first, w_gate=w_gate, w_up=w_up, w_down=w_down,
            hidden_in=front.hidden_in, w_out=w_out, w_qkv=front.w_qkv, normed_one=front.normed_one.reshape(dp, rows, width),
            qk_pre=front.qk_pre.reshape(dp, rows, q_cols + kv_cols), query=front.query, keys_values=front.keys_values,
            log_total=front.log_total, mixed=front.mixed, bias=bias, tables=front.tables, gains=front.gains, own_x=inputs[0],
        ),
        dp, lines, head, 1,
    )
    place = lax.axis_index("dp").reshape(1)
    query_grad, key_grad, value_grad, out_grad, gate_grad, up_grad, down_grad = widen(
        made.totals, place, dp, width, f8, q_cols, kv_cols
    )
    gains = made.gain_sum
    return (
        made.output[None], made.input_grad[None], lax.dynamic_slice_in_dim(gains[0], place[0] * piece, piece, 0), query_grad, key_grad,
        value_grad, gains[2, :head], gains[3, :head], out_grad, lax.dynamic_slice_in_dim(gains[1], place[0] * piece, piece, 0),
        gate_grad, up_grad, down_grad,
    )


def solution(mesh):
    dp, ctx = mesh.shape["dp"], mesh.shape["ctx"]
    fine = Mesh(mesh.devices.reshape(dp, ctx // 2, 2), ("dp", "z", "core"))
    tokens = P("dp", ("z", "core"), None)
    rows = P("dp", None)
    in_specs = (
        tokens, P("dp"), rows, rows, rows, P(), P(), rows, P("dp"), rows, rows, rows, P(), P("dp", ("z", "core")), tokens,
    )
    out_specs = (tokens, tokens, P("dp"), rows, rows, rows, P(), P(), rows, P("dp"), rows, rows, rows)
    return jax.shard_map(local, mesh=fine, in_specs=in_specs, out_specs=out_specs, check_vma=False)
```

```python
from functools import partial
from types import SimpleNamespace
from typing import Any, NamedTuple

import jax
import jax.numpy as jnp
from jax import lax
from jax.experimental import pallas as pl
from jax.experimental.pallas import tpu as pltpu
from jax.sharding import Mesh, PartitionSpec as P

NORM_EPSILON = 1e-05
ROPE_BASE = 1000000.0
MASKED_SCORE = -1e30
BF16 = jnp.bfloat16
F32 = jnp.float32
MESH = pl.DeviceIdType.MESH
MIB = 2**20


def dot(left, right):
    return jnp.dot(left, right, preferred_element_type=F32)


def contract_rows(left, right):
    return lax.dot_general(left, right, (((0,), (0,)), ((), ())), preferred_element_type=F32)


def contract_cols(left, right):
    return lax.dot_general(left, right, (((1,), (1,)), ((), ())), preferred_element_type=F32)


def places():
    dp, z, core = lax.axis_index("dp"), lax.axis_index("z"), lax.axis_index("core")
    return dp, z, core


def line_of(z, lines):
    left = z < lines // 2
    step = jnp.where(left, 1, -1)
    place = jnp.where(left, z, lines - 1 - z)
    inner = z + step
    outer = jnp.clip(z - step, 0, lines - 1)
    return place, inner, outer


class Line:
    def __init__(self, refs, dims):
        vars(self).update(vars(refs))
        vars(self).update(vars(dims))
        self.dp, self.z, self.core = places()
        self.place, self.inner, self.outer = line_of(self.z, self.lines)
        self.middle = self.lines // 2 - 1
        self.side = self.z // (self.lines // 2)
        self.other = 1 - self.core
        self.second = self.totals.at[self.core]
        self.quarter = self.rows // 4
        self.half = self.rows // 2
        self.ahead = 4
        self.lag = 7 + 6 * (self.middle - self.place)
        self.most = 7 + 6 * self.middle + 3
        self.n_ffn = self.n_blocks * self.per_block
        self.q_first = self.n_ffn + 2
        self.piece = self.qkv_cols // 3
        self.across = 512 // self.piece
        self.per_chunk = 2 * self.across
        self.position = 0

    def ours(self, k):
        return lax.rem(k // self.per_block + lax.rem(k, self.per_block), 2) == self.side

    def shift_of(self, k):
        part = lax.rem(k, self.per_block) - self.down_block
        return jnp.where(k < self.n_ffn, jnp.maximum(part, 0), 0)

    def send_inner(self, k, src):
        return pltpu.make_async_remote_copy(
            src, self.first.at[k], self.first_send.at[k], self.first_recv.at[k],
            device_id=(self.dp, self.inner, self.core), device_id_type=MESH)

    def send_across(self, k, src):
        return pltpu.make_async_remote_copy(
            src, self.cross.at[k], self.first_send.at[k], self.cross_recv.at[k],
            device_id=(self.dp, self.inner, self.core), device_id_type=MESH)

    def send_owner(self, k):
        total = self.total_slot.at[lax.rem(k, 8)]
        shift = self.shift_of(k)
        local = pltpu.make_async_copy(total, self.second.at[k], self.second_recv.at[k])
        remote = pltpu.make_async_remote_copy(
            total, self.second.at[k], self.owner_send.at[k], self.second_recv.at[k],
            device_id=(lax.rem(self.dp + shift, self.dp_n), self.z, self.core), device_id_type=MESH)
        return shift, local, remote

    def spread_across(self, k):
        return pltpu.make_async_remote_copy(
            self.second.at[k], self.second.at[k], self.across_send.at[k], self.second_recv.at[k],
            device_id=(self.dp, self.inner, self.core), device_id_type=MESH)

    def spread_outer(self, k):
        return pltpu.make_async_remote_copy(
            self.second.at[k], self.second.at[k], self.second_send.at[k], self.second_recv.at[k],
            device_id=(self.dp, self.outer, self.core), device_id_type=MESH)

    def load(self, src, dst, n):
        return pltpu.make_async_copy(src, dst, self.load_sem.at[n])

    def ready(self, k):
        @pl.when(k >= self.q_first)
        def _():
            for c in range(self.per_chunk):
                number = (k - self.q_first) * self.per_chunk + c
                spot = self.q_own(number)
                pltpu.make_async_copy(spot, spot, self.own_sem.at[number]).wait()

    def stage_one(self, k):
        self.ready(k)
        mine = self.sum_slot.at[lax.rem(k, 8)]

        @pl.when(self.place == 0)
        def _():
            @pl.when(k >= self.ahead)
            def _():
                self.send_inner(k - self.ahead, self.own.at[k - self.ahead]).wait_send()

            self.send_inner(k, self.own.at[k]).start()

        @pl.when(self.place > 0)
        def _():
            self.load(self.own.at[k], mine, 0).start()
            self.send_inner(k, mine).wait_recv()
            self.load(self.first.at[k], self.in_slot, 1).start()
            self.load(self.own.at[k], mine, 0).wait()
            self.load(self.first.at[k], self.in_slot, 1).wait()
            add_chunk(mine, mine, self.in_slot)

            @pl.when(self.place < self.middle)
            def _():
                self.send_inner(k, mine).start()

            @pl.when((self.place == self.middle) & jnp.logical_not(self.ours(k)))
            def _():
                self.send_across(k, mine).start()

    def stage_sum(self, k):
        @pl.when((self.place == self.middle) & self.ours(k))
        def _():
            mine = self.sum_slot.at[lax.rem(k, 8)]
            self.send_across(k, mine).wait_recv()
            arrived = self.load(self.cross.at[k], self.in_slot, 2)
            arrived.start()
            arrived.wait()
            add_chunk(self.total_slot.at[lax.rem(k, 8)], mine, self.in_slot)
            shift, local, remote = self.send_owner(k)

            @pl.when(shift == 0)
            def _():
                local.start()

            @pl.when(shift > 0)
            def _():
                remote.start()

    def stage_sent(self, k):
        @pl.when((self.place > 0) & ((self.place < self.middle) | jnp.logical_not(self.ours(k))))
        def _():
            self.send_inner(k, self.own.at[k]).wait_send()

    def stage_handed(self, k):
        shift, _, remote = self.send_owner(k)

        @pl.when((self.place == self.middle) & self.ours(k) & (shift > 0))
        def _():
            remote.wait_send()

    def stage_two(self, k):
        self.spread_outer(k).wait_recv()

        @pl.when((self.place == self.middle) & self.ours(k))
        def _():
            self.spread_across(k).start()

        @pl.when(self.place > 0)
        def _():
            self.spread_outer(k).start()

        self.deliver(k).start()

    def stage_three(self, k):
        @pl.when((self.place == self.middle) & self.ours(k))
        def _():
            self.spread_across(k).wait_send()

        @pl.when(self.place > 0)
        def _():
            self.spread_outer(k).wait_send()

        @pl.when((self.place == 0) & (k >= self.chunks - self.ahead))
        def _():
            self.send_inner(k, self.own.at[k]).wait_send()

        self.deliver(k).wait_send()

    def q_place(self, number):
        spot = lax.rem(number, self.per_chunk)
        column = lax.rem(spot, self.across) * self.piece
        if not isinstance(column, int):
            column = pl.multiple_of(column, 128)
        return number // self.per_chunk, pl.ds((spot // self.across) * self.half, self.half), pl.ds(column, self.piece)

    def q_own(self, number):
        chunk, where, columns = self.q_place(number)
        return self.own.at[self.q_first + chunk, where, columns]

    def deliver(self, k):
        return pltpu.make_async_remote_copy(
            self.second.at[k], self.second.at[k], self.core_send.at[k], self.core_recv.at[k],
            device_id=(self.dp, self.z, self.other), device_id_type=MESH)

    def advance(self, count):
        start = self.position
        self.position += count

        @pl.loop(start, start + count)
        def _(t):
            self.slot(t)

    def slot(self, t):
        @pl.when(t < self.chunks)
        def _():
            self.stage_one(t)

        at_middle = self.place == self.middle

        def upto(most, least):
            begin = self.n_ffn - 2

            def last(n):
                caught = jnp.minimum(n - least, 2 * n - begin - most)
                return jnp.clip(jnp.where(n < begin, n - most, caught), -1, self.chunks - 1)

            return pl.loop(last(t - 1) + 1, last(t) + 1)

        def fixed(k, act):
            @pl.when((k >= 0) & (k < self.chunks))
            def _():
                act(k)

        fixed(t - 9, self.stage_handed)

        @upto(2, 1)
        def _(k):
            self.stage_sum(k)

        fixed(t - 7, self.stage_sent)

        @upto(4, 2)
        def _(k):
            @pl.when(at_middle & self.ours(k))
            def _():
                self.stage_two(k)

        steps = self.middle - self.place

        @upto(7 + 6 * steps, 3 + 2 * steps)
        def _(k):
            @pl.when(jnp.logical_not(at_middle & self.ours(k)))
            def _():
                self.stage_two(k)

        fixed(t - self.lag - 3, self.stage_three)

    def advance_at(self, first, count):
        for j in range(count):
            self.slot(first + j)

    def finish(self):
        self.advance(self.chunks + self.most - self.position)

        @pl.loop(0, self.chunks)
        def _(k):
            self.deliver(k).wait_recv()


def add_chunk(into, left, right):
    rows = into.shape[0]

    @pl.loop(0, rows // 64)
    def _(i):
        part = pl.ds(i * 64, 64)
        into[part] = (left[part].astype(F32) + right[part].astype(F32)).astype(BF16)


class BackIn(NamedTuple):
    normed_two: Any
    cot_all: Any
    w_first: Any
    w_gate: Any
    w_up: Any
    w_down: Any
    hidden_in: Any
    w_out: Any
    w_qkv: Any
    normed_one: Any
    qk_pre: Any
    query: Any
    keys_values: Any
    log_total: Any
    mixed: Any
    bias: Any
    tables: Any
    gains: Any
    own_x: Any


class BackOut(NamedTuple):
    output: Any
    input_grad: Any
    gain_sum: Any
    totals: Any
    own: Any
    first: Any
    cross: Any
    w_land: Any
    dn2_pair: Any
    out_pair: Any
    out_land: Any
    out_keep: Any


class BackScratch(NamedTuple):
    sum_slot: Any
    total_slot: Any
    in_slot: Any
    kv_sum: Any
    grad_query: Any
    grad_qkv: Any
    dn2_land: Any
    land_slot: Any
    hidden_v: Any
    grad_hidden: Any
    own_x_v: Any
    cot_own: Any
    gains_v: Any
    gain_acc: Any
    dx_all: Any
    kv_pair: Any
    kv_land: Any
    gain_core: Any
    gain_dp: Any
    gain_z: Any
    dn1_land: Any
    result: Any
    pair_slot: Any
    pair_o: Any
    pair_q: Any
    load_sem: Any
    own_sem: Any
    first_send: Any
    first_recv: Any
    second_send: Any
    cross_recv: Any
    owner_send: Any
    across_send: Any
    second_recv: Any
    core_send: Any
    core_recv: Any
    w_send: Any
    w_recv: Any
    stage_sem: Any
    in_sem: Any
    sum_send: Any
    pair_recv: Any
    land_recv: Any
    dx_send: Any
    dx_recv: Any
    kv_send: Any
    kv_recv: Any
    pair_send: Any
    pair_land: Any
    dn1_send: Any
    dn1_recv: Any
    q_send: Any
    gain_send: Any
    gain_recv: Any


def norm_rows(values):
    inverse = lax.rsqrt(jnp.mean(values * values, axis=-1, keepdims=True) + NORM_EPSILON)
    return values * inverse, inverse


def back_kernel(dims, *refs):
    r = SimpleNamespace()
    for kind, first in ((BackIn, 0), (BackOut, len(BackIn._fields)), (BackScratch, len(BackIn._fields + BackOut._fields))):
        vars(r).update(kind(*refs[first : first + len(kind._fields)])._asdict())
    dp_n, lines, tokens, width = dims.dp_n, dims.lines, dims.tokens, dims.width
    rows, f8, n_blocks, per_block, down_block = dims.rows, dims.f8, dims.n_blocks, dims.per_block, dims.down_block
    head, group, kv_heads = dims.head, dims.group, dims.kv_heads
    q_cols, kv_cols, cols = dims.q_cols, dims.kv_cols, dims.qkv_cols
    plane = 2 * dp_n * tokens
    seq_tokens = dp_n * tokens
    length = lines * 2 * tokens
    scale = head ** (-0.5)
    line = Line(r, dims)
    dp, z, core, other = line.dp, line.z, line.core, line.other
    own = r.own
    half, quarter = rows // 2, rows // 4
    partner = (dp, z, other)
    n_ffn = line.n_ffn
    pairs = range(1, dp_n)

    def peer(shift):
        return lax.rem(dp + shift, dp_n)

    def local(src, dst, sem, n=0):
        return pltpu.make_async_copy(src, dst, sem.at[n])

    def remote(src, dst, send, n, recv, m, device):
        return pltpu.make_async_remote_copy(
            src, dst, send.at[n], recv.at[m], device_id=device, device_id_type=MESH)

    def span(index, size):
        return pl.ds(pl.multiple_of(index * size, size), size)

    def start(copies):
        for copy in copies:
            copy.start()

    def wait(copies):
        for copy in copies:
            copy.wait()

    barrier = pltpu.get_barrier_semaphore()
    for shift in pairs:
        pl.semaphore_signal(barrier, device_id=(peer(shift), z, core), device_id_type=MESH)
    for shift in range(1, 2 * lines):
        spot = lax.rem(2 * z + core + shift, 2 * lines)
        pl.semaphore_signal(barrier, device_id=(dp, spot // 2, lax.rem(spot, 2)), device_id_type=MESH)

    w_land = r.w_land

    def weight_copies(b):
        mine, sent = [], []
        for c, weight in enumerate((r.w_gate, r.w_up)):
            for shift in range(dp_n):
                to = peer(shift)
                src = weight.at[:, pl.ds(pl.multiple_of((2 * to + core) * f8 + b * 256, 256), 256)]
                dst = w_land.at[b, span(dp, rows), pl.ds(c * 256, 256)]
                slot = (b * dp_n + dp) * 2 + c
                if shift == 0:
                    mine.append(local(src, dst, r.w_recv, slot))
                else:
                    sent.append(remote(src, dst, r.w_send, (b * dp_n + shift) * 2 + c, r.w_recv, slot, (to, z, core)))
        return mine, sent

    def feed_forward(act, grads, wd, w_gu, stage):
        def blocks(n2, dy):
            loads = [
                local(r.normed_two, n2, r.in_sem, 0), local(r.cot_all, dy, r.in_sem, 1),
                local(r.w_down.at[span(core, f8)], wd, r.in_sem, 2),
            ]
            start(loads)

            first_weights = local(r.w_first, w_gu.at[0], r.in_sem, 3)
            first_weights.start()

            @pl.loop(1, n_blocks)
            def _(b):
                start(weight_copies(b)[0])

            pl.semaphore_wait(barrier, dp_n - 1 + 2 * lines - 1)

            start(weight_copies(1)[1])
            wait(loads)
            first_weights.wait()

            @pl.loop(0, n_blocks)
            def _(b):
                @pl.when(b > 0)
                def _():
                    @pl.loop(0, dp_n)
                    def _(src):
                        for c in range(2):
                            dst = w_land.at[b, pl.ds(0, rows), pl.ds(c * 256, 256)]
                            local(dst, dst, r.w_recv, (b * dp_n + src) * 2 + c).wait()

                    weights = local(w_land.at[b], w_gu.at[b], r.in_sem, 3)
                    weights.start()

                    @pl.when(b + 1 < n_blocks)
                    def _():
                        start(weight_copies(b + 1)[1])

                    weights.wait()

                @pl.loop(0, plane // 256)
                def _(i):
                    where = span(i, 256)
                    both = dot(n2[where], w_gu[b])
                    gate, up = both[:, :256], both[:, 256:]
                    grad_act = contract_cols(dy[where], wd[span(b, 256)])
                    sig = jax.nn.sigmoid(gate)
                    silu = gate * sig
                    act[b, where] = (silu * up).astype(BF16)
                    grads[b, where, 0:256] = (grad_act * up * sig * (1.0 + gate * (1.0 - sig))).astype(BF16)
                    grads[b, where, 256:512] = (grad_act * silu).astype(BF16)

                def to_own(j):
                    return local(stage.at[j], own.at[b * per_block + j], r.stage_sem, j)

                @pl.loop(0, 4)
                def _(c):
                    grad = contract_rows(act[b], dy[:, span(c, 512)]).astype(BF16)
                    for j in range(down_block):
                        stage[j, span(c, quarter), :] = grad[j * quarter : (j + 1) * quarter]

                for j in range(down_block):
                    to_own(j).start()
                for j in range(down_block):
                    to_own(j).wait()
                line.advance_at(b * 2, 1)

                @pl.loop(0, dp_n)
                def _(shift):
                    stage[down_block + shift] = contract_rows(n2[:, span(peer(shift), rows)], grads[b]).astype(BF16)
                    to_own(down_block + shift).start()

                @pl.loop(down_block, per_block)
                def _(j):
                    to_own(j).wait()


                line.advance_at(b * 2 + 1, 1)

        pl.run_scoped(blocks, pltpu.VMEM((plane, width), BF16), pltpu.VMEM((plane, width), BF16))
        line.position = n_blocks * 2

        def sums(part):
            def own_sum(turn):
                to = peer(turn)
                return remote(part.at[to, span(core, tokens)], r.dn2_land.at[dp], r.sum_send, 2 * dp_n + turn, r.land_recv, dp, (to, z, core))

            def plane_sum(hidden, product, every):
                def to_pair(i):
                    base = 0 if hidden else dp_n
                    pair = r.dn2_pair if hidden else r.out_pair
                    return remote(part.at[i, span(other, tokens)], pair.at[i], r.sum_send, base + i, r.pair_recv, base + i, partner), pair

                @pl.loop(0, dp_n + 1)
                def _(turn):
                    @pl.when(turn < dp_n)
                    def _():
                        i = peer(turn + 1)

                        @pl.loop(0, width // 512)
                        def _(n):
                            part[i, :, span(n, 512)] = product(span(i, 2 * tokens), span(n, 512)).astype(BF16)

                        to_pair(i)[0].start()

                    @pl.when(turn > 0)
                    def _():
                        i = peer(turn)
                        copy, pair = to_pair(i)
                        copy.wait_recv()
                        copy = local(pair.at[i], r.land_slot, r.in_sem, 3)
                        copy.start()
                        copy.wait()
                        mine = part.at[i, span(core, tokens)]
                        add_rows(mine, mine, r.land_slot)
                        if hidden:
                            @pl.when(turn < dp_n)
                            def _():
                                own_sum(turn).start()
                        else:
                            local(mine, r.out_keep.at[i], r.in_sem, 7 + turn).start()

                        @pl.when(lax.rem(turn, every) == 0)
                        def _():
                            line.advance_at(line.position + turn // every - 1, 1)

                line.position += dp_n // every

            def hidden_grad(where, columns):
                total = contract_cols(grads[0, where], w_gu[0, columns])
                for b in range(1, n_blocks):
                    total += contract_cols(grads[b, where], w_gu[b, columns])
                return total

            def ffn_out(where, columns):
                total = dot(act[0, where], wd[pl.ds(0, 256), columns])
                for b in range(1, n_blocks):
                    total += dot(act[b, where], wd[pl.ds(b * 256, 256), columns])
                return total

            def pair_sent(base):
                for i in range(dp_n):
                    remote(part.at[i, span(other, tokens)], r.dn2_pair.at[i], r.sum_send, base + i, r.pair_recv, base + i, partner).wait_send()

            plane_sum(True, hidden_grad, max(1, dp_n // 4))
            mine = local(part.at[dp, span(core, tokens)], r.dn2_land.at[dp], r.in_sem, 4)
            mine.start()
            mine.wait()
            pair_sent(0)
            for shift in pairs:
                own_sum(shift).wait_send()
            plane_sum(False, ffn_out, max(1, dp_n // 2))
            for turn in range(1, dp_n + 1):
                local(part.at[0, span(core, tokens)], r.out_keep.at[0], r.in_sem, 7 + turn).wait()
            pair_sent(dp_n)

        pl.run_scoped(sums, pltpu.VMEM((dp_n, 2 * tokens, width), BF16))

    pl.run_scoped(
        feed_forward,
        pltpu.VMEM((n_blocks, plane, 256), BF16), pltpu.VMEM((n_blocks, plane, 512), BF16), pltpu.VMEM((f8, width), BF16),
        pltpu.VMEM((n_blocks, width, 512), BF16), pltpu.VMEM((per_block, rows, 512), BF16),
    )

    def landed(land, base):
        for shift in pairs:
            src = peer(shift)
            local(land.at[src], land.at[src], r.land_recv, base + src).wait()

    hidden_in, grad_hidden, gains = r.hidden_v, r.grad_hidden, r.gains_v
    own_loads = [
        local(r.cot_all.at[span(2 * dp + core, tokens)], r.cot_own, r.in_sem, 4), local(r.hidden_in, hidden_in, r.in_sem, 5), local(r.gains, gains, r.in_sem, 6), local(r.own_x, r.own_x_v, r.in_sem, 7),
    ]
    start(own_loads)
    wait(own_loads)
    landed(r.dn2_land, 0)
    gain_acc = r.gain_acc
    gain_acc[...] = jnp.zeros_like(gain_acc)

    @pl.loop(0, tokens // 32)
    def _(i):
        where = span(i, 32)
        grad = r.dn2_land[0, where].astype(F32)
        for src in range(1, dp_n):
            grad += r.dn2_land[src, where].astype(F32)
        hat, inverse = norm_rows(hidden_in[where])
        gain_acc[1:2] += jnp.sum(grad * hat, axis=0, keepdims=True)
        back = grad * gains[1:2]
        dy_own = r.cot_own
        total = dy_own[where].astype(F32) + inverse * (back - hat * jnp.mean(back * hat, axis=-1, keepdims=True))
        grad_hidden[where] = total
        r.dx_all[dp, where] = total.astype(BF16)

    dx_sends = []
    for shift in pairs:
        to = peer(shift)
        dx_sends.append(remote(r.dx_all.at[dp], r.dx_all.at[dp], r.dx_send, shift, r.dx_recv, dp, (to, z, core)))
    start(dx_sends)
    line.advance(2)

    kv_sum, grad_query, grad_qkv = r.kv_sum, r.grad_query, r.grad_qkv
    step = max(1, min(group, MIB // (4 * length * tokens)))

    def kv_copies(s):
        found = []
        for shift in range(1, lines):
            to = lax.rem(z + shift, lines)
            found.append(remote(kv_sum.at[s, to], r.kv_land.at[z, s], r.kv_send, dp_n + s * lines + shift,
                                r.kv_recv, dp_n + s * lines + z, (dp, to, core)))
        return found

    every = max(1, dp_n // 4)

    def sequences(w_out, query, keys_values, bias, grad_mixed, grad_kv):
        loads = [
            local(src, dst, r.in_sem, 8 + n)
            for n, (src, dst) in enumerate(((r.w_out, w_out), (r.query, query), (r.keys_values, keys_values), (r.bias, bias)))
        ]
        start(loads)
        wait(loads)

        def pair_copy(s):
            return remote(grad_kv.at[s, :, other], r.kv_pair.at[s], r.kv_send, s, r.kv_recv, s, partner)

        def one_sequence(turn):
            s = peer(turn)

            @pl.when(turn > 0)
            def _():
                local(r.dx_all.at[s], r.dx_all.at[s], r.dx_recv, s).wait()

            grad_mixed[...] = contract_cols(r.dx_all[s], w_out[...]).astype(BF16)
            both = keys_values[:, s].reshape(length, 2 * kv_cols)
            grads = [None] * (2 * kv_heads)
            mask = jnp.concatenate([bias[...]] * step, axis=1)
            for g in range(kv_heads):
                keys = both[:, g * head : (g + 1) * head]
                values = both[:, (kv_heads + g) * head : (kv_heads + g + 1) * head]
                key_grad = value_grad = None
                for first in range(g * group, (g + 1) * group, step):
                    names = [slice(h * head, (h + 1) * head) for h in range(first, first + step)]
                    queries = jnp.concatenate([query[s, :, n] for n in names], axis=0)
                    grad_out = jnp.concatenate([grad_mixed[:, n] for n in names], axis=0)
                    scores = contract_cols(keys, queries) * scale + mask
                    offset = (first - g * group) * tokens
                    probs = jnp.exp(scores - r.log_total[s, pl.ds(g, 1), offset : offset + step * tokens])
                    grad_probs = contract_cols(values, grad_out)
                    inner = jnp.sum(probs * grad_probs, axis=0, keepdims=True)
                    grad_scores = (probs * (grad_probs - inner)).astype(BF16)
                    key_part = dot(grad_scores, queries)
                    value_part = dot(probs.astype(BF16), grad_out)
                    key_grad = key_part if key_grad is None else key_grad + key_part
                    value_grad = value_part if value_grad is None else value_grad + value_part
                    back = (contract_rows(keys, grad_scores) * scale).T.astype(BF16)
                    grad_query[s, :, first * head : (first + step) * head] = jnp.concatenate(
                        [back[h * tokens : (h + 1) * tokens] for h in range(step)], axis=1)
                grads[g] = key_grad * scale
                grads[kv_heads + g] = value_grad
            grad_kv[s] = jnp.concatenate(grads, axis=1).astype(BF16).reshape(lines, 2, tokens, 2 * kv_cols)
            pair_copy(s).start()

        def pass_on(turn):
            s = peer(turn)
            pair_copy(s).wait_recv()

            @pl.loop(0, lines)
            def _(n):
                kv_sum[s, n] = (grad_kv[s, n, core].astype(F32) + r.kv_pair[s, n].astype(F32)).astype(BF16)

            start(kv_copies(s))

        @pl.loop(0, dp_n)
        def _(turn):
            one_sequence(turn)

            @pl.when(turn > 0)
            def _():
                pass_on(turn - 1)

            @pl.when(lax.rem(turn, every) == 0)
            def _():
                line.advance_at(line.position + turn // every, 1)

        pass_on(dp_n - 1)

        @pl.loop(0, dp_n)
        def _(s):
            pair_copy(s).wait_send()

    seqs = lambda *shape: pltpu.VMEM((dp_n,) + shape, BF16)
    pl.run_scoped(
        sequences,
        pltpu.VMEM((rows, width), BF16), seqs(tokens, q_cols), pltpu.VMEM((2 * lines, dp_n, tokens, 2 * kv_cols), BF16),
        pltpu.VMEM((length, tokens), F32), pltpu.VMEM((tokens, q_cols), BF16), seqs(lines, 2, tokens, 2 * kv_cols),
    )
    line.position += dp_n // every
    assert line.position <= n_ffn

    def projections(w_qkv, normed_one, qk_pre, mixed, tables, out_part, qkv_part, dn1_part):
        loads = [
            local(src, dst, r.in_sem, 8 + n)
            for n, (src, dst) in enumerate((
                (r.qk_pre, qk_pre), (r.tables, tables), (r.mixed, mixed), (r.normed_one, normed_one), (r.w_qkv, w_qkv)))
        ]
        start(loads)
        wait(loads)

        @pl.loop(0, width // 512)
        def _(n):
            total = jnp.zeros((rows, 512), F32)
            for s in range(dp_n):
                total += contract_rows(mixed[s], r.dx_all[s, :, span(n, 512)])
            out_part[:, span(n, 512)] = total.astype(BF16)

            @pl.when(n == 1)
            def _():
                line.advance_at(line.position, 1)

        line.position += 1

        pair_o = remote(out_part.at[span(other, half)], r.pair_o, r.pair_send, 0, r.pair_land, 0, partner)
        pair_o.start()

        q_gain, k_gain = gains[2:3, 0:head], gains[3:4, 0:head]
        zero = jnp.zeros((1, head), F32)

        def rotate(turn, carry):
            s = peer(turn)
            for shift in range(1, lines):
                src = lax.rem(z + shift, lines)
                land = r.kv_land.at[src, s]
                local(land, land, r.kv_recv, dp_n + s * lines + src).wait()
            kv = kv_sum[s, z].astype(F32)
            for shift in range(1, lines):
                kv += r.kv_land[lax.rem(z + shift, lines), s].astype(F32)
            kv = kv.astype(BF16)
            cosine, sine = tables[s, :, 0:head], tables[s, :, head : 2 * head]
            sums = list(carry)
            outs = []
            for h in range(kv_heads * (group + 1)):
                is_key = h >= kv_heads * group
                if is_key:
                    g = h - kv_heads * group
                    grad = kv[:, g * head : (g + 1) * head].astype(F32)
                else:
                    grad = grad_query[s, :, h * head : (h + 1) * head].astype(F32)
                turned = jnp.concatenate([grad[:, head // 2 :], grad[:, : head // 2]], axis=1)
                grad = grad * cosine - turned * sine
                hat, inverse = norm_rows(qk_pre[s, :, h * head : (h + 1) * head])
                sums[is_key] = sums[is_key] + jnp.sum(grad * hat, axis=0, keepdims=True)
                back = grad * (k_gain if is_key else q_gain)
                outs.append((inverse * (back - hat * jnp.mean(back * hat, axis=-1, keepdims=True))).astype(BF16))
            grad_qkv[s] = jnp.concatenate(outs + [kv[:, kv_cols:]], axis=1)

            @pl.when(lax.rem(turn, max(1, dp_n // 2)) == 0)
            def _():
                line.advance_at(line.position + turn // max(1, dp_n // 2), 1)

            return tuple(sums)

        q_sum, k_sum = lax.fori_loop(0, dp_n, rotate, (zero, zero))
        line.position += 2
        assert line.position <= n_ffn
        slot = r.pair_slot
        pair_o.wait_recv()
        for j in range(2):
            for c in range(4):
                mine = out_part[pl.ds(pl.multiple_of(core * half + j * quarter, quarter), quarter), pl.ds(c * 512, 512)]
                arrived = r.pair_o[pl.ds(j * quarter, quarter), pl.ds(c * 512, 512)]
                slot[j, pl.ds(c * quarter, quarter), :] = (mine.astype(F32) + arrived.astype(F32)).astype(BF16)
        copies = [local(slot.at[j], own.at[n_ffn + j], r.stage_sem, j) for j in range(2)]
        start(copies)
        wait(copies)
        gain_acc[2:3, 0:head] = q_sum
        gain_acc[3:4, 0:head] = k_sum
        line.advance(1)

        @pl.loop(0, dp_n)
        def _(i):
            total = jnp.zeros((rows, cols), F32)
            for s in range(dp_n):
                total += contract_rows(normed_one[s, :, span(i, rows)], grad_qkv[s])
            qkv_part[i] = total.astype(BF16)

        pair_q = [
            remote(qkv_part.at[i, span(other, half)], r.pair_q.at[i], r.pair_send, 1 + i, r.pair_land, 1 + i, partner)
            for i in range(dp_n)
        ]
        start(pair_q)
        line.advance(1)

        @pl.loop(0, width // 512)
        def _(n):
            weights = w_qkv[span(n, 512)]
            for s in range(dp_n):
                dn1_part[s, :, span(n, 512)] = contract_cols(grad_qkv[s], weights).astype(BF16)

        dn1_sends = []
        for shift in pairs:
            to = peer(shift)
            dn1_sends.append(remote(dn1_part.at[to], r.dn1_land.at[dp], r.dn1_send, shift, r.dn1_recv, dp, (to, z, core)))
        r.dn1_land[dp] = dn1_part[dp]
        line.advance(1)

        piece = line.piece
        q_sends = []
        q_mine = []
        for i in range(dp_n):
            pair_q[i].wait_recv()
            mine = qkv_part.at[i, span(core, half)]
            mine[...] = (mine[...].astype(F32) + r.pair_q[i].astype(F32)).astype(BF16)
        for shift in range(dp_n):
            to = peer(shift)
            for j in range(3):
                number = dp * 3 + j
                src = qkv_part.at[to, span(core, half), pl.ds(j * piece, piece)]
                if shift == 0:
                    q_mine.append(local(src, line.q_own(number), r.own_sem, number))
                else:
                    q_sends.append(remote(src, line.q_own(number), r.q_send, shift * 3 + j, r.own_sem, number, (to, z, core)))
        start(q_sends + q_mine)
        assert line.position <= line.q_first
        start(dn1_sends)
        line.advance(1)
        out_sends = [
            remote(r.out_keep.at[peer(shift)], r.out_land.at[dp], r.sum_send, 3 * dp_n + shift, r.land_recv, dp_n + dp, (peer(shift), z, core))
            for shift in pairs
        ]
        out_mine = local(r.out_keep.at[dp], r.out_land.at[dp], r.in_sem, 4)
        start(out_sends + [out_mine])
        line.advance(1)

        for shift in pairs:
            src = peer(shift)
            local(r.dn1_land.at[src], r.dn1_land.at[src], r.dn1_recv, src).wait()

        @pl.loop(0, tokens // 32)
        def _(i):
            where = span(i, 32)
            grad = r.dn1_land[0, where].astype(F32)
            for src in range(1, dp_n):
                grad += r.dn1_land[src, where].astype(F32)
            hat, inverse = norm_rows(r.own_x_v[where].astype(F32))
            gain_acc[0:1] += jnp.sum(grad * hat, axis=0, keepdims=True)
            back = grad * gains[0:1]
            total = grad_hidden[where] + inverse * (back - hat * jnp.mean(back * hat, axis=-1, keepdims=True))
            r.result[where] = total.astype(BF16)

        written = local(r.result, r.input_grad, r.in_sem, 0)
        written.start()
        written.wait()

        def gain_total(land, count, me):
            land[me] = gain_acc[...]
            total = land[0]
            for n in range(1, count):
                total = total + land[n]
            return total

        sends = [remote(gain_acc, r.gain_core.at[core], r.gain_send, 0, r.gain_recv, 0, partner)]
        start(sends)
        line.advance(1)
        wait(sends)
        gain_acc[...] = gain_total(r.gain_core, 2, core)
        sends = [
            remote(gain_acc, r.gain_dp.at[dp], r.gain_send, shift, r.gain_recv, shift, (peer(shift), z, core)) for shift in pairs
        ]
        start(sends)
        line.advance(1)
        wait(sends)
        gain_acc[...] = gain_total(r.gain_dp, dp_n, dp)
        sends = [
            remote(gain_acc, r.gain_z.at[z], r.gain_send, dp_n + shift, r.gain_recv, dp_n + shift,
                   (dp, lax.rem(z + shift, lines), core))
            for shift in range(1, lines)
        ]
        start(sends)
        line.advance(1)
        wait(sends)
        gain_acc[...] = gain_total(r.gain_z, lines, z)
        written = local(gain_acc, r.gain_sum, r.in_sem, 1)
        written.start()
        written.wait()

        landed(r.out_land, dp_n)
        wait([out_mine])

        @pl.loop(0, dp_n)
        def _(src):
            copy = local(r.out_land.at[src], r.land_slot, r.in_sem, 3)
            copy.start()
            copy.wait()

            @pl.loop(0, tokens // 32)
            def _(i):
                where = span(i, 32)
                hidden_in[where] += r.land_slot[where].astype(F32)

        r.result[...] = hidden_in[...].astype(BF16)
        done = local(r.result, r.output, r.in_sem, 0)
        done.start()
        done.wait()
        line.finish()

        for copy in out_sends + q_sends + dn1_sends + pair_q + [pair_o]:
            copy.wait_send()

        @pl.loop(0, dp_n)
        def _(s):
            for copy in kv_copies(s):
                copy.wait_send()

    pl.run_scoped(
        projections,
        pltpu.VMEM((width, cols), BF16), seqs(tokens, width), pltpu.VMEM((dp_n, tokens, q_cols + kv_cols), F32), seqs(tokens, q_cols),
        pltpu.VMEM((dp_n, tokens, 2 * head), F32), pltpu.VMEM((rows, width), BF16), seqs(rows, cols), seqs(tokens, width),
    )

    for copy in dx_sends:
        copy.wait_send()

    @pl.loop(1, n_blocks)
    def _(b):
        for copy in weight_copies(b)[1]:
            copy.wait_send()


def add_rows(into, left, right):
    @pl.loop(0, into.shape[0] // 32)
    def _(i):
        where = pl.ds(pl.multiple_of(i * 32, 32), 32)
        into[where] = (left[where].astype(F32) + right[where].astype(F32)).astype(BF16)


def backward(arrays, dp_n, lines, head, collective_id):
    x = arrays
    tokens, width = x.own_x.shape
    rows = width // dp_n
    f8 = x.w_down.shape[0] // 2
    n_blocks = f8 // 256
    down_block = 1024 // rows
    q_cols = x.query.shape[2]
    cols = x.w_qkv.shape[1]
    kv_cols = (cols - q_cols) // 2
    kv_heads = kv_cols // head
    per_block = down_block + dp_n
    chunks = n_blocks * per_block + 2 + dp_n * cols // 1024
    plane = 2 * dp_n * tokens
    dims = SimpleNamespace(
        dp_n=dp_n, lines=lines, tokens=tokens, width=width, rows=rows, f8=f8, n_blocks=n_blocks, per_block=per_block,
        down_block=down_block, head=head, group=q_cols // kv_cols, kv_heads=kv_heads, q_cols=q_cols, kv_cols=kv_cols,
        qkv_cols=cols, chunks=chunks,
    )
    bf16 = lambda *shape: jax.ShapeDtypeStruct(shape, BF16)
    outs = BackOut(
        output=bf16(tokens, width), input_grad=bf16(tokens, width), gain_sum=jax.ShapeDtypeStruct((8, width), F32),
        totals=bf16(2, chunks, rows, 512), own=bf16(chunks, rows, 512), first=bf16(chunks, rows, 512),
        cross=bf16(chunks, rows, 512), w_land=bf16(n_blocks, width, 512), dn2_pair=bf16(dp_n, tokens, width), out_pair=bf16(dp_n, tokens, width), out_land=bf16(dp_n, tokens, width), out_keep=bf16(dp_n, tokens, width),
    )
    vmem = lambda *shape: pltpu.VMEM(shape, BF16)
    dma = lambda n: pltpu.SemaphoreType.DMA((n,))
    scratch = BackScratch(
        sum_slot=vmem(8, rows, 512), total_slot=vmem(8, rows, 512), in_slot=vmem(rows, 512),
        kv_sum=vmem(dp_n, lines, tokens, 2 * kv_cols), grad_query=vmem(dp_n, tokens, q_cols), grad_qkv=vmem(dp_n, tokens, cols),
        dn2_land=vmem(dp_n, tokens, width),
        land_slot=vmem(tokens, width), hidden_v=pltpu.VMEM((tokens, width), F32), grad_hidden=pltpu.VMEM((tokens, width), F32),
        own_x_v=vmem(tokens, width), cot_own=vmem(tokens, width), gains_v=pltpu.VMEM((8, width), F32), gain_acc=pltpu.VMEM((8, width), F32),
        dx_all=vmem(dp_n, tokens, width), kv_pair=vmem(dp_n, lines, tokens, 2 * kv_cols), kv_land=vmem(lines, dp_n, tokens, 2 * kv_cols),
        gain_core=pltpu.VMEM((2, 8, width), F32), gain_dp=pltpu.VMEM((dp_n, 8, width), F32), gain_z=pltpu.VMEM((lines, 8, width), F32),
        dn1_land=vmem(dp_n, tokens, width), result=vmem(tokens, width), pair_slot=vmem(2, rows, 512), pair_o=vmem(rows // 2, width), pair_q=vmem(dp_n, rows // 2, cols),
        load_sem=dma(3), own_sem=dma(3 * dp_n), first_send=dma(chunks), first_recv=dma(chunks),
        second_send=dma(chunks), cross_recv=dma(chunks), owner_send=dma(chunks), across_send=dma(chunks), second_recv=dma(chunks), core_send=dma(chunks), core_recv=dma(chunks),
        w_send=dma(2 * n_blocks * dp_n), w_recv=dma(2 * n_blocks * dp_n), stage_sem=dma(per_block),
        in_sem=dma(8 + max(8, dp_n)), sum_send=dma(4 * dp_n), pair_recv=dma(2 * dp_n), land_recv=dma(2 * dp_n), dx_send=dma(dp_n), dx_recv=dma(dp_n),
        kv_send=dma(dp_n + dp_n * lines), kv_recv=dma(dp_n + dp_n * lines), pair_send=dma(1 + dp_n), pair_land=dma(1 + dp_n),
        dn1_send=dma(dp_n), dn1_recv=dma(dp_n), q_send=dma(3 * dp_n), gain_send=dma(dp_n + lines), gain_recv=dma(dp_n + lines),
    )
    hbm = pl.BlockSpec(memory_space=pl.ANY)
    in_vmem = pl.BlockSpec(memory_space=pltpu.VMEM)
    flops = 6 * plane * width * f8 * 3
    results = pl.pallas_call(
        partial(back_kernel, dims),
        out_shape=tuple(outs),
        in_specs=list(BackIn(*[hbm] * len(x))._replace(log_total=in_vmem)),
        out_specs=(hbm,) * len(outs),
        scratch_shapes=list(scratch),
        compiler_params=pltpu.CompilerParams(collective_id=collective_id, has_side_effects=True, vmem_limit_bytes=63 * MIB),
        cost_estimate=pl.CostEstimate(flops=flops, bytes_accessed=100 * MIB, transcendentals=0),
        name="backward",
    )(*x)
    return BackOut(*results)


def widen_pair_kernel(n_blocks, place, *refs):
    gate, up = refs[n_blocks:]
    for b in range(n_blocks):
        columns = slice(b * 256, (b + 1) * 256)
        gate[:, columns] = refs[b][0, 0, :, 0:256].astype(F32)
        up[:, columns] = refs[b][0, 0, :, 256:512].astype(F32)


def widen_rows(out, chunks):
    quarter = chunks[0].shape[2] // 4
    for j, chunk in enumerate(chunks):
        for c in range(4):
            out[j * quarter : (j + 1) * quarter, c * 512 : (c + 1) * 512] = chunk[0, 0, c * quarter : (c + 1) * quarter, :].astype(F32)


def widen_rows_kernel(place, *refs):
    widen_rows(refs[-1], refs[:-1])


def widen_heads_kernel(dp_n, q_cols, kv_cols, place, *refs):
    out, query, key, value = refs[-4:]
    widen_rows(out, refs[:2])
    chunks = refs[2:-4]
    half = query.shape[0]
    piece = (q_cols + 2 * kv_cols) // 3
    across = 512 // piece
    for src in range(dp_n):
        for j in range(3):
            chunk, spot = divmod(3 * src + j, 2 * across)
            row, column = spot // across * half, spot % across * piece
            part = chunks[chunk][0, 0, row : row + half, column : column + piece].astype(F32)
            if j < 2:
                query[:, src * q_cols + j * piece : src * q_cols + (j + 1) * piece] = part
            else:
                key[:, src * kv_cols : (src + 1) * kv_cols] = part[:, :kv_cols]
                value[:, src * kv_cols : (src + 1) * kv_cols] = part[:, kv_cols:]


def widen(totals, place, dp_n, width, f8, q_cols, kv_cols):
    _, chunks, rows, _ = totals.shape
    half = rows // 2
    down_block = 1024 // rows
    per_block = down_block + dp_n
    n_blocks = f8 // 256
    n_ffn = n_blocks * per_block
    f32 = lambda *shape: jax.ShapeDtypeStruct(shape, F32)

    def call(kernel, grid, in_maps, out_specs, out_shape, name):
        return pl.pallas_call(
            kernel,
            grid_spec=pltpu.PrefetchScalarGridSpec(
                num_scalar_prefetch=1, grid=grid, in_specs=[pl.BlockSpec((1, 1, rows, 512), m) for m in in_maps], out_specs=out_specs),
            out_shape=out_shape, compiler_params=pltpu.CompilerParams(vmem_limit_bytes=48 * MIB), name=name,
        )(place, *[totals] * len(in_maps))

    def gate_map(b):
        return lambda src, who, place: (who, b * per_block + down_block + lax.rem(place[0] - src + dp_n, dp_n), 0, 0)

    gate, up = call(
        partial(widen_pair_kernel, n_blocks), (dp_n, 2), [gate_map(b) for b in range(n_blocks)],
        (pl.BlockSpec((rows, f8), lambda src, who, place: (0, 2 * src + who)),) * 2, (f32(rows, 2 * dp_n * f8),) * 2, "widen_gate_up")

    def down_map(j):
        return lambda who, b, place: (who, b * per_block + j, 0, 0)

    down = call(
        widen_rows_kernel, (2, n_blocks), [down_map(j) for j in range(down_block)],
        pl.BlockSpec((256, width), lambda who, b, place: (who * n_blocks + b, 0)), f32(2 * f8, width), "widen_down")

    def tail_map(k):
        return lambda who, place: (who, k, 0, 0)

    half_rows = lambda columns: pl.BlockSpec((half, columns), lambda who, place: (who, 0))
    widths = (width, dp_n * q_cols, dp_n * kv_cols, dp_n * kv_cols)
    out, query, key, value = call(
        partial(widen_heads_kernel, dp_n, q_cols, kv_cols), (2,), [tail_map(k) for k in range(n_ffn, chunks)],
        tuple(half_rows(columns) for columns in widths), tuple(f32(rows, columns) for columns in widths), "widen_heads")
    return query, key, value, out, gate, up, down


class FrontIn(NamedTuple):
    own_x: Any
    own_cot: Any
    w_query: Any
    w_key: Any
    w_value: Any
    gain_piece: Any
    own_tables: Any
    bias: Any
    w_out: Any
    w_gate: Any
    w_up: Any


class FrontOut(NamedTuple):
    normed_two: Any
    cot_all: Any
    w_first: Any
    hidden_in: Any
    w_qkv: Any
    normed_one: Any
    qk_pre: Any
    query: Any
    keys_values: Any
    log_total: Any
    mixed: Any
    tables: Any
    gains: Any


class FrontScratch(NamedTuple):
    x_all: Any
    n1: Any
    w_all: Any
    qk: Any
    value: Any
    q_rot: Any
    kv: Any
    log_v: Any
    mix: Any
    tables_v: Any
    gains_v: Any
    bias_v: Any
    w_out_v: Any
    part: Any
    land: Any
    hidden: Any
    n2: Any
    in_sem: Any
    out_sem: Any
    x_send: Any
    x_recv: Any
    w_send: Any
    w_recv: Any
    w_pass: Any
    w_passed: Any
    kv_send: Any
    kv_recv: Any
    kv_pass: Any
    kv_passed: Any
    part_send: Any
    part_recv: Any
    plane_send: Any
    plane_recv: Any
    plane_pass: Any
    plane_passed: Any
    first_send: Any
    first_recv: Any


def front_kernel(dims, *refs):
    r = SimpleNamespace()
    for kind, first in ((FrontIn, 0), (FrontOut, len(FrontIn._fields)), (FrontScratch, len(FrontIn._fields + FrontOut._fields))):
        vars(r).update(kind(*refs[first : first + len(kind._fields)])._asdict())
    dp_n, lines, tokens, width, rows, f8 = dims.dp_n, dims.lines, dims.tokens, dims.width, dims.rows, dims.f8
    head, group, kv_heads, q_cols, kv_cols = dims.head, dims.group, dims.kv_heads, dims.q_cols, dims.kv_cols
    length = 2 * lines * tokens
    half = rows // 2
    scale = head ** (-0.5)
    dp, z, core = places()
    other = 1 - core
    partner = (dp, z, other)
    pairs = range(1, dp_n)
    me = 2 * z + core

    def peer(shift):
        return lax.rem(dp + shift, dp_n)

    def local(src, dst, sem, n=0):
        return pltpu.make_async_copy(src, dst, sem.at[n])

    def remote(src, dst, send, n, recv, m, device):
        return pltpu.make_async_remote_copy(
            src, dst, send.at[n], recv.at[m], device_id=device, device_id_type=MESH)

    def span(index, size):
        return pl.ds(pl.multiple_of(index * size, size), size)

    def start(copies):
        for copy in copies:
            copy.start()

    def wait(copies):
        for copy in copies:
            copy.wait()

    def landed(ref, sem, n):
        local(ref, ref, sem, n).wait()

    barrier = pltpu.get_barrier_semaphore()
    for shift in pairs:
        pl.semaphore_signal(barrier, device_id=(peer(shift), z, core), device_id_type=MESH)
    pl.semaphore_signal(barrier, device_id=partner, device_id_type=MESH)
    for shift in range(1, lines):
        pl.semaphore_signal(barrier, device_id=(dp, lax.rem(z + shift, lines), core), device_id_type=MESH)

    mine = [
        local(r.own_x, r.x_all.at[dp], r.in_sem, 0), local(r.own_tables, r.tables_v.at[dp], r.in_sem, 1),
        local(r.gain_piece, r.gains_v.at[:, span(dp, rows)], r.in_sem, 2), local(r.bias, r.bias_v, r.in_sem, 3),
        local(r.w_out, r.w_out_v, r.in_sem, 4),
    ]
    ends = (0, q_cols, q_cols + kv_cols, q_cols + 2 * kv_cols) if kv_cols % 128 == 0 else (0, q_cols, q_cols + 2 * kv_cols)
    n_pieces = len(ends) - 1

    def weight_from(to, where):
        if n_pieces == 3:
            return [r.w_query.at[where, span(to, q_cols)], r.w_key.at[where, span(to, kv_cols)], r.w_value.at[where, span(to, kv_cols)]]
        return [r.w_query.at[where, span(to, q_cols)], r.w_key.at[to, where]]

    def weight_to(where):
        return [r.w_all.at[where, pl.ds(a, b - a)] for a, b in zip(ends, ends[1:])]

    whole = pl.ds(0, rows)
    mine += [local(src, dst, r.in_sem, 5 + n) for n, (src, dst) in enumerate(zip(weight_from(dp, whole), weight_to(span(dp, rows))))]
    start(mine)
    pl.semaphore_wait(barrier, dp_n + lines - 1)

    small = []
    for shift in pairs:
        to = peer(shift)
        device = (to, z, core)
        small += [
            remote(r.own_x, r.x_all.at[dp], r.x_send, 3 * shift, r.x_recv, 3 * dp, device),
            remote(r.own_tables, r.tables_v.at[dp], r.x_send, 3 * shift + 1, r.x_recv, 3 * dp + 1, device),
            remote(r.gain_piece, r.gains_v.at[:, span(dp, rows)], r.x_send, 3 * shift + 2, r.x_recv, 3 * dp + 2, device),
        ]
    start(small)

    def weight_spot(src, side):
        return weight_to(pl.ds(pl.multiple_of(src * rows + side * half, half), half))

    weights = []
    for shift in pairs:
        to = peer(shift)
        for n, (src, dst) in enumerate(zip(weight_from(to, span(core, half)), weight_spot(dp, core))):
            weights.append(remote(src, dst, r.w_send, 3 * shift + n, r.w_recv, 3 * dp + n, (to, z, core)))
    start(weights)

    wait(mine[1:3])
    for shift in pairs:
        landed(r.gains_v.at[:, span(peer(shift), rows)], r.x_recv, 3 * peer(shift) + 2)
    mine[0].wait()

    @pl.loop(0, dp_n)
    def _(turn):
        s = peer(turn)

        @pl.when(turn > 0)
        def _():
            landed(r.x_all.at[s], r.x_recv, 3 * s)

        @pl.loop(0, tokens // 32)
        def _(i):
            hat, _ = norm_rows(r.x_all[s, span(i, 32)].astype(F32))
            r.n1[pl.ds(pl.multiple_of(s * tokens + i * 32, 32), 32)] = (hat * r.gains_v[0:1]).astype(BF16)

    passes = []
    for shift in pairs:
        src = peer(shift)
        for n, spot in enumerate(weight_spot(src, core)):
            landed(spot, r.w_recv, 3 * src + n)
            copy = remote(spot, spot, r.w_pass, 3 * shift + n, r.w_passed, 3 * src + n, partner)
            copy.start()
            passes.append(copy)
    wait(mine[3:])
    for shift in pairs:
        src = peer(shift)
        for n, spot in enumerate(weight_spot(src, other)):
            landed(spot, r.w_passed, 3 * src + n)
        landed(r.tables_v.at[src], r.x_recv, 3 * src + 1)

    slot_of = lambda d, c: pl.ds(pl.multiple_of((2 * d + c) * tokens, tokens), tokens)

    def plane_copies(src, target, base):
        spot = target.at[slot_of(dp, core)]
        found = [remote(src, spot, r.plane_send, base + shift, r.plane_recv, base + dp, (peer(shift), z, core)) for shift in pairs]
        return found + [remote(src, spot, r.plane_send, base, r.plane_recv, base + dp_n, partner)]

    def plane_pass(target, base):
        found = []
        for shift in pairs:
            src = peer(shift)
            spot = target.at[slot_of(src, core)]
            landed(spot, r.plane_recv, base + src)
            copy = remote(spot, spot, r.plane_pass, base + shift, r.plane_passed, base + src, partner)
            copy.start()
            found.append(copy)
        return found

    def plane_done(target, base):
        landed(target.at[slot_of(dp, other)], r.plane_recv, base + dp_n)
        for shift in pairs:
            src = peer(shift)
            landed(target.at[slot_of(src, other)], r.plane_passed, base + src)

    cots = plane_copies(r.own_cot, r.cot_all, 0)
    firsts, first_mine = [], []
    for n, weight in enumerate((r.w_gate, r.w_up)):
        for shift in range(dp_n):
            to = peer(shift)
            src = weight.at[:, pl.ds(pl.multiple_of((2 * to + core) * f8, 256), 256)]
            dst = r.w_first.at[span(dp, rows), pl.ds(256 * n, 256)]
            if shift == 0:
                first_mine.append(local(src, dst, r.out_sem, n))
            else:
                firsts.append(remote(src, dst, r.first_send, 2 * shift + n, r.first_recv, 2 * dp + n, (to, z, core)))
    cot_mine = local(r.own_cot, r.cot_all.at[slot_of(dp, core)], r.out_sem, 2)
    start(cots + firsts + first_mine + [cot_mine])

    split = q_cols + kv_cols
    r.qk[:, 0:q_cols] = dot(r.n1[...], r.w_all[:, 0:q_cols])
    pair = dot(r.n1[...], r.w_all[:, q_cols : q_cols + 2 * kv_cols])
    r.qk[:, q_cols:split] = pair[:, :kv_cols]
    r.value[...] = pair[:, kv_cols:].astype(BF16)
    outs = [
        local(r.n1, r.normed_one, r.out_sem, 3), local(r.w_all, r.w_qkv, r.out_sem, 4), local(r.qk, r.qk_pre, r.out_sem, 5),
        local(r.tables_v, r.tables, r.out_sem, 6), local(r.gains_v, r.gains, r.out_sem, 7),
    ]
    start(outs)

    def kv_copies(s):
        spot = r.kv.at[me, s]
        found = [
            remote(spot, spot, r.kv_send, s * lines + shift, r.kv_recv, s * (lines + 1) + z, (dp, lax.rem(z + shift, lines), core))
            for shift in range(1, lines)
        ]
        return found + [remote(spot, spot, r.kv_send, s * lines, r.kv_recv, s * (lines + 1) + lines, partner)]

    def kv_pass(s):
        found = []
        for shift in range(1, lines):
            src = lax.rem(z + shift, lines)
            spot = r.kv.at[2 * src + core, s]
            found.append((spot, s * (lines + 1) + src,
                          remote(spot, spot, r.kv_pass, s * lines + shift, r.kv_passed, s * lines + src, partner)))
        return found

    @pl.loop(0, dp_n)
    def _(turn):
        s = peer(turn + 1)
        cosine, sine = r.tables_v[s, :, 0:head], r.tables_v[s, :, head : 2 * head]
        turned = []
        where = span(s, tokens)
        for h in range(kv_heads * (group + 1)):
            gain = r.gains_v[2:3, 0:head] if h < kv_heads * group else r.gains_v[3:4, 0:head]
            hat, _ = norm_rows(r.qk[where, h * head : (h + 1) * head])
            hat = hat * gain
            swapped = jnp.concatenate([hat[:, head // 2 :], hat[:, : head // 2]], axis=1)
            turned.append((hat * cosine + swapped * sine).astype(BF16))
        r.q_rot[s] = jnp.concatenate(turned[: kv_heads * group], axis=1)
        r.kv[me, s] = jnp.concatenate(turned[kv_heads * group :] + [r.value[where]], axis=1)
        start(kv_copies(s))

    step = max(1, min(group, MIB // (2 * length * tokens)))

    def part_copy(s, shift):
        return remote(r.part.at[s], r.land.at[dp], r.part_send, shift, r.part_recv, dp, (s, z, core))

    @pl.loop(0, dp_n)
    def _(turn):
        s = peer(turn + 1)
        for spot, n, copy in kv_pass(s):
            landed(spot, r.kv_recv, n)
            copy.start()
        landed(r.kv.at[2 * z + other, s], r.kv_recv, s * (lines + 1) + lines)
        for shift in range(1, lines):
            src = lax.rem(z + shift, lines)
            landed(r.kv.at[2 * src + other, s], r.kv_passed, s * lines + src)
        both = r.kv[:, s].reshape(length, 2 * kv_cols)
        mask = jnp.concatenate([r.bias_v[...]] * step, axis=1)
        for g in range(kv_heads):
            keys = both[:, g * head : (g + 1) * head]
            values = both[:, (kv_heads + g) * head : (kv_heads + g + 1) * head]
            for first in range(g * group, (g + 1) * group, step):
                queries = jnp.concatenate([r.q_rot[s, :, h * head : (h + 1) * head] for h in range(first, first + step)], axis=0)
                scores = contract_cols(keys, queries) * scale + mask
                top = jnp.max(scores, axis=0, keepdims=True)
                weight = jnp.exp(scores - top)
                total = jnp.sum(weight, axis=0, keepdims=True)
                probs = (weight * (1.0 / total)).astype(BF16)
                offset = (first - g * group) * tokens
                r.log_v[s, pl.ds(g, 1), offset : offset + step * tokens] = top + jnp.log(total)
                out = contract_rows(values, probs).T.astype(BF16)
                r.mix[s, :, first * head : (first + step) * head] = jnp.concatenate(
                    [out[h * tokens : (h + 1) * tokens] for h in range(step)], axis=1)
        r.part[s] = dot(r.mix[s], r.w_out_v[...]).astype(BF16)

        @pl.when(turn < dp_n - 1)
        def _():
            part_copy(s, turn + 1).start()

    outs += [
        local(r.q_rot, r.query, r.out_sem, 8), local(r.kv, r.keys_values, r.out_sem, 9),
        local(r.log_v, r.log_total, r.out_sem, 10), local(r.mix, r.mixed, r.out_sem, 11),
    ]
    start(outs[5:])

    for shift in pairs:
        landed(r.land.at[peer(shift)], r.part_recv, peer(shift))
    r.land[dp] = r.part[dp]

    @pl.loop(0, tokens // 32)
    def _(i):
        where = span(i, 32)
        total = r.land[0, where].astype(F32)
        for src in range(1, dp_n):
            total += r.land[src, where].astype(F32)
        total += r.x_all[dp, where].astype(F32)
        r.hidden[where] = total
        hat, _ = norm_rows(total)
        r.n2[where] = (hat * r.gains_v[1:2]).astype(BF16)

    n2_base = dp_n + 1
    n2_copies = plane_copies(r.n2, r.normed_two, n2_base)
    start(n2_copies)
    n2_mine = local(r.n2, r.normed_two.at[slot_of(dp, core)], r.out_sem, 12)
    outs += [local(r.hidden, r.hidden_in, r.out_sem, 13), n2_mine]
    start(outs[9:])
    passed = plane_pass(r.cot_all, 0)
    passed += plane_pass(r.normed_two, n2_base)
    plane_done(r.cot_all, 0)
    for shift in pairs:
        src = peer(shift)
        for n in range(2):
            landed(r.w_first.at[span(src, rows), pl.ds(256 * n, 256)], r.first_recv, 2 * src + n)
    plane_done(r.normed_two, n2_base)
    wait(outs + first_mine + [cot_mine])
    for copy in small + weights + passes + cots + firsts + n2_copies + passed:
        copy.wait_send()

    @pl.loop(0, dp_n)
    def _(s):
        for copy in kv_copies(s):
            copy.wait_send()
        for _, _, copy in kv_pass(s):
            copy.wait_send()

    @pl.loop(0, dp_n - 1)
    def _(turn):
        part_copy(peer(turn + 1), turn + 1).wait_send()


def forward(x, dp_n, lines, head, collective_id):
    tokens, width = x.own_x.shape
    rows = width // dp_n
    q_cols = x.w_query.shape[1] // dp_n
    kv_cols = x.w_value.shape[1] // dp_n
    kv_heads = kv_cols // head
    f8 = x.w_gate.shape[1] // (2 * dp_n)
    cols = q_cols + 2 * kv_cols
    length = 2 * lines * tokens
    dims = SimpleNamespace(
        dp_n=dp_n, lines=lines, tokens=tokens, width=width, rows=rows, f8=f8, head=head, group=q_cols // kv_cols,
        kv_heads=kv_heads, q_cols=q_cols, kv_cols=kv_cols,
    )
    bf16 = lambda *shape: jax.ShapeDtypeStruct(shape, BF16)
    f32 = lambda *shape: jax.ShapeDtypeStruct(shape, F32)
    all_tokens = dp_n * tokens
    group_rows = q_cols // kv_cols * tokens
    outs = FrontOut(
        normed_two=bf16(2 * all_tokens, width), cot_all=bf16(2 * all_tokens, width), w_first=bf16(width, 512),
        hidden_in=f32(tokens, width), w_qkv=bf16(width, cols), normed_one=bf16(all_tokens, width), qk_pre=f32(all_tokens, q_cols + kv_cols),
        query=bf16(dp_n, tokens, q_cols), keys_values=bf16(2 * lines, dp_n, tokens, 2 * kv_cols), log_total=f32(dp_n, kv_heads, group_rows),
        mixed=bf16(dp_n, tokens, q_cols), tables=f32(dp_n, tokens, 2 * head), gains=f32(8, width),
    )
    vmem = lambda *shape: pltpu.VMEM(shape, BF16)
    wide = lambda *shape: pltpu.VMEM(shape, F32)
    dma = lambda n: pltpu.SemaphoreType.DMA((n,))
    scratch = FrontScratch(
        x_all=vmem(dp_n, tokens, width), n1=vmem(all_tokens, width), w_all=vmem(width, cols), qk=wide(all_tokens, q_cols + kv_cols),
        value=vmem(all_tokens, kv_cols), q_rot=vmem(dp_n, tokens, q_cols), kv=vmem(2 * lines, dp_n, tokens, 2 * kv_cols),
        log_v=wide(dp_n, kv_heads, group_rows), mix=vmem(dp_n, tokens, q_cols), tables_v=wide(dp_n, tokens, 2 * head), gains_v=wide(8, width),
        bias_v=wide(length, tokens), w_out_v=vmem(rows, width), part=vmem(dp_n, tokens, width), land=vmem(dp_n, tokens, width),
        hidden=wide(tokens, width), n2=vmem(tokens, width), in_sem=dma(8), out_sem=dma(14), x_send=dma(3 * dp_n), x_recv=dma(3 * dp_n),
        w_send=dma(3 * dp_n), w_recv=dma(3 * dp_n), w_pass=dma(3 * dp_n), w_passed=dma(3 * dp_n), kv_send=dma(dp_n * lines),
        kv_recv=dma(dp_n * (lines + 1)), kv_pass=dma(dp_n * lines), kv_passed=dma(dp_n * lines), part_send=dma(dp_n), part_recv=dma(dp_n),
        plane_send=dma(2 * dp_n + 2), plane_recv=dma(2 * dp_n + 2), plane_pass=dma(2 * dp_n + 2), plane_passed=dma(2 * dp_n + 2),
        first_send=dma(2 * dp_n), first_recv=dma(2 * dp_n),
    )
    hbm = pl.BlockSpec(memory_space=pl.ANY)
    results = pl.pallas_call(
        partial(front_kernel, dims),
        out_shape=tuple(outs),
        in_specs=[hbm] * len(x),
        out_specs=(hbm,) * len(outs),
        scratch_shapes=list(scratch),
        compiler_params=pltpu.CompilerParams(collective_id=collective_id, has_side_effects=True, vmem_limit_bytes=63 * MIB),
        cost_estimate=pl.CostEstimate(flops=10**10, bytes_accessed=50 * MIB, transcendentals=0),
        name="forward",
    )(*x)
    return FrontOut(*results)


def local(
    inputs, attn_gain, w_query, w_key, w_value, q_gain, key_norm_gain, w_out, ffn_gain,
    w_gate, w_up, w_down, stretch_map, pos_ids, cotangent,
):
    dp, lines, cores = lax.axis_size("dp"), lax.axis_size("z"), lax.axis_size("core")
    core = lax.axis_index("core")
    rows, width = inputs.shape[1], inputs.shape[2]
    head = q_gain.shape[0]
    query_width, key_width, hidden = w_query.shape[1], w_key.shape[1], w_gate.shape[1]
    half = rows // 2
    stretches = stretch_map.shape[0]
    length = stretches * half
    ctx = lax.axis_index("z") * cores + core

    within = jnp.arange(half, dtype=jnp.int32)
    key_places = (stretch_map[:, None] * half + within[None, :]).reshape(length)
    query_places = lax.dynamic_slice_in_dim(key_places, ctx * rows, rows, 0)
    bias = jnp.where(key_places[:, None] <= query_places[None, :], 0.0, MASKED_SCORE).astype(F32)
    frequency = jnp.power(F32(ROPE_BASE), -2.0 * jnp.arange(head // 2, dtype=F32) / head)
    angles = pos_ids[0].astype(F32)[:, None] * frequency[None, :]
    cosine, sine = jnp.cos(angles), jnp.sin(angles)
    tables = jnp.concatenate([cosine, cosine, -sine, sine], axis=1)
    piece = width // dp
    gain_piece = jnp.zeros((8, piece), F32).at[0].set(attn_gain.astype(F32)).at[1].set(ffn_gain.astype(F32))
    gain_piece = gain_piece.at[2, :head].set(q_gain.astype(F32)).at[3, :head].set(key_norm_gain.astype(F32))
    kv_cols, q_cols = key_width // dp, query_width // dp
    if kv_cols % 128 == 0:
        pair = (w_key, w_value)
    else:
        cut = [jnp.concatenate([w[:, n * kv_cols : (n + 1) * kv_cols] for w in (w_key, w_value)], axis=1) for n in range(dp)]
        pair = (jnp.stack(cut), w_value)
    front = forward(
        FrontIn(
            own_x=inputs[0], own_cot=cotangent[0], w_query=w_query, w_key=pair[0], w_value=pair[1], gain_piece=gain_piece, own_tables=tables,
            bias=bias, w_out=w_out, w_gate=w_gate, w_up=w_up,
        ),
        dp, lines, head, 2,
    )
    f8 = hidden // (2 * dp)
    made = backward(
        BackIn(
            normed_two=front.normed_two, cot_all=front.cot_all, w_first=front.w_first, w_gate=w_gate, w_up=w_up, w_down=w_down,
            hidden_in=front.hidden_in, w_out=w_out, w_qkv=front.w_qkv, normed_one=front.normed_one.reshape(dp, rows, width),
            qk_pre=front.qk_pre.reshape(dp, rows, q_cols + kv_cols), query=front.query, keys_values=front.keys_values,
            log_total=front.log_total, mixed=front.mixed, bias=bias, tables=front.tables, gains=front.gains, own_x=inputs[0],
        ),
        dp, lines, head, 1,
    )
    place = lax.axis_index("dp").reshape(1)
    query_grad, key_grad, value_grad, out_grad, gate_grad, up_grad, down_grad = widen(
        made.totals, place, dp, width, f8, q_cols, kv_cols
    )
    gains = made.gain_sum
    return (
        made.output[None], made.input_grad[None], lax.dynamic_slice_in_dim(gains[0], place[0] * piece, piece, 0), query_grad, key_grad,
        value_grad, gains[2, :head], gains[3, :head], out_grad, lax.dynamic_slice_in_dim(gains[1], place[0] * piece, piece, 0),
        gate_grad, up_grad, down_grad,
    )


def solution(mesh):
    dp, ctx = mesh.shape["dp"], mesh.shape["ctx"]
    fine = Mesh(mesh.devices.reshape(dp, ctx // 2, 2), ("dp", "z", "core"))
    tokens = P("dp", ("z", "core"), None)
    rows = P("dp", None)
    in_specs = (
        tokens, P("dp"), rows, rows, rows, P(), P(), rows, P("dp"), rows, rows, rows, P(), P("dp", ("z", "core")), tokens,
    )
    out_specs = (tokens, tokens, P("dp"), rows, rows, rows, P(), P(), rows, P("dp"), rows, rows, rows)
    return jax.shard_map(local, mesh=fine, in_specs=in_specs, out_specs=out_specs, check_vma=False)
```
